32 devices in a mesh: groups: 1, wide: 32 (over z, y, x, core).
Axes of the slice: x: 2, y: 2, z: 4, core: 2. Of those that a mesh axis runs over, the one named last changes fastest.
Arguments:
- activations: bfloat16 [128, 16384], P('groups', 'wide'), may hold values from -6 to 6
- norm_gain: float32 [16384], replicated, may hold values from 0.1 to 1.9
- query_weight: bfloat16 [16384, 16384], P(None, 'wide'), may hold values from -1 to 1
- key_weight: bfloat16 [16384, 1024], P('wide'), may hold values from -1 to 1
- value_weight: bfloat16 [16384, 1024], P('wide'), may hold values from -0.046875 to 0.046875
- output_weight: bfloat16 [16384, 16384], P('wide'), may hold values from -0.09375 to 0.09375
Outputs:
- layer_output: bfloat16 [128, 16384], P('groups', 'wide')
The draws below stay inside these ranges and needn't reach their ends.
All inputs are finite; a program needn't handle non-finite values.
Results may differ from the reference program's by a relative error of at most 0.0087.
Values may be sent and summed in bfloat16 or wider, within the bound.
No kernel may reach another device: no remote copies, remote signals or barrier semaphores. Data moves between devices by JAX's collectives and lax.ppermute only.
A program may use at most 128 MiB of HBM per device.

```python
import jax
import jax.numpy as jnp
from jax import lax

D = 16384
HEADS = 128
KVH = 8
HEAD = 128
TOKENS = 128


def draw_query_weight(key, part):
    key = jax.random.fold_in(key, 11)
    base = jax.random.normal(key, (D, HEADS * HEAD), jnp.float32) * D ** (-0.5)
    return jnp.clip(base, -1.0, 1.0).astype(jnp.bfloat16)


def draw_key_weight(key, part):
    key = jax.random.fold_in(key, 13)
    base = jax.random.normal(key, (D, KVH * HEAD), jnp.float32) * D ** (-0.5)
    return jnp.clip(base, -1.0, 1.0).astype(jnp.bfloat16)


def raised(array, stream_key, source, target, shards_of, factor):
    def block_of(dim):
        return (jnp.arange(array.shape[dim]) // (array.shape[dim] // shards_of)).reshape((-1,) + (1,) * (array.ndim - 1 - dim))

    first = jax.random.permutation(stream_key, shards_of)[block_of(target)]
    second = (block_of(target) + shards_of // 2) % shards_of
    return jnp.where((block_of(source) == first) | (block_of(source) == second), factor * array, array)


def block_levels(rng, extent, cuts, smallest, high):
    def one(dim, blocks):
        heights = jax.random.uniform(jax.random.fold_in(jax.random.fold_in(rng, 6), dim), (blocks,), jnp.float32, smallest / len(cuts), high / len(cuts))
        return jnp.repeat(jnp.exp(heights), extent[dim] // blocks).reshape((-1,) + (1,) * (len(extent) - dim - 1))

    gain = one(*cuts[0])
    for cut in cuts[1:]:
        gain = gain * one(*cut)
    return gain


def gaussian(key, dims, scale, limit, shards=(), held_as=jnp.bfloat16):
    gain = block_levels(key, dims, shards, -0.22, 0.18) if shards else 1.0
    array = jax.random.normal(key, dims, jnp.float32) * scale * gain
    return jnp.minimum(jnp.maximum(array, -limit), limit).astype(held_as)


def heavy_noise(own_key, extent, scale, limit, pieces, heavy, kind=jnp.bfloat16):
    drawn = scale * jax.random.normal(own_key, extent, jnp.float32)
    if pieces:
        drawn = drawn * block_levels(own_key, extent, pieces, -0.22, 0.18)
    return jnp.clip(raised(drawn, jax.random.fold_in(own_key, 3), *heavy), -limit, limit).astype(kind)


def setup_inputs(seed: int = 0, part: int = 0) -> dict:
    key_of = jax.random.split(jax.random.key(seed), 7)
    part_keys = jax.random.split(jax.random.fold_in(key_of[6], part), 7)
    activations = gaussian(part_keys[0], (TOKENS, D), 1.0, 6.0, ((1, 32),))
    norm_gain = jnp.clip(1.0 + 0.18 * jax.random.normal(key_of[1], (D,), jnp.float32), 0.1, 1.9)
    query_weight = draw_query_weight(jax.random.fold_in(key_of[6], 71), part)
    key_weight = draw_key_weight(jax.random.fold_in(key_of[6], 71), part)
    value_weight = gaussian(key_of[4], (D, KVH * HEAD), D ** -0.5, 0.046875, ((0, 32),))
    output_weight = heavy_noise(key_of[5], (HEADS * HEAD, D), (HEADS * HEAD) ** -0.5, 0.09375, ((0, 32),), (0, 1, 32, 2.75))
    return dict(activations=activations, norm_gain=norm_gain, query_weight=query_weight, key_weight=key_weight, value_weight=value_weight, output_weight=output_weight)


def rotary(heads_field, positions):
    half_width = heads_field.shape[-1] // 2
    frequency = 500000.0 ** (-(jnp.arange(half_width, dtype=jnp.float32) * 2.0) / heads_field.shape[-1])
    angles = positions[:, None] * frequency[None, :]
    cosine = jnp.cos(angles)[:, None, :]
    sine_part = jnp.sin(angles)[:, None, :]
    first_half = heads_field[..., :half_width]
    second = heads_field[..., half_width:]
    return jnp.concatenate([first_half * cosine - second * sine_part, second * cosine + first_half * sine_part], axis=-1)

def reference(activations, norm_gain, query_weight, key_weight, value_weight, output_weight):
    values_f = activations.astype(jnp.float32)
    mean_square = lax.optimization_barrier(jnp.mean(values_f * values_f, axis=1, keepdims=True))
    normed = (values_f * lax.rsqrt(mean_square + 1e-05) * norm_gain[None, :]).astype(jnp.bfloat16)
    queries = jnp.dot(normed, query_weight, preferred_element_type=jnp.float32)
    key_rows = jnp.dot(normed, key_weight, preferred_element_type=jnp.float32).astype(jnp.bfloat16)
    value_rows = jnp.dot(normed, value_weight, preferred_element_type=jnp.float32).astype(jnp.bfloat16)
    positions = jnp.arange(TOKENS, dtype=jnp.float32)
    query_rot = rotary(queries.reshape(TOKENS, HEADS, HEAD), positions).astype(jnp.bfloat16)
    key_rot = rotary(key_rows.astype(jnp.float32).reshape(TOKENS, KVH, HEAD), positions).astype(jnp.bfloat16)
    key_full = jnp.repeat(key_rot, HEADS // KVH, axis=1)
    value_full = jnp.repeat(value_rows.reshape(TOKENS, KVH, HEAD), HEADS // KVH, axis=1)
    scores = jnp.einsum('qhd,khd->hqk', query_rot.astype(jnp.float32), key_full.astype(jnp.float32)) * HEAD ** (-0.5)
    causal = jnp.arange(TOKENS)[:, None] >= jnp.arange(TOKENS)[None, :]
    scores = jnp.where(causal[None, :, :], scores, -1e+30)
    row_peak = lax.optimization_barrier(jnp.max(scores, axis=2, keepdims=True))
    weights = jnp.exp(scores - row_peak)
    probabilities = (weights / lax.optimization_barrier(jnp.sum(weights, axis=2, keepdims=True))).astype(jnp.bfloat16)
    attended = jnp.einsum('hqk,khd->qhd', probabilities.astype(jnp.float32), value_full.astype(jnp.float32))
    attended = attended.astype(jnp.bfloat16).reshape(TOKENS, HEADS * HEAD)
    return jnp.dot(attended, output_weight, preferred_element_type=jnp.float32).astype(jnp.bfloat16)
```

```python
import functools

import jax
import jax.numpy as jnp
from jax import lax
from jax.experimental import pallas as pl
from jax.experimental.pallas import tpu as pltpu
from jax.sharding import PartitionSpec as P

HEADS = 128
KVH = 8
HEAD = 128
EPS = 1e-05
MIB = 1 << 20


def combos(bits):
    out = [0]
    for b in bits:
        out = out + [o ^ b for o in out]
    return out


def exchange(x, offset, n):
    return lax.ppermute(x, "wide", [(i, i ^ offset) for i in range(n)])


def vmem():
    return pl.BlockSpec(memory_space=pltpu.VMEM)


def smem():
    return pl.BlockSpec(memory_space=pltpu.SMEM)


def hbm():
    return pl.BlockSpec(memory_space=pl.ANY)


def dot(a, b):
    return jnp.dot(a, b, preferred_element_type=jnp.float32)


def kv_kernel(table, act, gain, wk, wv, send, keep):
    scaled = (act[...].astype(jnp.float32) * gain[...]).astype(jnp.bfloat16)
    core = table[0]
    for j in range(send.shape[0]):
        cols = pl.ds(pl.multiple_of(table[1 + j] * HEAD, HEAD), HEAD)
        k = dot(scaled, wk[:, cols])
        v = dot(scaled, wv[:, cols])
        keep[j] = jnp.where(core == 0, k, v)
        send[j] = jnp.where(core == 0, v, k).astype(jnp.bfloat16)


def kv_terms(table, act, gain_own, wk, wv):
    tokens = act.shape[0]
    return pl.pallas_call(
        kv_kernel,
        out_shape=[
            jax.ShapeDtypeStruct((KVH, tokens, HEAD), jnp.bfloat16),
            jax.ShapeDtypeStruct((KVH, tokens, HEAD), jnp.float32),
        ],
        in_specs=[smem(), vmem(), vmem(), vmem(), vmem()],
        out_specs=[vmem(), vmem()],
        compiler_params=pltpu.CompilerParams(vmem_limit_bytes=24 * MIB),
        cost_estimate=pl.CostEstimate(
            flops=4 * tokens * act.shape[1] * KVH * HEAD,
            bytes_accessed=2 * wk.size * 2,
            transcendentals=0,
        ),
    )(table, act, gain_own, wk, wv)


def attend(queries, k_sum, v_sum, cosine, sine, scale):
    k_rows = (k_sum * scale).astype(jnp.bfloat16).astype(jnp.float32)
    value = (v_sum * scale).astype(jnp.bfloat16)

    def rotate(x):
        half = HEAD // 2
        turned = jnp.concatenate([x[:, half:], x[:, :half]], axis=1)
        return (x * cosine + turned * sine).astype(jnp.bfloat16)

    key = rotate(k_rows)
    tokens = key.shape[0]
    rows = lax.broadcasted_iota(jnp.int32, (tokens, tokens), 0)
    cols = lax.broadcasted_iota(jnp.int32, (tokens, tokens), 1)
    out = []
    for h in range(queries.shape[1] // HEAD):
        q = rotate(queries[:, h * HEAD : (h + 1) * HEAD] * scale)
        scores = lax.dot_general(
            q, key, (((1,), (1,)), ((), ())), preferred_element_type=jnp.float32
        ) * HEAD ** (-0.5)
        scores = jnp.where(rows >= cols, scores, -1e30)
        weights = jnp.exp(scores - jnp.max(scores, axis=1, keepdims=True))
        probs = (weights / jnp.sum(weights, axis=1, keepdims=True)).astype(jnp.bfloat16)
        out.append(dot(probs, value).astype(jnp.bfloat16))
    return jnp.concatenate(out, axis=1)


def query_kernel(plan, pieces, last, features, *refs):
    table, gain = refs[0], refs[1]
    blocks = refs[2 : 2 + pieces]
    rest = refs[2 + pieces :]
    if last:
        weight, q_in, sq_in, k_sum, v_sum, cosine, sine, out, wbuf, sems = rest
    else:
        weight, q_out, sq_out, wbuf, sems = rest
    depth = wbuf.shape[1]

    def fetch(i):
        start = pl.multiple_of(table[i] * depth, depth)
        return pltpu.make_async_copy(weight.at[pl.ds(start, depth), :], wbuf.at[i], sems.at[i])

    for i in range(len(plan)):
        fetch(i).start()
    if last:
        queries, squares = q_in[...], sq_in[...]
    else:
        queries, squares = None, None
    for i, (piece, block, column) in enumerate(plan):
        x = blocks[piece][block, :, column : column + depth].astype(jnp.float32)
        scaled = (x * gain[pl.ds(table[i], 1), :]).astype(jnp.bfloat16)
        fetch(i).wait()
        term = dot(scaled, wbuf[i])
        queries = term if queries is None else queries + term
        squares = x * x if squares is None else squares + x * x
    if last:
        mean = jnp.sum(squares, axis=1, keepdims=True) * (1.0 / features)
        out[...] = attend(
            queries, k_sum[...], v_sum[...], cosine[...], sine[...], lax.rsqrt(mean + EPS)
        )
    else:
        q_out[...] = queries
        sq_out[...] = squares


def query_call(plan, table, gain, blocks, weight, carry=None, extra=()):
    depth = gain.shape[1]
    tokens, columns = blocks[0].shape[1], weight.shape[1]
    last = carry is not None
    if last:
        out_shape = [jax.ShapeDtypeStruct((tokens, columns), jnp.bfloat16)]
    else:
        out_shape = [
            jax.ShapeDtypeStruct((tokens, columns), jnp.float32),
            jax.ShapeDtypeStruct((tokens, depth), jnp.float32),
        ]
    more = (list(carry) + list(extra)) if last else []
    return pl.pallas_call(
        functools.partial(query_kernel, plan, len(blocks), last, weight.shape[0]),
        out_shape=out_shape,
        in_specs=[smem(), vmem()] + [vmem()] * len(blocks) + [hbm()] + [vmem()] * len(more),
        out_specs=[vmem()] * len(out_shape),
        scratch_shapes=[
            pltpu.VMEM((len(plan), depth, columns), jnp.bfloat16),
            pltpu.SemaphoreType.DMA((len(plan),)),
        ],
        compiler_params=pltpu.CompilerParams(vmem_limit_bytes=32 * MIB),
        cost_estimate=pl.CostEstimate(
            flops=2 * tokens * columns * depth * len(plan),
            bytes_accessed=2 * columns * depth * len(plan),
            transcendentals=0,
        ),
    )(table, gain, *blocks, weight, *more)


def output_kernel(sizes, added, table, attended, *refs):
    if added:
        arrived, weight, refs = refs[0], refs[1], refs[2:]
    else:
        arrived, weight, refs = None, refs[0], refs[1:]
    outs, wbuf, sems = refs[: len(sizes)], refs[len(sizes)], refs[len(sizes) + 1]
    width = wbuf.shape[2]

    def fetch(i):
        start = pl.multiple_of(table[i] * width, width)
        return pltpu.make_async_copy(weight.at[:, pl.ds(start, width)], wbuf.at[i], sems.at[i])

    for i in range(sum(sizes)):
        fetch(i).start()
    i = 0
    for out in outs:
        for j in range(out.shape[0]):
            fetch(i).wait()
            term = dot(attended[...], wbuf[i])
            if added:
                term = term + arrived[i].astype(jnp.float32)
            out[j] = term.astype(out.dtype)
            i += 1


def output_call(sizes, dtype, table, attended, weight, width, arrived=None):
    tokens, depth = attended.shape
    count = sum(sizes)
    added = arrived is not None
    return pl.pallas_call(
        functools.partial(output_kernel, sizes, added),
        out_shape=[jax.ShapeDtypeStruct((s, tokens, width), dtype) for s in sizes],
        in_specs=[smem(), vmem()] + [vmem()] * added + [hbm()],
        out_specs=[vmem()] * len(sizes),
        scratch_shapes=[
            pltpu.VMEM((count, depth, width), jnp.bfloat16),
            pltpu.SemaphoreType.DMA((count,)),
        ],
        compiler_params=pltpu.CompilerParams(vmem_limit_bytes=32 * MIB),
        cost_estimate=pl.CostEstimate(
            flops=2 * tokens * depth * width * count,
            bytes_accessed=2 * depth * width * count,
            transcendentals=0,
        ),
    )(table, attended, *([arrived] if added else []), weight)


def rotary_tables(tokens):
    half = HEAD // 2
    frequency = 500000.0 ** (-(jnp.arange(half, dtype=jnp.float32) * 2.0) / HEAD)
    angles = jnp.arange(tokens, dtype=jnp.float32)[:, None] * frequency[None, :]
    cosine, sine = jnp.cos(angles), jnp.sin(angles)
    return jnp.concatenate([cosine, cosine], axis=1), jnp.concatenate([-sine, sine], axis=1)


def per_device(n, act, norm_gain, wq, wk, wv, wo):
    tokens, width = act.shape
    me = lax.axis_index("wide")
    count = n.bit_length() - 1
    bits = [1 << i for i in range(count)]
    core = bits[0]
    parts = 2 if width % 256 == 0 else 1
    depth = width // parts
    orders = [(bits[1], bits[2]), (bits[2], bits[1])][:parts]
    far = combos(bits[3:])
    swap = functools.partial(exchange, n=n)

    def halves(x, p):
        return x[..., p * depth : (p + 1) * depth]

    def index_of(offset, p):
        return (me ^ offset) * parts + p

    def table_of(pairs):
        return jnp.stack([index_of(o, p) for o, p in pairs]).astype(jnp.int32)

    shared = (n // KVH).bit_length() - 1
    first, others = bits[shared], combos(bits[shared + 1 :])
    head_offsets = [o ^ first for o in others] + others
    is_core0 = (me & core) == 0
    kv_table = jnp.stack([me & core] + [(me ^ o) >> shared for o in head_offsets]).astype(jnp.int32)
    gain_own = lax.dynamic_slice_in_dim(norm_gain, me * width, width)[None, :]
    kv_send, kv_keep = kv_terms(kv_table, act, gain_own, wk, wv)
    kv = kv_keep + swap(kv_send, core).astype(jnp.float32)
    kv = kv[len(others) :] + swap(kv[: len(others)].astype(jnp.bfloat16), first).astype(jnp.float32)
    total = kv[0]
    for i, o in enumerate(others):
        if o:
            total = total + swap(kv[i].astype(jnp.bfloat16), o).astype(jnp.float32)
    for b in bits[1:shared]:
        total = total + swap(total.astype(jnp.bfloat16), b).astype(jnp.float32)
    other = swap(total, core)
    k_sum = jnp.where(is_core0, total, other)
    v_sum = jnp.where(is_core0, other, total)

    held = jnp.stack([act] + [swap(act, o) for o in far[1:]])
    near = [swap(halves(held, p), orders[p][0]) for p in range(parts)]
    last = [
        swap(jnp.concatenate([halves(held, p), near[p]]), orders[p][1]) for p in range(parts)
    ]
    held_other = swap(held, core)
    near_other = [swap(x, core) for x in near]
    last_other = [swap(x, core) for x in last]

    def plan_of(groups):
        plan, pairs = [], []
        for piece, (offsets, ps) in enumerate(groups):
            for p in ps:
                for block, o in enumerate(offsets):
                    plan.append((piece, block, ps.index(p) * depth))
                    pairs.append((o, p))
        return plan, table_of(pairs)

    near_of = [[o ^ orders[p][0] for o in far] for p in range(parts)]
    last_of = [[o ^ orders[p][1] for o in far + near_of[p]] for p in range(parts)]
    every = list(range(parts))
    gain = norm_gain.reshape(n * parts, depth)

    def both(offsets, ps):
        return [(offsets, ps), ([o ^ core for o in offsets], ps)]

    groups = both(far, every)
    blocks = [held, held_other]
    for p in every:
        groups += both(near_of[p], [p])
        blocks += [near[p], near_other[p]]
    plan, table = plan_of(groups)
    carry = query_call(plan, table, gain, blocks, wq)
    groups, blocks = [], []
    for p in every:
        groups += both(last_of[p], [p])
        blocks += [last[p], last_other[p]]
    plan, table = plan_of(groups)
    cosine, sine = rotary_tables(tokens)
    (attended,) = query_call(
        plan, table, gain, blocks, wq, carry, (k_sum, v_sum, cosine, sine)
    )

    def offsets_of(p, first_set):
        a, b = orders[p]
        low = [o ^ b for o in far] + far
        return [o ^ a for o in low] if first_set else low

    sizes = [2 * len(far)] * parts

    def table_for(first_set, other_core):
        return table_of(
            [
                (o ^ core if other_core else o, p)
                for p in every
                for o in offsets_of(p, first_set)
            ]
        )

    whole = [sum(sizes)]
    (send_1,) = output_call(whole, jnp.bfloat16, table_for(True, True), attended, wo, depth)
    got_1 = swap(send_1, core)
    (send_2,) = output_call(whole, jnp.bfloat16, table_for(False, True), attended, wo, depth)
    got_2 = swap(send_2, core)
    firsts = output_call(sizes, jnp.bfloat16, table_for(True, False), attended, wo, depth, got_1)
    got_first = [swap(firsts[p], orders[p][0]) for p in every]
    keeps = output_call(sizes, jnp.float32, table_for(False, False), attended, wo, depth, got_2)
    f = len(far)
    finals = []
    for p in every:
        send = (keeps[p][:f] + got_first[p][:f].astype(jnp.float32)).astype(jnp.bfloat16)
        got = swap(send, orders[p][1])
        keep = keeps[p][f:] + got_first[p][f:].astype(jnp.float32)
        finals.append(keep + got.astype(jnp.float32))
    final = jnp.concatenate(finals, axis=2)
    out = final[0]
    for i in range(1, f):
        out = out + swap(final[i].astype(jnp.bfloat16), far[i]).astype(jnp.float32)
    return out.astype(jnp.bfloat16)


def solution(mesh):
    return jax.shard_map(
        functools.partial(per_device, mesh.shape["wide"]),
        mesh=mesh,
        in_specs=(
            P("groups", "wide"),
            P(),
            P(None, "wide"),
            P("wide", None),
            P("wide", None),
            P("wide", None),
        ),
        out_specs=P("groups", "wide"),
        check_vma=False,
    )
```

```python
import functools

import jax
import jax.numpy as jnp
from jax import lax
from jax.experimental import pallas as pl
from jax.experimental.pallas import tpu as pltpu
from jax.sharding import PartitionSpec as P

HEADS = 128
KVH = 8
HEAD = 128
LANE = 128
EPS = 1e-05
MIB = 1 << 20
CORE = 1


def combos(bits):
    out = [0]
    for b in bits:
        out = out + [o ^ b for o in out]
    return out


def vmem():
    return pl.BlockSpec(memory_space=pltpu.VMEM)


def smem():
    return pl.BlockSpec(memory_space=pltpu.SMEM)


def hbm():
    return pl.BlockSpec(memory_space=pltpu.HBM)


def dot(a, b):
    return jnp.dot(a, b, preferred_element_type=jnp.float32)


def kv_kernel(shared, where, act, gain, wk, wv, send, keep):
    me = where[0]
    width = act.shape[1]
    own = gain[:, pl.ds(pl.multiple_of(me * width, LANE), width)]
    scaled = (act[...].astype(jnp.float32) * own).astype(jnp.bfloat16)
    k, v = dot(scaled, wk[...]), dot(scaled, wv[...])
    core0 = (me & CORE) == 0
    for h in range(KVH):
        off = h ^ (me >> shared)
        spot = ((off & 1) ^ 1) * (KVH // 2) + (off >> 1)
        kh, vh = k[:, h * HEAD : (h + 1) * HEAD], v[:, h * HEAD : (h + 1) * HEAD]
        keep[spot] = jnp.where(core0, kh, vh)
        send[spot] = jnp.where(core0, vh, kh)


def kv_terms(shared, where, act, gain, wk, wv):
    tokens = act.shape[0]
    return pl.pallas_call(
        functools.partial(kv_kernel, shared),
        out_shape=[jax.ShapeDtypeStruct((KVH, tokens, HEAD), jnp.float32)] * 2,
        in_specs=[smem(), vmem(), vmem(), vmem(), vmem()],
        out_specs=[vmem(), vmem()],
        compiler_params=pltpu.CompilerParams(vmem_limit_bytes=24 * MIB),
        cost_estimate=pl.CostEstimate(
            flops=4 * tokens * wk.size, bytes_accessed=4 * wk.size, transcendentals=0
        ),
    )(where, act, gain, wk, wv)


def attend(queries, k_sum, v_sum, cosine, sine, scale):
    k_rows = (k_sum * scale).astype(jnp.bfloat16).astype(jnp.float32)
    value = (v_sum * scale).astype(jnp.bfloat16)

    def rotate(x):
        half = HEAD // 2
        turned = jnp.concatenate([x[:, half:], x[:, :half]], axis=1)
        return (x * cosine + turned * sine).astype(jnp.bfloat16)

    key = rotate(k_rows)
    tokens = key.shape[0]
    rows = lax.broadcasted_iota(jnp.int32, (tokens, tokens), 0)
    cols = lax.broadcasted_iota(jnp.int32, (tokens, tokens), 1)
    out = []
    for h in range(queries.shape[1] // HEAD):
        q = rotate(queries[:, h * HEAD : (h + 1) * HEAD] * scale)
        scores = lax.dot_general(
            q, key, (((1,), (1,)), ((), ())), preferred_element_type=jnp.float32
        ) * HEAD ** (-0.5)
        scores = jnp.where(rows >= cols, scores, -1e30)
        weights = jnp.exp(scores - jnp.max(scores, axis=1, keepdims=True))
        probs = (weights / jnp.sum(weights, axis=1, keepdims=True)).astype(jnp.bfloat16)
        out.append(dot(probs, value).astype(jnp.bfloat16))
    return jnp.concatenate(out, axis=1)


def query_kernel(places, width, carried, last, *refs):
    refs = list(refs)
    where, gain = refs.pop(0), refs.pop(0)
    pieces = [refs.pop(0) for _ in places]
    weight = refs.pop(0)
    queries = refs.pop(0)[...] if carried else None
    squares = refs.pop(0)[...] if carried else None
    extra = [refs.pop(0) for _ in range(4)] if last else None
    outs = [refs.pop(0) for _ in range(1 if last else 2)]
    sems = refs.pop()
    bufs = refs

    fetches, starts, i = [], [], 0
    for piece, (symbols, first), buf in zip(pieces, places, bufs):
        depth = piece.shape[2]
        mine = []
        for block, (const, pick) in enumerate(symbols):
            start = pl.multiple_of((where[pick] ^ const) * width + first, LANE)
            copy = pltpu.make_async_copy(
                weight.at[pl.ds(start, depth), :],
                buf.at[pl.ds(block * depth, depth), :],
                sems.at[i],
            )
            copy.start()
            mine.append((start, copy))
            i += 1
        fetches.append(mine)
    for piece, mine, buf in zip(pieces, fetches, bufs):
        depth = piece.shape[2]
        scaled = []
        for block, (start, _) in enumerate(mine):
            x = piece[block].astype(jnp.float32)
            scaled.append((x * gain[:, pl.ds(start, depth)]).astype(jnp.bfloat16))
            for c in range(0, depth, LANE):
                square = x[:, c : c + LANE] * x[:, c : c + LANE]
                squares = square if squares is None else squares + square
        for _, copy in mine:
            copy.wait()
        term = dot(jnp.concatenate(scaled, axis=1), buf[...])
        queries = term if queries is None else queries + term
    if last:
        mean = jnp.sum(squares, axis=1, keepdims=True) * (1.0 / weight.shape[0])
        mine, other, cosine, sine = extra
        core0 = (where[0] & CORE) == 0
        k_sum = jnp.where(core0, mine[...], other[...])
        v_sum = jnp.where(core0, other[...], mine[...])
        outs[0][...] = attend(
            queries, k_sum, v_sum, cosine[...], sine[...], lax.rsqrt(mean + EPS)
        )
    else:
        outs[0][...] = queries
        outs[1][...] = squares


def query_call(where, gain, pieces, weight, width, carry=(), extra=()):
    arrays = [a for a, _, _ in pieces]
    places = [(symbols, first) for _, symbols, first in pieces]
    tokens, columns = arrays[0].shape[1], weight.shape[1]
    if extra:
        out_shape = [jax.ShapeDtypeStruct((tokens, columns), jnp.bfloat16)]
    else:
        out_shape = [
            jax.ShapeDtypeStruct((tokens, columns), jnp.float32),
            jax.ShapeDtypeStruct((tokens, LANE), jnp.float32),
        ]
    rows = [a.shape[0] * a.shape[2] for a in arrays]
    return pl.pallas_call(
        functools.partial(query_kernel, places, width, bool(carry), bool(extra)),
        out_shape=out_shape,
        in_specs=[smem(), vmem()]
        + [vmem()] * len(arrays)
        + [hbm()]
        + [vmem()] * (len(carry) + len(extra)),
        out_specs=[vmem()] * len(out_shape),
        scratch_shapes=[pltpu.VMEM((r, columns), weight.dtype) for r in rows]
        + [pltpu.SemaphoreType.DMA((sum(a.shape[0] for a in arrays),))],
        compiler_params=pltpu.CompilerParams(vmem_limit_bytes=50 * MIB),
        cost_estimate=pl.CostEstimate(
            flops=2 * tokens * columns * sum(rows),
            bytes_accessed=2 * columns * sum(rows),
            transcendentals=0,
        ),
    )(where, gain, *arrays, weight, *carry, *extra)


def output_kernel(groups, width, where, attended, *refs):
    refs = list(refs)
    added = [refs.pop(0) if g[3] else None for g in groups]
    weight = refs.pop(0)
    outs = [refs.pop(0) for _ in groups]
    sems = refs.pop()
    fetches, i = [], 0
    for (symbols, first, size, _), buf in zip(groups, refs):
        mine = []
        for block, (const, pick) in enumerate(symbols):
            start = pl.multiple_of((where[pick] ^ const) * width + first, LANE)
            copy = pltpu.make_async_copy(
                weight.at[:, pl.ds(start, size)],
                buf.at[:, pl.ds(block * size, size)],
                sems.at[i],
            )
            copy.start()
            mine.append(copy)
            i += 1
        fetches.append(mine)
    left = attended[...]
    for (symbols, _, size, _), arrived, out, mine, buf in zip(groups, added, outs, fetches, refs):
        for copy in mine:
            copy.wait()
        terms = dot(left, buf[...])
        for block in range(len(symbols)):
            term = terms[:, block * size : (block + 1) * size]
            if arrived is not None:
                term = term + arrived[block].astype(jnp.float32)
            out[block] = term.astype(out.dtype)


def output_call(where, attended, weight, width, groups):
    tokens, depth = attended.shape
    columns = [len(symbols) * size for symbols, _, size, _, _ in groups]
    added = [g[4] for g in groups if g[4] is not None]
    return pl.pallas_call(
        functools.partial(
            output_kernel, [(s, f, c, a is not None) for s, f, c, _, a in groups], width
        ),
        out_shape=[
            jax.ShapeDtypeStruct((len(s), tokens, c), dtype) for s, _, c, dtype, _ in groups
        ],
        in_specs=[smem(), vmem()] + [vmem()] * len(added) + [hbm()],
        out_specs=[vmem()] * len(groups),
        scratch_shapes=[pltpu.VMEM((depth, c), weight.dtype) for c in columns]
        + [pltpu.SemaphoreType.DMA((sum(len(g[0]) for g in groups),))],
        compiler_params=pltpu.CompilerParams(vmem_limit_bytes=50 * MIB),
        cost_estimate=pl.CostEstimate(
            flops=2 * tokens * depth * sum(columns),
            bytes_accessed=2 * depth * sum(columns),
            transcendentals=0,
        ),
    )(where, attended, *added, weight)


def rotary_tables(tokens):
    half = HEAD // 2
    frequency = 500000.0 ** (-(jnp.arange(half, dtype=jnp.float32) * 2.0) / HEAD)
    angles = jnp.arange(tokens, dtype=jnp.float32)[:, None] * frequency[None, :]
    cosine, sine = jnp.cos(angles), jnp.sin(angles)
    return jnp.concatenate([cosine, cosine], axis=1), jnp.concatenate([-sine, sine], axis=1)


def per_device(n, act, norm_gain, wq, wk, wv, wo):
    tokens, width = act.shape
    me = lax.axis_index("wide")
    bits = [1 << i for i in range(n.bit_length() - 1)]
    side = (bits[1], bits[2])
    diagonal = bits[1] ^ bits[2]
    far = combos(bits[3:])
    f = len(far)
    late = LANE if width >= 4 * LANE else 0
    early = width - late
    f32, bf16 = jnp.float32, jnp.bfloat16

    def swap(x, offset):
        return lax.ppermute(x, "wide", [(i, i ^ offset) for i in range(n)])

    def turn(x, step):
        return lax.ppermute(x, "wide", [(i, i ^ side[(step + (i & CORE)) % 2]) for i in range(n)])

    bit = jnp.where((me & CORE) == 0, side[0], side[1])
    where = jnp.stack([me, me ^ bit, me ^ bit ^ diagonal]).astype(jnp.int32)
    gain = norm_gain.reshape(1, -1)

    def plain(offsets, pick=0):
        return [(o, pick) for o in offsets]

    def across(symbols):
        return [(const ^ CORE, (0, 2, 1)[pick]) for const, pick in symbols]

    square = [(0, 0), (0, 1), (0, 2), (diagonal, 0)]

    def shift(symbols, offset):
        return [(const ^ offset, pick) for const, pick in symbols]

    mine = act[:, :early]
    got = [swap(mine, o) for o in far[1:]]
    row = jnp.stack([mine] + got)
    if late:
        own = act[:, early:]
        one, two = turn(own, 0), turn(own, 1)
        plane = jnp.stack([own, one, two, turn(one, 1)])
        planes = [swap(plane, o) for o in far[1:]]
    side_1, side_2 = turn(row, 0), turn(row, 1)
    corner = turn(side_1, 1)

    shared = (n // KVH).bit_length() - 1
    act_kv = lax.optimization_barrier((act, got[0]))[0]
    others = combos(bits[shared + 1 :])
    kv_send, kv_keep = kv_terms(shared, where, act_kv, gain, wk, wv)
    kv = kv_keep + swap(kv_send, CORE)
    half = KVH // 2
    kv = kv[half:] + swap(kv[:half].astype(bf16), bits[shared]).astype(f32)
    total = kv[0]
    for i, o in enumerate(others):
        if o:
            total = total + swap(kv[i].astype(bf16), o).astype(f32)
    kv_mine, kv_other = total, None
    for o in combos(bits[:shared])[1:]:
        got = swap(total, o)
        if o & CORE:
            kv_other = got if kv_other is None else kv_other + got
        else:
            kv_mine = kv_mine + got

    def pair(array, symbols, first):
        return [(array, symbols, first)], [(swap(array, CORE), across(symbols), first)]

    row_own, row_other = pair(row, plain(far), 0)
    one_own, one_other = pair(side_1, plain(far, 1), 0)
    two_own, two_other = pair(side_2, plain(far, 2), 0)
    plane_own, plane_other, planes_own, planes_other = [], [], [], []
    if late:
        plane_own, plane_other = pair(plane, square, early)
    call = functools.partial(query_call, where, gain, weight=wq, width=width)
    carry = call(row_own + row_other)
    carry = call(one_own + two_own + plane_own + plane_other, carry=carry)
    corner, *carry = lax.optimization_barrier((corner, *carry))
    corner_own, corner_other = pair(corner, plain([o ^ diagonal for o in far]), 0)
    if late:
        for o, array in zip(far[1:], planes):
            a, b = pair(array, shift(square, o), early)
            planes_own += a
            planes_other += b
    carry = call(one_other + two_other + corner_own, carry=carry)
    (attended,) = call(
        corner_other + planes_own + planes_other,
        carry=carry,
        extra=(kv_mine, kv_other, *rotary_tables(tokens)),
    )

    at_corner = plain([o ^ diagonal for o in far])
    at_one, at_two, at_home = plain(far, 1), plain(far, 2), plain(far)
    leave = [(at_corner, 0, early, bf16)]
    stay = [
        (at_two, 0, early, f32),
        (at_one, 0, early, bf16),
        (at_home, 0, early, f32),
    ]
    if late:
        leave += [(shift(square, o), early, late, bf16) for o in far[1:]]
        stay += [(square, early, late, f32)]

    def project(left, groups, arrived=None):
        if arrived is None:
            groups = [(across(s), first, c, bf16, None) for s, first, c, _ in groups]
        else:
            groups = [(*g, a) for g, a in zip(groups, arrived)]
        return output_call(where, left, wo, width, groups)

    send_1 = project(attended, leave)
    attended, *send_1 = lax.optimization_barrier((attended, *send_1))
    send_2 = project(attended, stay)
    leaving = project(attended, leave, [swap(x, CORE) for x in send_1])
    from_corner = turn(leaving[0], 0)
    from_planes = [swap(x, o) for x, o in zip(leaving[1:], far[1:])]
    staying = project(attended, stay, [swap(x, CORE) for x in send_2])
    two, one, home = staying[:3]
    got_1 = turn(one, 0)
    got_2 = turn((two + from_corner.astype(f32)).astype(bf16), 1)
    home = home + got_1.astype(f32) + got_2.astype(f32)
    out = home[0]
    for i in range(1, f):
        out = out + swap(home[i].astype(bf16), far[i]).astype(f32)
    if late:
        plane = staying[3]
        for x in from_planes:
            plane = plane + x.astype(f32)
        got = turn(plane[3].astype(bf16), 0)
        got_1 = turn(plane[1].astype(bf16), 0)
        got_2 = turn((plane[2] + got.astype(f32)).astype(bf16), 1)
        rest = plane[0] + got_1.astype(f32) + got_2.astype(f32)
        out = jnp.concatenate([out, rest], axis=1)
    return out.astype(bf16)


def solution(mesh):
    return jax.shard_map(
        functools.partial(per_device, mesh.shape["wide"]),
        mesh=mesh,
        in_specs=(
            P("groups", "wide"),
            P(),
            P(None, "wide"),
            P("wide", None),
            P("wide", None),
            P("wide", None),
        ),
        out_specs=P("groups", "wide"),
        check_vma=False,
    )
```

```python
import functools

import jax
import jax.numpy as jnp
from jax import lax
from jax.experimental import pallas as pl
from jax.experimental.pallas import tpu as pltpu
from jax.sharding import PartitionSpec as P

HEADS = 128
KVH = 8
HEAD = 128
LANE = 128
EPS = 1e-05
MIB = 1 << 20
CORE = 1


def combos(bits):
    out = [0]
    for b in bits:
        out = out + [o ^ b for o in out]
    return out


def vmem():
    return pl.BlockSpec(memory_space=pltpu.VMEM)


def smem():
    return pl.BlockSpec(memory_space=pltpu.SMEM)


def hbm():
    return pl.BlockSpec(memory_space=pltpu.HBM)


def in_hbm(x):
    return pltpu.with_memory_space_constraint(x, pltpu.HBM)


def dot(a, b):
    return jnp.dot(a, b, preferred_element_type=jnp.float32)


def fetch_kernel(source, target, sems):
    count = sems.shape[0]
    rows = source.shape[0] // count
    copies = [
        pltpu.make_async_copy(
            source.at[pl.ds(i * rows, rows), :], target.at[pl.ds(i * rows, rows), :], sems.at[i]
        )
        for i in range(count)
    ]
    for copy in copies:
        copy.start()
    for copy in copies:
        copy.wait()


def fetched(weight):
    return pl.pallas_call(
        fetch_kernel,
        out_shape=jax.ShapeDtypeStruct(weight.shape, weight.dtype),
        in_specs=[hbm()],
        out_specs=vmem(),
        scratch_shapes=[pltpu.SemaphoreType.DMA((8,))],
        compiler_params=pltpu.CompilerParams(vmem_limit_bytes=MIB),
        cost_estimate=pl.CostEstimate(
            flops=0, bytes_accessed=4 * weight.size, transcendentals=0
        ),
    )(in_hbm(weight))


def kv_kernel(shared, where, act, gain, wk, wv, send, keep, kbuf, vbuf, sems):
    copies = [
        pltpu.make_async_copy(wk, kbuf, sems.at[0]),
        pltpu.make_async_copy(wv, vbuf, sems.at[1]),
    ]
    for c in copies:
        c.start()
    me = where[0]
    width = act.shape[1]
    own = gain[:, pl.ds(pl.multiple_of(me * width, LANE), width)]
    scaled = (act[...].astype(jnp.float32) * own).astype(jnp.bfloat16)
    for c in copies:
        c.wait()
    k, v = dot(scaled, kbuf[...]), dot(scaled, vbuf[...])
    core0 = (me & CORE) == 0
    for h in range(KVH):
        off = h ^ (me >> shared)
        spot = ((off & 1) ^ 1) * (KVH // 2) + (off >> 1)
        kh, vh = k[:, h * HEAD : (h + 1) * HEAD], v[:, h * HEAD : (h + 1) * HEAD]
        keep[spot] = jnp.where(core0, kh, vh)
        send[spot] = jnp.where(core0, vh, kh)


def kv_terms(shared, where, act, gain, wk, wv):
    tokens = act.shape[0]
    return pl.pallas_call(
        functools.partial(kv_kernel, shared),
        out_shape=[jax.ShapeDtypeStruct((KVH, tokens, HEAD), jnp.float32)] * 2,
        in_specs=[smem(), vmem(), vmem(), hbm(), hbm()],
        out_specs=[vmem(), vmem()],
        scratch_shapes=[
            pltpu.VMEM(wk.shape, wk.dtype),
            pltpu.VMEM(wv.shape, wv.dtype),
            pltpu.SemaphoreType.DMA((2,)),
        ],
        compiler_params=pltpu.CompilerParams(vmem_limit_bytes=12 * MIB),
        cost_estimate=pl.CostEstimate(
            flops=4 * tokens * wk.size, bytes_accessed=4 * wk.size, transcendentals=0
        ),
    )(where, act, gain, in_hbm(wk), in_hbm(wv))


def attend(queries, k_sum, v_sum, cosine, sine, scale):
    k_rows = (k_sum * scale).astype(jnp.bfloat16).astype(jnp.float32)
    value = (v_sum * scale).astype(jnp.bfloat16)

    def rotate(x):
        half = HEAD // 2
        turned = jnp.concatenate([x[:, half:], x[:, :half]], axis=1)
        return (x * cosine + turned * sine).astype(jnp.bfloat16)

    key = rotate(k_rows)
    tokens = key.shape[0]
    rows = lax.broadcasted_iota(jnp.int32, (tokens, tokens), 0)
    cols = lax.broadcasted_iota(jnp.int32, (tokens, tokens), 1)
    out = []
    for h in range(queries.shape[1] // HEAD):
        q = rotate(queries[:, h * HEAD : (h + 1) * HEAD] * scale)
        scores = lax.dot_general(
            q, key, (((1,), (1,)), ((), ())), preferred_element_type=jnp.float32
        ) * HEAD ** (-0.5)
        scores = jnp.where(rows >= cols, scores, -1e30)
        weights = jnp.exp(scores - jnp.max(scores, axis=1, keepdims=True))
        probs = (weights / jnp.sum(weights, axis=1, keepdims=True)).astype(jnp.bfloat16)
        out.append(dot(probs, value).astype(jnp.bfloat16))
    return jnp.concatenate(out, axis=1)


def query_kernel(places, carried, last, *refs):
    refs = list(refs)
    where, gain = refs.pop(0), refs.pop(0)
    pieces = [refs.pop(0) for _ in places]
    weight = refs.pop(0)
    queries = refs.pop(0)[...] if carried else None
    squares = refs.pop(0)[...] if carried else None
    for piece, symbols in zip(pieces, places):
        width = piece.shape[2]
        for block, (const, pick) in enumerate(symbols):
            span = pl.ds(pl.multiple_of((where[pick] ^ const) * width, LANE), width)
            x = piece[block].astype(jnp.float32)
            term = dot((x * gain[:, span]).astype(jnp.bfloat16), weight[span, :])
            queries = term if queries is None else queries + term
            for c in range(0, width, LANE):
                square = x[:, c : c + LANE] * x[:, c : c + LANE]
                squares = square if squares is None else squares + square
    if last:
        mean = jnp.sum(squares, axis=1, keepdims=True) * (1.0 / weight.shape[0])
        mine, other, cosine, sine, out = refs
        core0 = (where[0] & CORE) == 0
        k_sum = jnp.where(core0, mine[...], other[...])
        v_sum = jnp.where(core0, other[...], mine[...])
        out[...] = attend(
            queries, k_sum, v_sum, cosine[...], sine[...], lax.rsqrt(mean + EPS)
        )
    else:
        refs[0][...] = queries
        refs[1][...] = squares


def query_call(where, gain, pieces, weight, carry=(), extra=()):
    arrays, places = [a for a, _ in pieces], [symbols for _, symbols in pieces]
    tokens, columns = arrays[0].shape[1], weight.shape[1]
    if extra:
        out_shape = [jax.ShapeDtypeStruct((tokens, columns), jnp.bfloat16)]
    else:
        out_shape = [
            jax.ShapeDtypeStruct((tokens, columns), jnp.float32),
            jax.ShapeDtypeStruct((tokens, LANE), jnp.float32),
        ]
    rows = sum(a.shape[0] * a.shape[2] for a in arrays)
    count = 1 + len(arrays) + 1 + len(carry) + len(extra)
    return pl.pallas_call(
        functools.partial(query_kernel, places, bool(carry), bool(extra)),
        out_shape=out_shape,
        in_specs=[smem()] + [vmem()] * count,
        out_specs=[vmem()] * len(out_shape),
        compiler_params=pltpu.CompilerParams(vmem_limit_bytes=12 * MIB),
        cost_estimate=pl.CostEstimate(
            flops=2 * tokens * columns * rows,
            bytes_accessed=2 * columns * rows,
            transcendentals=0,
        ),
    )(where, gain, *arrays, weight, *carry, *extra)


def output_kernel(groups, width, where, attended, *refs):
    refs = list(refs)
    added = [refs.pop(0) if g[1] else None for g in groups]
    weight = refs.pop(0)
    left = attended[...]
    for (symbols, _), arrived, out in zip(groups, added, refs):
        for block, (const, pick) in enumerate(symbols):
            span = pl.ds(pl.multiple_of((where[pick] ^ const) * width, LANE), width)
            term = dot(left, weight[:, span])
            if arrived is not None:
                term = term + arrived[block].astype(jnp.float32)
            out[block] = term.astype(out.dtype)


def output_call(where, attended, weight, width, groups):
    tokens, depth = attended.shape
    blocks = sum(len(g[0]) for g in groups)
    added = [g[2] for g in groups if g[2] is not None]
    return pl.pallas_call(
        functools.partial(output_kernel, [(s, a is not None) for s, _, a in groups], width),
        out_shape=[jax.ShapeDtypeStruct((len(s), tokens, width), t) for s, t, _ in groups],
        in_specs=[smem()] + [vmem()] * (2 + len(added)),
        out_specs=[vmem()] * len(groups),
        compiler_params=pltpu.CompilerParams(vmem_limit_bytes=12 * MIB),
        cost_estimate=pl.CostEstimate(
            flops=2 * tokens * depth * width * blocks,
            bytes_accessed=2 * depth * width * blocks,
            transcendentals=0,
        ),
    )(where, attended, *added, weight)


def rotary_tables(tokens):
    half = HEAD // 2
    frequency = 500000.0 ** (-(jnp.arange(half, dtype=jnp.float32) * 2.0) / HEAD)
    angles = jnp.arange(tokens, dtype=jnp.float32)[:, None] * frequency[None, :]
    cosine, sine = jnp.cos(angles), jnp.sin(angles)
    return jnp.concatenate([cosine, cosine], axis=1), jnp.concatenate([-sine, sine], axis=1)


def per_device(n, act, norm_gain, wq, wk, wv, wo):
    tokens, width = act.shape
    me = lax.axis_index("wide")
    bits = [1 << i for i in range(n.bit_length() - 1)]
    side = (bits[1], bits[2])
    diagonal = bits[1] ^ bits[2]
    far = combos(bits[3:])
    f32, bf16 = jnp.float32, jnp.bfloat16

    def swap(x, offset):
        return lax.ppermute(x, "wide", [(i, i ^ offset) for i in range(n)])

    def turn(x, step):
        return lax.ppermute(x, "wide", [(i, i ^ side[(step + (i & CORE)) % 2]) for i in range(n)])

    bit = jnp.where((me & CORE) == 0, side[0], side[1])
    where = jnp.stack([me, me ^ bit, me ^ bit ^ diagonal]).astype(jnp.int32)
    gain = norm_gain.reshape(1, -1)

    def plain(offsets, pick=0):
        return [(o, pick) for o in offsets]

    def across(symbols):
        return [(const ^ CORE, (0, 2, 1)[pick]) for const, pick in symbols]

    at_home, at_one, at_two = plain(far), plain(far, 1), plain(far, 2)
    at_corner = plain([o ^ diagonal for o in far])

    shared = (n // KVH).bit_length() - 1
    others = combos(bits[shared + 1 :])
    kv_send, kv_keep = kv_terms(shared, where, act, gain, wk, wv)
    kv = kv_keep + swap(kv_send, CORE)
    half = KVH // 2
    kv = kv[half:] + swap(kv[:half].astype(bf16), bits[shared]).astype(f32)
    total = kv[0]
    for i, o in enumerate(others):
        if o:
            total = total + swap(kv[i].astype(bf16), o).astype(f32)
    for b in bits[1:shared]:
        total = total + swap(total.astype(bf16), b).astype(f32)
    kv_sums = (total, swap(total, CORE))

    row = jnp.stack([act] + [swap(act, o) for o in far[1:]])
    row, wq = lax.optimization_barrier((row, fetched(wq)))
    side_1, side_2 = turn(row, 0), turn(row, 1)
    corner = turn(side_1, 1)
    call = functools.partial(query_call, where, gain, weight=wq)
    carry = call([(row, at_home), (swap(row, CORE), across(at_home))])
    carry = call([(side_1, at_one), (side_2, at_two)], carry=carry)
    corner, wo, *carry = lax.optimization_barrier((corner, fetched(wo), *carry))
    carry = call(
        [
            (swap(side_1, CORE), across(at_one)),
            (swap(side_2, CORE), across(at_two)),
            (corner, at_corner),
        ],
        carry=carry,
    )
    (attended,) = call(
        [(swap(corner, CORE), across(at_corner))],
        carry=carry,
        extra=(*kv_sums, *rotary_tables(tokens)),
    )

    leave = [(at_corner, bf16)]
    stay = [(at_two, f32), (at_one, bf16), (at_home, f32)]

    def project(left, groups, arrived=None):
        if arrived is None:
            groups = [(across(s), bf16, None) for s, _ in groups]
        else:
            groups = [(*g, a) for g, a in zip(groups, arrived)]
        return output_call(where, left, wo, width, groups)

    send_1 = project(attended, leave)
    attended, *send_1 = lax.optimization_barrier((attended, *send_1))
    send_2 = project(attended, stay)
    (leaving,) = project(attended, leave, [swap(x, CORE) for x in send_1])
    from_corner = turn(leaving, 0)
    two, one, home = project(attended, stay, [swap(x, CORE) for x in send_2])
    got_1 = turn(one, 0)
    got_2 = turn((two + from_corner.astype(f32)).astype(bf16), 1)
    home = home + got_1.astype(f32) + got_2.astype(f32)
    out = home[0]
    for i, o in enumerate(far):
        if o:
            out = out + swap(home[i].astype(bf16), o).astype(f32)
    return out.astype(bf16)


def solution(mesh):
    return jax.shard_map(
        functools.partial(per_device, mesh.shape["wide"]),
        mesh=mesh,
        in_specs=(
            P("groups", "wide"),
            P(),
            P(None, "wide"),
            P("wide", None),
            P("wide", None),
            P("wide", None),
        ),
        out_specs=P("groups", "wide"),
        check_vma=False,
    )
```

```python
import functools

import jax
import jax.numpy as jnp
from jax import lax
from jax.experimental import pallas as pl
from jax.experimental.pallas import tpu as pltpu
from jax.sharding import PartitionSpec as P

HEADS = 128
KVH = 8
HEAD = 128
LANE = 128
EPS = 1e-05
MIB = 1 << 20
CORE = 1


def combos(bits):
    out = [0]
    for b in bits:
        out = out + [o ^ b for o in out]
    return out


def vmem():
    return pl.BlockSpec(memory_space=pltpu.VMEM)


def smem():
    return pl.BlockSpec(memory_space=pltpu.SMEM)


def hbm():
    return pl.BlockSpec(memory_space=pltpu.HBM)


def in_hbm(x):
    return pltpu.with_memory_space_constraint(x, pltpu.HBM)


def dot(a, b):
    return jnp.dot(a, b, preferred_element_type=jnp.float32)


def kv_kernel(shared, where, act, gain, wk, wv, send, keep, abuf, gbuf, kbuf, vbuf, sems):
    me = where[0]
    width = act.shape[1]
    own = pl.ds(pl.multiple_of(me * width, LANE), width)
    pairs = [(act, abuf), (gain.at[:, own], gbuf), (wk, kbuf), (wv, vbuf)]
    copies = [pltpu.make_async_copy(x, y, sems.at[i]) for i, (x, y) in enumerate(pairs)]
    for c in copies:
        c.start()
    for c in copies:
        c.wait()
    scaled = (abuf[...].astype(jnp.float32) * gbuf[...]).astype(jnp.bfloat16)
    k, v = dot(scaled, kbuf[...]), dot(scaled, vbuf[...])
    core0 = (me & CORE) == 0
    for h in range(KVH):
        off = h ^ (me >> shared)
        spot = 0
        for b in range(KVH.bit_length() - 1):
            spot = spot * 2 + (1 - ((off >> b) & 1))
        kh, vh = k[:, h * HEAD : (h + 1) * HEAD], v[:, h * HEAD : (h + 1) * HEAD]
        keep[spot] = jnp.where(core0, kh, vh)
        send[spot] = jnp.where(core0, vh, kh)


def kv_terms(shared, where, act, gain, wk, wv):
    tokens, width = act.shape
    return pl.pallas_call(
        functools.partial(kv_kernel, shared),
        out_shape=[jax.ShapeDtypeStruct((KVH, tokens, HEAD), jnp.float32)] * 2,
        in_specs=[smem()] + [hbm()] * 4,
        out_specs=[vmem(), vmem()],
        scratch_shapes=[
            pltpu.VMEM(act.shape, act.dtype),
            pltpu.VMEM((1, width), gain.dtype),
            pltpu.VMEM(wk.shape, wk.dtype),
            pltpu.VMEM(wv.shape, wv.dtype),
            pltpu.SemaphoreType.DMA((4,)),
        ],
        compiler_params=pltpu.CompilerParams(vmem_limit_bytes=12 * MIB),
        cost_estimate=pl.CostEstimate(
            flops=4 * tokens * wk.size, bytes_accessed=4 * wk.size, transcendentals=0
        ),
    )(where, in_hbm(act), in_hbm(gain), in_hbm(wk), in_hbm(wv))


def attend(queries, k_sum, v_sum, cosine, sine, scale):
    k_rows = (k_sum * scale).astype(jnp.bfloat16).astype(jnp.float32)
    value = (v_sum * scale).astype(jnp.bfloat16)

    def rotate(x):
        half = HEAD // 2
        turned = jnp.concatenate([x[:, half:], x[:, :half]], axis=1)
        return (x * cosine + turned * sine).astype(jnp.bfloat16)

    key = rotate(k_rows)
    tokens = key.shape[0]
    rows = lax.broadcasted_iota(jnp.int32, (tokens, tokens), 0)
    cols = lax.broadcasted_iota(jnp.int32, (tokens, tokens), 1)
    out = []
    for h in range(queries.shape[1] // HEAD):
        q = rotate(queries[:, h * HEAD : (h + 1) * HEAD] * scale)
        scores = lax.dot_general(
            q, key, (((1,), (1,)), ((), ())), preferred_element_type=jnp.float32
        ) * HEAD ** (-0.5)
        scores = jnp.where(rows >= cols, scores, -1e30)
        weights = jnp.exp(scores - jnp.max(scores, axis=1, keepdims=True))
        probs = (weights / jnp.sum(weights, axis=1, keepdims=True)).astype(jnp.bfloat16)
        out.append(dot(probs, value).astype(jnp.bfloat16))
    return jnp.concatenate(out, axis=1)


def query_kernel(places, ahead, carried, last, *refs):
    refs = list(refs)
    where, gain = refs.pop(0), refs.pop(0)
    pieces = [refs.pop(0) for _ in places]
    weight = refs.pop(0)
    queries = refs.pop(0)[...] if carried else None
    squares = refs.pop(0)[...] if carried else None
    extra = [refs.pop(0) for _ in range(4)] if last else None
    outs = [refs.pop(0) for _ in range(1 if last else 3 if ahead else 2)]
    width = pieces[0].shape[2]

    def first_row(symbol):
        return pl.multiple_of((where[symbol[1]] ^ symbol[0]) * width, LANE)

    copies = []
    if refs:
        buf, sems = refs
        wanted = [s for symbols, held in places for s in symbols]
        for i, symbol in enumerate(wanted + list(ahead)):
            target, row = (buf, i) if i < len(wanted) else (outs[2], i - len(wanted))
            copy = pltpu.make_async_copy(
                weight.at[pl.ds(first_row(symbol), width), :],
                target.at[pl.ds(row * width, width), :],
                sems.at[i],
            )
            copy.start()
            copies.append(copy)
    i = 0
    for piece, (symbols, held) in zip(pieces, places):
        for block, symbol in enumerate(symbols):
            x = piece[block].astype(jnp.float32)
            for c in range(0, width, LANE):
                square = x[:, c : c + LANE] * x[:, c : c + LANE]
                squares = square if squares is None else squares + square
            scaled = (x * gain[:, pl.ds(first_row(symbol), width)]).astype(jnp.bfloat16)
            if copies:
                copies[i].wait()
                rows = buf[i * width : (i + 1) * width, :]
            else:
                rows = weight[(held + block) * width : (held + block + 1) * width, :]
            term = dot(scaled, rows)
            queries = term if queries is None else queries + term
            i += 1
    for copy in copies[i:]:
        copy.wait()
    if last:
        mean = jnp.sum(squares, axis=1, keepdims=True) * (1.0 / gain.shape[1])
        mine, other, cosine, sine = extra
        core0 = (where[0] & CORE) == 0
        k_sum = jnp.where(core0, mine[...], other[...])
        v_sum = jnp.where(core0, other[...], mine[...])
        outs[0][...] = attend(
            queries, k_sum, v_sum, cosine[...], sine[...], lax.rsqrt(mean + EPS)
        )
    else:
        outs[0][...] = queries
        outs[1][...] = squares


def query_call(where, gain, pieces, weight, carry=(), extra=(), ahead=(), held=None):
    arrays, places, row = [], [], held or 0
    for array, symbols in pieces:
        arrays.append(array)
        places.append((symbols, row))
        row += len(symbols)
    tokens, width, columns = *arrays[0].shape[1:], weight.shape[1]
    blocks = sum(len(symbols) for symbols, _ in places)
    if extra:
        out_shape = [jax.ShapeDtypeStruct((tokens, columns), jnp.bfloat16)]
    else:
        out_shape = [
            jax.ShapeDtypeStruct((tokens, columns), jnp.float32),
            jax.ShapeDtypeStruct((tokens, LANE), jnp.float32),
        ]
    if ahead:
        out_shape += [jax.ShapeDtypeStruct((len(ahead) * width, columns), weight.dtype)]
    scratch = []
    if held is None:
        weight = in_hbm(weight)
        scratch = [
            pltpu.VMEM((blocks * width, columns), weight.dtype),
            pltpu.SemaphoreType.DMA((blocks + len(ahead),)),
        ]
    return pl.pallas_call(
        functools.partial(query_kernel, places, ahead, bool(carry), bool(extra)),
        out_shape=out_shape,
        in_specs=[smem()]
        + [vmem()] * (1 + len(arrays))
        + [hbm() if held is None else vmem()]
        + [vmem()] * (len(carry) + len(extra)),
        out_specs=[vmem()] * len(out_shape),
        scratch_shapes=scratch,
        compiler_params=pltpu.CompilerParams(vmem_limit_bytes=16 * MIB),
        cost_estimate=pl.CostEstimate(
            flops=2 * tokens * columns * width * blocks,
            bytes_accessed=2 * columns * width * (blocks + len(ahead)),
            transcendentals=0,
        ),
    )(where, gain, *arrays, weight, *carry, *extra)


def output_kernel(groups, width, where, attended, *refs):
    refs = list(refs)
    added = [refs.pop(0) if g[1] else None for g in groups]
    weight = refs.pop(0)
    left = attended[...]
    for (symbols, _), arrived, out in zip(groups, added, refs):
        for block, (const, pick) in enumerate(symbols):
            span = pl.ds(pl.multiple_of((where[pick] ^ const) * width, LANE), width)
            term = dot(left, weight[:, span])
            if arrived is not None:
                term = term + arrived[block].astype(jnp.float32)
            out[block] = term.astype(out.dtype)


def output_call(where, attended, weight, width, groups):
    tokens, depth = attended.shape
    blocks = sum(len(g[0]) for g in groups)
    added = [g[2] for g in groups if g[2] is not None]
    return pl.pallas_call(
        functools.partial(output_kernel, [(s, a is not None) for s, _, a in groups], width),
        out_shape=[jax.ShapeDtypeStruct((len(s), tokens, width), t) for s, t, _ in groups],
        in_specs=[smem()] + [vmem()] * (2 + len(added)),
        out_specs=[vmem()] * len(groups),
        compiler_params=pltpu.CompilerParams(vmem_limit_bytes=12 * MIB),
        cost_estimate=pl.CostEstimate(
            flops=2 * tokens * depth * width * blocks,
            bytes_accessed=2 * depth * width * blocks,
            transcendentals=0,
        ),
    )(where, attended, *added, weight)


def rotary_tables(tokens):
    half = HEAD // 2
    frequency = 500000.0 ** (-(jnp.arange(half, dtype=jnp.float32) * 2.0) / HEAD)
    angles = jnp.arange(tokens, dtype=jnp.float32)[:, None] * frequency[None, :]
    cosine, sine = jnp.cos(angles), jnp.sin(angles)
    return jnp.concatenate([cosine, cosine], axis=1), jnp.concatenate([-sine, sine], axis=1)


def per_device(n, act, norm_gain, wq, wk, wv, wo):
    tokens, width = act.shape
    me = lax.axis_index("wide")
    bits = [1 << i for i in range(n.bit_length() - 1)]
    side = (bits[1], bits[2])
    diagonal = bits[1] ^ bits[2]
    near, top = combos(bits[3:-1]), bits[-1]
    far = [o ^ top for o in near]
    f32, bf16 = jnp.float32, jnp.bfloat16

    def swap(x, offset):
        return lax.ppermute(x, "wide", [(i, i ^ offset) for i in range(n)])

    def turn(x, step):
        return lax.ppermute(x, "wide", [(i, i ^ side[(step + (i & CORE)) % 2]) for i in range(n)])

    bit = jnp.where((me & CORE) == 0, side[0], side[1])
    where = jnp.stack([me, me ^ bit, me ^ bit ^ diagonal]).astype(jnp.int32)
    gain = norm_gain.reshape(1, -1)

    def plain(offsets, pick=0):
        return [(o, pick) for o in offsets]

    def across(symbols):
        return [(const ^ CORE, (0, 2, 1)[pick]) for const, pick in symbols]

    shared = (n // KVH).bit_length() - 1
    kv_send, kv_keep = kv_terms(shared, where, act, gain, wk, wv)
    kv = kv_keep + swap(kv_send, CORE)
    for b in bits[shared:]:
        half = kv.shape[0] // 2
        kv = kv[half:] + swap(kv[:half].astype(bf16), b).astype(f32)
    total = kv[0]
    for b in bits[1:shared]:
        total = total + swap(total.astype(bf16), b).astype(f32)
    kv_sums = (total, swap(total, CORE))

    groups = []
    for offsets, first in ((near, act), (far, swap(act, top))):
        row = jnp.stack([first] + [swap(first, o) for o in near[1:]])
        side_1, side_2 = turn(row, 0), turn(row, 1)
        groups.append((offsets, row, side_1, side_2, turn(side_1, 1)))

    def pieces_of(group):
        offsets, row, side_1, side_2, corner = group
        return [
            (row, plain(offsets)),
            (side_1, plain(offsets, 1)),
            (side_2, plain(offsets, 2)),
            (corner, plain([o ^ diagonal for o in offsets])),
        ]

    def other(pieces):
        return [(swap(x, CORE), across(symbols)) for x, symbols in pieces]

    call = functools.partial(query_call, where, gain)
    early, last = pieces_of(groups[0]), pieces_of(groups[1])
    ahead = [s for _, symbols in last[1:3] for s in across(symbols)] + last[3][1]
    ahead += across(last[3][1])
    *carry, held = call(early + other(early), wq, ahead=ahead)
    carry = call(last[:3] + other(last[:1]), wq, carry=carry)
    corner, *carry = lax.optimization_barrier((last[3][0], *carry))
    corner = [(corner, last[3][1])]
    corner_other = other(corner)
    pieces = other(last[1:3]) + corner
    carry = call(pieces, held, carry=carry, held=0)
    (attended,) = call(
        corner_other,
        held,
        carry=carry,
        extra=(*kv_sums, *rotary_tables(tokens)),
        held=sum(len(symbols) for _, symbols in pieces),
    )

    def project(left, wanted, arrived=None):
        if arrived is None:
            wanted = [(across(s), bf16, None) for s, _ in wanted]
        else:
            wanted = [(*g, a) for g, a in zip(wanted, arrived)]
        return output_call(where, left, wo, width, wanted)

    def blocks_of(offsets):
        leave = [(plain([o ^ diagonal for o in offsets]), bf16)]
        stay = [(plain(offsets, 2), f32), (plain(offsets, 1), bf16), (plain(offsets), f32)]
        return leave, stay

    def round_square(offsets, left, sent):
        leave, stay = blocks_of(offsets)
        got = [swap(x, CORE) for x in sent]
        (leaving,) = project(left, leave, got[:1])
        from_corner = turn(leaving, 0)
        two, one, home = project(left, stay, got[1:])
        got_1 = turn(one, 0)
        got_2 = turn((two + from_corner.astype(f32)).astype(bf16), 1)
        return home + got_1.astype(f32) + got_2.astype(f32)

    def along_z(blocks):
        total = blocks[0]
        for i, o in enumerate(near):
            if o:
                total = total + swap(blocks[i].astype(bf16), o).astype(f32)
        return total

    left = attended
    sent = []
    for offsets in (far, near):
        leave, stay = blocks_of(offsets)
        sent.append(project(left, leave + stay))
        left, *sent[-1] = lax.optimization_barrier((left, *sent[-1]))
    total = along_z(round_square(far, attended, sent[0]))
    got = swap(total.astype(bf16), top)
    out = along_z(round_square(near, attended, sent[1])) + got.astype(f32)
    return out.astype(bf16)


def solution(mesh):
    return jax.shard_map(
        functools.partial(per_device, mesh.shape["wide"]),
        mesh=mesh,
        in_specs=(
            P("groups", "wide"),
            P(),
            P(None, "wide"),
            P("wide", None),
            P("wide", None),
            P("wide", None),
        ),
        out_specs=P("groups", "wide"),
        check_vma=False,
    )
```

```python
import functools

import jax
import jax.numpy as jnp
from jax import lax
from jax.experimental import pallas as pl
from jax.experimental.pallas import tpu as pltpu
from jax.sharding import PartitionSpec as P

HEADS = 128
KVH = 8
HEAD = 128
LANE = 128
EPS = 1e-05
MIB = 1 << 20
CORE = 1


def combos(bits):
    out = [0]
    for b in bits:
        out = out + [o ^ b for o in out]
    return out


def vmem():
    return pl.BlockSpec(memory_space=pltpu.VMEM)


def smem():
    return pl.BlockSpec(memory_space=pltpu.SMEM)


def hbm():
    return pl.BlockSpec(memory_space=pltpu.HBM)


def in_hbm(x):
    return pltpu.with_memory_space_constraint(x, pltpu.HBM)


def dot(a, b):
    return jnp.dot(a, b, preferred_element_type=jnp.float32)


def fetch_kernel(symbols, width, where, source, target, sems):
    copies = []
    for i, (const, pick) in enumerate(symbols):
        start = pl.multiple_of((where[pick] ^ const) * width, LANE)
        copy = pltpu.make_async_copy(
            source.at[pl.ds(start, width), :], target.at[pl.ds(i * width, width), :], sems.at[i]
        )
        copy.start()
        copies.append(copy)
    for copy in copies:
        copy.wait()


def fetched(where, weight, width, symbols):
    shape = (len(symbols) * width, weight.shape[1])
    return pl.pallas_call(
        functools.partial(fetch_kernel, symbols, width),
        out_shape=jax.ShapeDtypeStruct(shape, weight.dtype),
        in_specs=[smem(), hbm()],
        out_specs=vmem(),
        scratch_shapes=[pltpu.SemaphoreType.DMA((len(symbols),))],
        compiler_params=pltpu.CompilerParams(vmem_limit_bytes=MIB),
        cost_estimate=pl.CostEstimate(
            flops=0, bytes_accessed=4 * shape[0] * shape[1], transcendentals=0
        ),
    )(where, in_hbm(weight))


def kv_kernel(shared, where, act, gain, wk, wv, send, keep, abuf, gbuf, kbuf, vbuf, sems):
    me = where[0]
    width = act.shape[1]
    own = pl.ds(pl.multiple_of(me * width, LANE), width)
    pairs = [(act, abuf), (gain, gbuf), (wk, kbuf), (wv, vbuf)]
    copies = [pltpu.make_async_copy(x, y, sems.at[i]) for i, (x, y) in enumerate(pairs)]
    for c in copies:
        c.start()
    for c in copies:
        c.wait()
    scaled = (abuf[...].astype(jnp.float32) * gbuf[:, own]).astype(jnp.bfloat16)
    k, v = dot(scaled, kbuf[...]), dot(scaled, vbuf[...])
    core0 = (me & CORE) == 0
    for h in range(KVH):
        off = h ^ (me >> shared)
        spot = 0
        for b in range(KVH.bit_length() - 1):
            spot = spot * 2 + (1 - ((off >> b) & 1))
        kh, vh = k[:, h * HEAD : (h + 1) * HEAD], v[:, h * HEAD : (h + 1) * HEAD]
        keep[spot] = jnp.where(core0, kh, vh)
        send[spot] = jnp.where(core0, vh, kh)


def kv_terms(shared, where, act, gain, wk, wv):
    tokens = act.shape[0]
    return pl.pallas_call(
        functools.partial(kv_kernel, shared),
        out_shape=[jax.ShapeDtypeStruct((KVH, tokens, HEAD), jnp.float32)] * 2
        + [jax.ShapeDtypeStruct(x.shape, x.dtype) for x in (act, gain)],
        in_specs=[smem()] + [hbm()] * 4,
        out_specs=[vmem()] * 4,
        scratch_shapes=[
            pltpu.VMEM(wk.shape, wk.dtype),
            pltpu.VMEM(wv.shape, wv.dtype),
            pltpu.SemaphoreType.DMA((4,)),
        ],
        compiler_params=pltpu.CompilerParams(vmem_limit_bytes=12 * MIB),
        cost_estimate=pl.CostEstimate(
            flops=4 * tokens * wk.size, bytes_accessed=4 * wk.size, transcendentals=0
        ),
    )(where, in_hbm(act), in_hbm(gain), in_hbm(wk), in_hbm(wv))


def attend(queries, k_sum, v_sum, cosine, sine, scale):
    k_rows = (k_sum * scale).astype(jnp.bfloat16).astype(jnp.float32)
    value = (v_sum * scale).astype(jnp.bfloat16)
    tokens, heads = queries.shape[0], queries.shape[1] // HEAD

    def rotate(x, cosine, sine):
        half = HEAD // 2
        turned = jnp.concatenate([x[:, half:], x[:, :half]], axis=1)
        return (x * cosine + turned * sine).astype(jnp.bfloat16)

    def stacked(parts):
        return jnp.concatenate(parts, axis=0)

    key = rotate(k_rows, cosine, sine)
    queries = queries * scale
    rows = stacked([queries[:, h * HEAD : (h + 1) * HEAD] for h in range(heads)])
    query = rotate(rows, stacked([cosine] * heads), stacked([sine] * heads))
    scores = lax.dot_general(
        query, key, (((1,), (1,)), ((), ())), preferred_element_type=jnp.float32
    ) * HEAD ** (-0.5)
    at = lax.broadcasted_iota(jnp.int32, (tokens, tokens), 0)
    seen = at >= lax.broadcasted_iota(jnp.int32, (tokens, tokens), 1)
    bias = jnp.where(seen, 0.0, -jnp.inf)
    scores = scores + stacked([bias] * heads)
    weights = jnp.exp(scores - jnp.max(scores, axis=1, keepdims=True))
    probs = (weights / jnp.sum(weights, axis=1, keepdims=True)).astype(jnp.bfloat16)
    out = dot(probs, value).astype(jnp.bfloat16)
    return jnp.concatenate([out[h * tokens : (h + 1) * tokens] for h in range(heads)], axis=1)


def query_kernel(places, carried, last, *refs):
    refs = list(refs)
    where, gain = refs.pop(0), refs.pop(0)
    pieces = [refs.pop(0) for _ in places]
    weight = refs.pop(0)
    queries = refs.pop(0)[...] if carried else None
    squares = refs.pop(0)[...] if carried else None
    width = pieces[0].shape[2]
    for piece, blocks in zip(pieces, places):
        for block, ((const, pick), row) in enumerate(blocks):
            start = pl.multiple_of((where[pick] ^ const) * width, LANE)
            x = piece[block].astype(jnp.float32)
            for c in range(0, width, LANE):
                square = x[:, c : c + LANE] * x[:, c : c + LANE]
                squares = square if squares is None else squares + square
            scaled = (x * gain[:, pl.ds(start, width)]).astype(jnp.bfloat16)
            term = dot(scaled, weight[row * width : (row + 1) * width, :])
            queries = term if queries is None else queries + term
    if last:
        mean = jnp.sum(squares, axis=1, keepdims=True) * (1.0 / gain.shape[1])
        mine, other, cosine, sine, out = refs
        core0 = (where[0] & CORE) == 0
        k_sum = jnp.where(core0, mine[...], other[...])
        v_sum = jnp.where(core0, other[...], mine[...])
        out[...] = attend(
            queries, k_sum, v_sum, cosine[...], sine[...], lax.rsqrt(mean + EPS)
        )
    else:
        refs[0][...] = queries
        refs[1][...] = squares


def query_call(where, gain, pieces, held, carry=(), extra=()):
    weight, order = held
    arrays = [array for array, _ in pieces]
    places = [[(s, order.index(s)) for s in symbols] for _, symbols in pieces]
    tokens, width, columns = *arrays[0].shape[1:], weight.shape[1]
    rows = width * sum(len(p) for p in places)
    if extra:
        out_shape = [jax.ShapeDtypeStruct((tokens, columns), jnp.bfloat16)]
    else:
        out_shape = [
            jax.ShapeDtypeStruct((tokens, columns), jnp.float32),
            jax.ShapeDtypeStruct((tokens, LANE), jnp.float32),
        ]
    count = 2 + len(arrays) + len(carry) + len(extra)
    return pl.pallas_call(
        functools.partial(query_kernel, places, bool(carry), bool(extra)),
        out_shape=out_shape,
        in_specs=[smem()] + [vmem()] * count,
        out_specs=[vmem()] * len(out_shape),
        compiler_params=pltpu.CompilerParams(vmem_limit_bytes=12 * MIB),
        cost_estimate=pl.CostEstimate(
            flops=2 * tokens * columns * rows,
            bytes_accessed=2 * columns * rows,
            transcendentals=0,
        ),
    )(where, gain, *arrays, weight, *carry, *extra)


def output_kernel(groups, width, where, attended, *refs):
    refs = list(refs)
    added = [refs.pop(0) if g[1] else None for g in groups]
    weight = refs.pop(0)
    left = attended[...]
    for (symbols, _), arrived, out in zip(groups, added, refs):
        for block, (const, pick) in enumerate(symbols):
            span = pl.ds(pl.multiple_of((where[pick] ^ const) * width, LANE), width)
            term = dot(left, weight[:, span])
            if arrived is not None:
                term = term + arrived[block].astype(jnp.float32)
            out[block] = term.astype(out.dtype)


def output_call(where, attended, weight, width, groups):
    tokens, depth = attended.shape
    blocks = sum(len(g[0]) for g in groups)
    added = [g[2] for g in groups if g[2] is not None]
    return pl.pallas_call(
        functools.partial(output_kernel, [(s, a is not None) for s, _, a in groups], width),
        out_shape=[jax.ShapeDtypeStruct((len(s), tokens, width), t) for s, t, _ in groups],
        in_specs=[smem()] + [vmem()] * (2 + len(added)),
        out_specs=[vmem()] * len(groups),
        compiler_params=pltpu.CompilerParams(vmem_limit_bytes=12 * MIB),
        cost_estimate=pl.CostEstimate(
            flops=2 * tokens * depth * width * blocks,
            bytes_accessed=2 * depth * width * blocks,
            transcendentals=0,
        ),
    )(where, attended, *added, weight)


def rotary_tables(tokens):
    half = HEAD // 2
    frequency = 500000.0 ** (-(jnp.arange(half, dtype=jnp.float32) * 2.0) / HEAD)
    angles = jnp.arange(tokens, dtype=jnp.float32)[:, None] * frequency[None, :]
    cosine, sine = jnp.cos(angles), jnp.sin(angles)
    return jnp.concatenate([cosine, cosine], axis=1), jnp.concatenate([-sine, sine], axis=1)


def per_device(n, act, norm_gain, wq, wk, wv, wo):
    tokens, width = act.shape
    me = lax.axis_index("wide")
    bits = [1 << i for i in range(n.bit_length() - 1)]
    ways = (bits[1], bits[2])
    diagonal = bits[1] ^ bits[2]
    near, top = combos(bits[3:-1]), bits[-1]
    far = [o ^ top for o in near]
    f32, bf16 = jnp.float32, jnp.bfloat16

    def swap(x, offset):
        return lax.ppermute(x, "wide", [(i, i ^ offset) for i in range(n)])

    def turn(x, step):
        return lax.ppermute(x, "wide", [(i, i ^ ways[(step + (i & CORE)) % 2]) for i in range(n)])

    bit = jnp.where((me & CORE) == 0, ways[0], ways[1])
    where = jnp.stack([me, me ^ bit, me ^ bit ^ diagonal]).astype(jnp.int32)
    gain = norm_gain.reshape(1, -1)

    def plain(offsets, pick=0):
        return [(o, pick) for o in offsets]

    def across(symbols):
        return [(const ^ CORE, (0, 2, 1)[pick]) for const, pick in symbols]

    def after(x, *others):
        return lax.optimization_barrier((x, *others))[0]

    shared = (n // KVH).bit_length() - 1
    kv_send, kv_keep, act, gain = kv_terms(shared, where, act, gain, wk, wv)

    def symbols_of(offsets):
        square = [(0, 0), (0, 1), (0, 2), (diagonal, 0)]
        return [[(const ^ o, pick) for o in offsets] for const, pick in square]

    def listed(groups):
        return [s for symbols in groups for s in symbols]

    def other(pieces):
        return [(swap(x, CORE), across(symbols)) for x, symbols in pieces]

    def order_of(offsets):
        own = listed(symbols_of(offsets))
        return own + across(own)

    early_order, last_order = order_of(near), order_of(far)

    pieces, joined, rows, early_weight, first = [], [], [], None, act
    for offsets in (near[:1], near[1:], far):
        at = symbols_of(offsets)
        if offsets is far:
            first = after(swap(act, top), pieces[0][2][0], *rows)
        row = jnp.stack([swap(first, o & ~top) if o & ~top else first for o in offsets])
        if offsets is far:
            row = after(row, joined[1])
        rows.append(row)
        side = turn(row, 0)
        if offsets is far:
            early_weight = fetched(after(where, row), wq, width, early_order)
            side = after(side, early_weight, pieces[1][2][0])
        joined.append(jnp.concatenate([row, side]))
        pieces.append([(row, at[0]), (side, at[1]), (turn(joined[-1], 1), at[2] + at[3])])
    last_weight = fetched(where, wq, width, last_order)

    kv = kv_keep + swap(kv_send, CORE)
    for b, step in zip(bits[shared:], joined):
        half = kv.shape[0] // 2
        got = after(swap(kv[:half].astype(bf16), b), step)
        kv = kv[half:] + got.astype(f32)
    total = kv[0]
    for b in bits[1:shared]:
        total = total + swap(total.astype(bf16), b).astype(f32)
    kv_sums = (total, swap(total, CORE))

    call = functools.partial(query_call, where, gain)
    early = pieces[0] + pieces[1]
    early_held, last_held = (early_weight, early_order), (last_weight, last_order)
    carry = call(early + other(early), early_held)
    row, side, both = pieces[2]
    carry = call([row, side] + other([row]), last_held, carry=carry)
    arrived, *carry = lax.optimization_barrier((both[0], *carry))
    both = [(arrived, both[1])]
    final = other(both)
    carry = call(other([side]) + both, last_held, carry=carry)
    (attended,) = call(final, last_held, carry=carry, extra=(*kv_sums, *rotary_tables(tokens)))

    def project(left, wanted, arrived=None):
        if arrived is None:
            wanted = [(across(s), bf16, None) for s, _ in wanted]
        else:
            wanted = [(*g, a) for g, a in zip(wanted, arrived)]
        return output_call(where, left, wo, width, wanted)

    def round_square(offsets, left):
        home, one, two, corner = symbols_of(offsets)
        k = len(offsets)
        leave, stay = [(corner + one, bf16)], [(two, f32), (home, f32)]
        sent = project(left, leave)
        got = [swap(x, CORE) for x in sent]
        left, *_ = lax.optimization_barrier((left, *sent))
        got_stay = [swap(x, CORE) for x in project(left, stay)]
        (leaving,) = project(left, leave, got)
        arrived = turn(leaving, 0)
        left = after(left, leaving)
        two, home = project(left, stay, got_stay)
        two = two + arrived[:k].astype(f32)
        got = turn(two.astype(bf16), 1)
        return [home, arrived[k:], got], after(left, two)

    def added_up(home, *arrived):
        for x in arrived:
            home = home + x.astype(f32)
        return home

    def along_z(blocks, offsets):
        return [swap(blocks[i].astype(bf16), o).astype(f32) for i, o in enumerate(offsets)]

    far_sums, left = round_square(far, attended)
    near_sums, left = round_square(near[1:], left)
    home_sums, left = round_square(near[:1], left)
    total = added_up(*far_sums)
    total = added_up(total[0], *along_z(total[1:], near[1:]))
    out = swap(total.astype(bf16), top).astype(f32)
    out = added_up(out, *along_z(added_up(*near_sums), near[1:]))
    out = out + added_up(*home_sums)[0]
    return out.astype(bf16)


def solution(mesh):
    return jax.shard_map(
        functools.partial(per_device, mesh.shape["wide"]),
        mesh=mesh,
        in_specs=(
            P("groups", "wide"),
            P(),
            P(None, "wide"),
            P("wide", None),
            P("wide", None),
            P("wide", None),
        ),
        out_specs=P("groups", "wide"),
        check_vma=False,
    )
```

```python
import functools

import jax
import jax.numpy as jnp
from jax import lax
from jax.experimental import pallas as pl
from jax.experimental.pallas import tpu as pltpu
from jax.sharding import PartitionSpec as P

HEADS = 128
KVH = 8
HEAD = 128
LANE = 128
EPS = 1e-05
MIB = 1 << 20
CORE = 1
KV_WEIGHT = 16


def combos(bits):
    out = [0]
    for b in bits:
        out = out + [o ^ b for o in out]
    return out


def vmem():
    return pl.BlockSpec(memory_space=pltpu.VMEM)


def smem():
    return pl.BlockSpec(memory_space=pltpu.SMEM)


def hbm():
    return pl.BlockSpec(memory_space=pltpu.HBM)


def in_hbm(x):
    return pltpu.with_memory_space_constraint(x, pltpu.HBM)


def dot(a, b):
    return jnp.dot(a, b, preferred_element_type=jnp.float32)


def kv_kernel(shared, where, act, gain, wk, wv, send, keep, abuf, gbuf, kbuf, vbuf, sems):
    me = where[0]
    width = act.shape[1]
    own = pl.ds(pl.multiple_of(me * width, LANE), width)
    pairs = [(act, abuf), (gain, gbuf), (wk, kbuf), (wv, vbuf)]
    copies = [pltpu.make_async_copy(x, y, sems.at[i]) for i, (x, y) in enumerate(pairs)]
    for c in copies:
        c.start()
    for c in copies:
        c.wait()
    scaled = (abuf[...].astype(jnp.float32) * gbuf[:, own]).astype(jnp.bfloat16)
    k, v = dot(scaled, kbuf[...]), dot(scaled, vbuf[...])
    core0 = (me & CORE) == 0
    for h in range(KVH):
        off = h ^ (me >> shared)
        spot = 0
        for b in range(KVH.bit_length() - 1):
            spot = spot * 2 + (1 - ((off >> b) & 1))
        kh, vh = k[:, h * HEAD : (h + 1) * HEAD], v[:, h * HEAD : (h + 1) * HEAD]
        keep[spot] = jnp.where(core0, kh, vh)
        send[spot] = jnp.where(core0, vh, kh)


def kv_terms(shared, where, act, gain, wk, wv):
    tokens = act.shape[0]
    return pl.pallas_call(
        functools.partial(kv_kernel, shared),
        out_shape=[jax.ShapeDtypeStruct((KVH, tokens, HEAD), jnp.float32)] * 2
        + [jax.ShapeDtypeStruct(x.shape, x.dtype) for x in (act, gain)],
        in_specs=[smem()] + [hbm()] * 4,
        out_specs=[vmem()] * 4,
        scratch_shapes=[
            pltpu.VMEM(wk.shape, wk.dtype),
            pltpu.VMEM(wv.shape, wv.dtype),
            pltpu.SemaphoreType.DMA((4,)),
        ],
        compiler_params=pltpu.CompilerParams(vmem_limit_bytes=12 * MIB),
        cost_estimate=pl.CostEstimate(
            flops=KV_WEIGHT * 4 * tokens * wk.size,
            bytes_accessed=KV_WEIGHT * 4 * wk.size,
            transcendentals=0,
        ),
    )(where, in_hbm(act), in_hbm(gain), in_hbm(wk), in_hbm(wv))


def attend(queries, k_sum, v_sum, cosine, sine, scale):
    k_rows = (k_sum * scale).astype(jnp.bfloat16).astype(jnp.float32)
    value = (v_sum * scale).astype(jnp.bfloat16)
    tokens, heads = queries.shape[0], queries.shape[1] // HEAD

    def rotate(x, cosine, sine):
        half = HEAD // 2
        turned = jnp.concatenate([x[:, half:], x[:, :half]], axis=1)
        return (x * cosine + turned * sine).astype(jnp.bfloat16)

    def stacked(parts):
        return jnp.concatenate(parts, axis=0)

    key = rotate(k_rows, cosine, sine)
    queries = queries * scale
    rows = stacked([queries[:, h * HEAD : (h + 1) * HEAD] for h in range(heads)])
    query = rotate(rows, stacked([cosine] * heads), stacked([sine] * heads))
    scores = lax.dot_general(
        query, key, (((1,), (1,)), ((), ())), preferred_element_type=jnp.float32
    ) * HEAD ** (-0.5)
    at = lax.broadcasted_iota(jnp.int32, (tokens, tokens), 0)
    seen = at >= lax.broadcasted_iota(jnp.int32, (tokens, tokens), 1)
    bias = jnp.where(seen, 0.0, -jnp.inf)
    scores = scores + stacked([bias] * heads)
    weights = jnp.exp(scores - jnp.max(scores, axis=1, keepdims=True))
    probs = (weights / jnp.sum(weights, axis=1, keepdims=True)).astype(jnp.bfloat16)
    out = dot(probs, value).astype(jnp.bfloat16)
    return jnp.concatenate([out[h * tokens : (h + 1) * tokens] for h in range(heads)], axis=1)


def query_kernel(places, carried, last, *refs):
    refs = list(refs)
    where, gain = refs.pop(0), refs.pop(0)
    pieces = [refs.pop(0) for _ in places]
    weight = refs.pop(0)
    queries = refs.pop(0)[...] if carried else None
    squares = refs.pop(0)[...] if carried else None
    width = pieces[0].shape[2]
    for piece, blocks in zip(pieces, places):
        for block, (const, pick) in enumerate(blocks):
            span = pl.ds(pl.multiple_of((where[pick] ^ const) * width, LANE), width)
            x = piece[block].astype(jnp.float32)
            for c in range(0, width, LANE):
                square = x[:, c : c + LANE] * x[:, c : c + LANE]
                squares = square if squares is None else squares + square
            term = dot((x * gain[:, span]).astype(jnp.bfloat16), weight[span, :])
            queries = term if queries is None else queries + term
    if last:
        mean = jnp.sum(squares, axis=1, keepdims=True) * (1.0 / gain.shape[1])
        mine, other, cosine, sine, out = refs
        core0 = (where[0] & CORE) == 0
        k_sum = jnp.where(core0, mine[...], other[...])
        v_sum = jnp.where(core0, other[...], mine[...])
        out[...] = attend(
            queries, k_sum, v_sum, cosine[...], sine[...], lax.rsqrt(mean + EPS)
        )
    else:
        refs[0][...] = queries
        refs[1][...] = squares


def query_call(where, gain, pieces, weight, carry=(), extra=()):
    arrays, places = [array for array, _ in pieces], [symbols for _, symbols in pieces]
    tokens, width, columns = *arrays[0].shape[1:], weight.shape[1]
    rows = width * sum(len(p) for p in places)
    if extra:
        out_shape = [jax.ShapeDtypeStruct((tokens, columns), jnp.bfloat16)]
    else:
        out_shape = [
            jax.ShapeDtypeStruct((tokens, columns), jnp.float32),
            jax.ShapeDtypeStruct((tokens, LANE), jnp.float32),
        ]
    count = 2 + len(arrays) + len(carry) + len(extra)
    return pl.pallas_call(
        functools.partial(query_kernel, places, bool(carry), bool(extra)),
        out_shape=out_shape,
        in_specs=[smem()] + [vmem()] * count,
        out_specs=[vmem()] * len(out_shape),
        compiler_params=pltpu.CompilerParams(vmem_limit_bytes=12 * MIB),
        cost_estimate=pl.CostEstimate(
            flops=2 * tokens * columns * rows,
            bytes_accessed=2 * columns * rows,
            transcendentals=0,
        ),
    )(where, gain, *arrays, weight, *carry, *extra)


def output_kernel(groups, width, where, attended, *refs):
    refs = list(refs)
    added = [refs.pop(0) if g[1] else None for g in groups]
    weight = refs.pop(0)
    left = attended[...]
    for (symbols, _), arrived, out in zip(groups, added, refs):
        for block, (const, pick) in enumerate(symbols):
            span = pl.ds(pl.multiple_of((where[pick] ^ const) * width, LANE), width)
            term = dot(left, weight[:, span])
            if arrived is not None:
                term = term + arrived[block].astype(jnp.float32)
            out[block] = term.astype(out.dtype)


def output_call(where, attended, weight, width, groups):
    tokens, depth = attended.shape
    blocks = sum(len(g[0]) for g in groups)
    added = [g[2] for g in groups if g[2] is not None]
    return pl.pallas_call(
        functools.partial(output_kernel, [(s, a is not None) for s, _, a in groups], width),
        out_shape=[jax.ShapeDtypeStruct((len(s), tokens, width), t) for s, t, _ in groups],
        in_specs=[smem()] + [vmem()] * (2 + len(added)),
        out_specs=[vmem()] * len(groups),
        compiler_params=pltpu.CompilerParams(vmem_limit_bytes=12 * MIB),
        cost_estimate=pl.CostEstimate(
            flops=2 * tokens * depth * width * blocks,
            bytes_accessed=2 * depth * width * blocks,
            transcendentals=0,
        ),
    )(where, attended, *added, weight)


def rotary_tables(tokens):
    half = HEAD // 2
    frequency = 500000.0 ** (-(jnp.arange(half, dtype=jnp.float32) * 2.0) / HEAD)
    angles = jnp.arange(tokens, dtype=jnp.float32)[:, None] * frequency[None, :]
    cosine, sine = jnp.cos(angles), jnp.sin(angles)
    return jnp.concatenate([cosine, cosine], axis=1), jnp.concatenate([-sine, sine], axis=1)


def per_device(n, act, norm_gain, wq, wk, wv, wo):
    tokens, width = act.shape
    me = lax.axis_index("wide")
    bits = [1 << i for i in range(n.bit_length() - 1)]
    ways = (bits[1], bits[2])
    diagonal = bits[1] ^ bits[2]
    near, top = combos(bits[3:-1]), bits[-1]
    far = [o ^ top for o in near]
    f32, bf16 = jnp.float32, jnp.bfloat16

    def swap(x, offset):
        return lax.ppermute(x, "wide", [(i, i ^ offset) for i in range(n)])

    def turn(x, step):
        return lax.ppermute(x, "wide", [(i, i ^ ways[(step + (i & CORE)) % 2]) for i in range(n)])

    bit = jnp.where((me & CORE) == 0, ways[0], ways[1])
    where = jnp.stack([me, me ^ bit, me ^ bit ^ diagonal]).astype(jnp.int32)
    gain = norm_gain.reshape(1, -1)

    def plain(offsets, pick=0):
        return [(o, pick) for o in offsets]

    def across(symbols):
        return [(const ^ CORE, (0, 2, 1)[pick]) for const, pick in symbols]

    def after(x, *others):
        return lax.optimization_barrier((x, *others))[0]

    shared = (n // KVH).bit_length() - 1
    raw = act
    kv_send, kv_keep, act, gain = kv_terms(shared, where, act, gain, wk, wv)

    def symbols_of(offsets):
        square = [(0, 0), (0, 1), (0, 2), (diagonal, 0)]
        return [[(const ^ o, pick) for o in offsets] for const, pick in square]

    def other(pieces):
        return [(swap(x, CORE), across(symbols)) for x, symbols in pieces]

    groups, z_first = [], [raw] + [swap(raw, o) for o in near[1:]]
    for offsets in (near, far):
        if offsets is far:
            first = swap(raw, top)
            row = jnp.stack([first] + [swap(first, o) for o in near[1:]])
        else:
            row = jnp.stack([act] + z_first[1:])
        one, two = turn(row, 0), turn(row, 1)
        corner = turn(one, 1)
        groups.append(list(zip((row, one, two, corner), symbols_of(offsets))))
    early, last = groups

    kv = kv_keep + swap(kv_send, CORE)
    steps = [early[1][0], early[3][0], last[1][0]]
    for b, step in zip(bits[shared:], steps):
        half = kv.shape[0] // 2
        got = after(swap(kv[:half].astype(bf16), b), step)
        kv = kv[half:] + got.astype(f32)
    total = after(kv[0], last[2][0])
    for b in bits[1:shared]:
        total = total + swap(total.astype(bf16), b).astype(f32)
    kv_sums = (total, swap(total, CORE))

    call = functools.partial(query_call, where, gain, weight=wq)
    carry = call(early + other(early))
    carry = call(last[:3] + other(last[:1]), carry=carry)
    corner, *carry = lax.optimization_barrier((last[3][0], *carry))
    corner = [(corner, last[3][1])]
    final = other(corner)
    carry = call(other(last[1:3]) + corner, carry=carry)
    (attended,) = call(final, carry=carry, extra=(*kv_sums, *rotary_tables(tokens)))

    def project(left, wanted, arrived=None):
        if arrived is None:
            wanted = [(across(s), bf16, None) for s, _ in wanted]
        else:
            wanted = [(*g, a) for g, a in zip(wanted, arrived)]
        return output_call(where, left, wo, width, wanted)

    def wanted(offsets):
        home, one, two, corner = symbols_of(offsets)
        return [(corner, bf16)], [(two, f32), (one, bf16), (home, f32)]

    def round_square(offsets, left, got):
        leave, stay = wanted(offsets)
        (leaving,) = project(left, leave, got[:1])
        from_corner = turn(leaving, 0)
        two, one, home = project(after(left, leaving), stay, got[1:])
        got_1 = turn(one, 0)
        two = (two + from_corner.astype(f32)).astype(bf16)
        return [home, got_1, turn(two, 1)], after(left, two)

    def added_up(home, *arrived):
        for x in arrived:
            home = home + x.astype(f32)
        return home

    def along_z(blocks):
        return added_up(
            blocks[0], *[swap(blocks[i].astype(bf16), o) for i, o in enumerate(near) if o]
        )

    left, sent = attended, []
    leave, stay = wanted(far)
    for groups in (leave, stay, sum(wanted(near), [])):
        sent += project(left, groups)
        left = after(left, sent[-1])
    got = [swap(x, CORE) for x in sent]
    far_sums, left = round_square(far, attended, got[:4])
    near_sums, _ = round_square(near, left, got[4:])
    got = swap(along_z(added_up(*far_sums)).astype(bf16), top)
    out = added_up(along_z(added_up(*near_sums)), got)
    return out.astype(bf16)


def solution(mesh):
    return jax.shard_map(
        functools.partial(per_device, mesh.shape["wide"]),
        mesh=mesh,
        in_specs=(
            P("groups", "wide"),
            P(),
            P(None, "wide"),
            P("wide", None),
            P("wide", None),
            P("wide", None),
        ),
        out_specs=P("groups", "wide"),
        check_vma=False,
    )
```

```python
import functools

import jax
import jax.numpy as jnp
from jax import lax
from jax.experimental import pallas as pl
from jax.experimental.pallas import tpu as pltpu
from jax.sharding import PartitionSpec as P

HEADS = 128
KVH = 8
HEAD = 128
LANE = 128
EPS = 1e-05
MIB = 1 << 20
CORE = 1
KV_WEIGHT = 16


def combos(bits):
    out = [0]
    for b in bits:
        out = out + [o ^ b for o in out]
    return out


def vmem():
    return pl.BlockSpec(memory_space=pltpu.VMEM)


def smem():
    return pl.BlockSpec(memory_space=pltpu.SMEM)


def hbm():
    return pl.BlockSpec(memory_space=pltpu.HBM)


def in_hbm(x):
    return pltpu.with_memory_space_constraint(x, pltpu.HBM)


def dot(a, b):
    return jnp.dot(a, b, preferred_element_type=jnp.float32)


def fetch_kernel(symbols, width, where, source, target, sems):
    copies = []
    for i, (const, pick) in enumerate(symbols):
        start = pl.multiple_of((where[pick] ^ const) * width, LANE)
        copy = pltpu.make_async_copy(
            source.at[:, pl.ds(start, width)], target.at[:, pl.ds(i * width, width)], sems.at[i]
        )
        copy.start()
        copies.append(copy)
    for copy in copies:
        copy.wait()


def fetched(where, weight, width, symbols):
    shape = (weight.shape[0], len(symbols) * width)
    columns = pl.pallas_call(
        functools.partial(fetch_kernel, symbols, width),
        out_shape=jax.ShapeDtypeStruct(shape, weight.dtype),
        in_specs=[smem(), hbm()],
        out_specs=vmem(),
        scratch_shapes=[pltpu.SemaphoreType.DMA((len(symbols),))],
        compiler_params=pltpu.CompilerParams(vmem_limit_bytes=MIB),
        cost_estimate=pl.CostEstimate(
            flops=0, bytes_accessed=4 * shape[0] * shape[1], transcendentals=0
        ),
    )(where, in_hbm(weight))
    return columns, symbols


def kv_kernel(shared, where, act, gain, wk, wv, send, keep, abuf, gbuf, kbuf, vbuf, sems):
    me = where[0]
    width = act.shape[1]
    own = pl.ds(pl.multiple_of(me * width, LANE), width)
    pairs = [(act, abuf), (gain, gbuf), (wk, kbuf), (wv, vbuf)]
    copies = [pltpu.make_async_copy(x, y, sems.at[i]) for i, (x, y) in enumerate(pairs)]
    for c in copies:
        c.start()
    for c in copies:
        c.wait()
    scaled = (abuf[...].astype(jnp.float32) * gbuf[:, own]).astype(jnp.bfloat16)
    k, v = dot(scaled, kbuf[...]), dot(scaled, vbuf[...])
    core0 = (me & CORE) == 0
    for h in range(KVH):
        off = h ^ (me >> shared)
        spot = 0
        for b in range(KVH.bit_length() - 1):
            spot = spot * 2 + (1 - ((off >> b) & 1))
        kh, vh = k[:, h * HEAD : (h + 1) * HEAD], v[:, h * HEAD : (h + 1) * HEAD]
        keep[spot] = jnp.where(core0, kh, vh)
        send[spot] = jnp.where(core0, vh, kh)


def kv_terms(shared, where, act, gain, wk, wv):
    tokens = act.shape[0]
    return pl.pallas_call(
        functools.partial(kv_kernel, shared),
        out_shape=[jax.ShapeDtypeStruct((KVH, tokens, HEAD), jnp.float32)] * 2
        + [jax.ShapeDtypeStruct(x.shape, x.dtype) for x in (act, gain)],
        in_specs=[smem()] + [hbm()] * 4,
        out_specs=[vmem()] * 4,
        scratch_shapes=[
            pltpu.VMEM(wk.shape, wk.dtype),
            pltpu.VMEM(wv.shape, wv.dtype),
            pltpu.SemaphoreType.DMA((4,)),
        ],
        compiler_params=pltpu.CompilerParams(vmem_limit_bytes=12 * MIB),
        cost_estimate=pl.CostEstimate(
            flops=KV_WEIGHT * 4 * tokens * wk.size,
            bytes_accessed=KV_WEIGHT * 4 * wk.size,
            transcendentals=0,
        ),
    )(where, in_hbm(act), in_hbm(gain), in_hbm(wk), in_hbm(wv))


def attend(queries, k_sum, v_sum, cosine, sine, scale):
    k_rows = (k_sum * scale).astype(jnp.bfloat16).astype(jnp.float32)
    value = (v_sum * scale).astype(jnp.bfloat16)
    tokens, heads = queries.shape[0], queries.shape[1] // HEAD

    def rotate(x, cosine, sine):
        half = HEAD // 2
        turned = jnp.concatenate([x[:, half:], x[:, :half]], axis=1)
        return (x * cosine + turned * sine).astype(jnp.bfloat16)

    def stacked(parts):
        return jnp.concatenate(parts, axis=0)

    key = rotate(k_rows, cosine, sine)
    queries = queries * scale
    rows = stacked([queries[:, h * HEAD : (h + 1) * HEAD] for h in range(heads)])
    query = rotate(rows, stacked([cosine] * heads), stacked([sine] * heads))
    scores = lax.dot_general(
        query, key, (((1,), (1,)), ((), ())), preferred_element_type=jnp.float32
    ) * HEAD ** (-0.5)
    at = lax.broadcasted_iota(jnp.int32, (tokens, tokens), 0)
    seen = at >= lax.broadcasted_iota(jnp.int32, (tokens, tokens), 1)
    bias = jnp.where(seen, 0.0, -jnp.inf)
    scores = scores + stacked([bias] * heads)
    weights = jnp.exp(scores - jnp.max(scores, axis=1, keepdims=True))
    probs = (weights / jnp.sum(weights, axis=1, keepdims=True)).astype(jnp.bfloat16)
    out = dot(probs, value).astype(jnp.bfloat16)
    return jnp.concatenate([out[h * tokens : (h + 1) * tokens] for h in range(heads)], axis=1)


def query_kernel(places, carried, last, *refs):
    refs = list(refs)
    where, gain = refs.pop(0), refs.pop(0)
    pieces = [refs.pop(0) for _ in places]
    weight = refs.pop(0)
    queries = refs.pop(0)[...] if carried else None
    squares = refs.pop(0)[...] if carried else None
    width = pieces[0].shape[2]
    for piece, blocks in zip(pieces, places):
        for block, (const, pick) in enumerate(blocks):
            span = pl.ds(pl.multiple_of((where[pick] ^ const) * width, LANE), width)
            x = piece[block].astype(jnp.float32)
            for c in range(0, width, LANE):
                square = x[:, c : c + LANE] * x[:, c : c + LANE]
                squares = square if squares is None else squares + square
            term = dot((x * gain[:, span]).astype(jnp.bfloat16), weight[span, :])
            queries = term if queries is None else queries + term
    if last:
        mean = jnp.sum(squares, axis=1, keepdims=True) * (1.0 / gain.shape[1])
        mine, other, cosine, sine, out = refs
        core0 = (where[0] & CORE) == 0
        k_sum = jnp.where(core0, mine[...], other[...])
        v_sum = jnp.where(core0, other[...], mine[...])
        out[...] = attend(
            queries, k_sum, v_sum, cosine[...], sine[...], lax.rsqrt(mean + EPS)
        )
    else:
        refs[0][...] = queries
        refs[1][...] = squares


def query_call(where, gain, pieces, weight, carry=(), extra=()):
    arrays, places = [array for array, _ in pieces], [symbols for _, symbols in pieces]
    tokens, width, columns = *arrays[0].shape[1:], weight.shape[1]
    rows = width * sum(len(p) for p in places)
    if extra:
        out_shape = [jax.ShapeDtypeStruct((tokens, columns), jnp.bfloat16)]
    else:
        out_shape = [
            jax.ShapeDtypeStruct((tokens, columns), jnp.float32),
            jax.ShapeDtypeStruct((tokens, LANE), jnp.float32),
        ]
    count = 2 + len(arrays) + len(carry) + len(extra)
    return pl.pallas_call(
        functools.partial(query_kernel, places, bool(carry), bool(extra)),
        out_shape=out_shape,
        in_specs=[smem()] + [vmem()] * count,
        out_specs=[vmem()] * len(out_shape),
        compiler_params=pltpu.CompilerParams(vmem_limit_bytes=4 * MIB),
        cost_estimate=pl.CostEstimate(
            flops=2 * tokens * columns * rows,
            bytes_accessed=2 * columns * rows,
            transcendentals=0,
        ),
    )(where, gain, *arrays, weight, *carry, *extra)


def output_kernel(groups, width, attended, weight, *outs):
    left = attended[...]
    for spots, out in zip(groups, outs):
        for block, spot in enumerate(spots):
            columns = weight[:, spot * width : (spot + 1) * width]
            out[block] = dot(left, columns).astype(out.dtype)


def output_call(attended, held, width, groups):
    weight, order = held
    tokens, depth = attended.shape
    spots = [[order.index(s) for s in symbols] for symbols, _ in groups]
    columns = width * sum(len(s) for s in spots)
    return pl.pallas_call(
        functools.partial(output_kernel, spots, width),
        out_shape=[jax.ShapeDtypeStruct((len(s), tokens, width), t) for s, t in groups],
        in_specs=[vmem(), vmem()],
        out_specs=[vmem()] * len(groups),
        compiler_params=pltpu.CompilerParams(vmem_limit_bytes=4 * MIB),
        cost_estimate=pl.CostEstimate(
            flops=2 * tokens * depth * columns,
            bytes_accessed=2 * depth * columns,
            transcendentals=0,
        ),
    )(attended, weight)


def rotary_tables(tokens):
    half = HEAD // 2
    frequency = 500000.0 ** (-(jnp.arange(half, dtype=jnp.float32) * 2.0) / HEAD)
    angles = jnp.arange(tokens, dtype=jnp.float32)[:, None] * frequency[None, :]
    cosine, sine = jnp.cos(angles), jnp.sin(angles)
    return jnp.concatenate([cosine, cosine], axis=1), jnp.concatenate([-sine, sine], axis=1)


def per_device(n, act, norm_gain, wq, wk, wv, wo):
    tokens, width = act.shape
    me = lax.axis_index("wide")
    bits = [1 << i for i in range(n.bit_length() - 1)]
    ways = (bits[1], bits[2])
    diagonal = bits[1] ^ bits[2]
    near, top = combos(bits[3:-1]), bits[-1]
    far = [o ^ top for o in near]
    f32, bf16 = jnp.float32, jnp.bfloat16

    def swap(x, offset):
        return lax.ppermute(x, "wide", [(i, i ^ offset) for i in range(n)])

    def turn(x, step):
        return lax.ppermute(x, "wide", [(i, i ^ ways[(step + (i & CORE)) % 2]) for i in range(n)])

    bit = jnp.where((me & CORE) == 0, ways[0], ways[1])
    where = jnp.stack([me, me ^ bit, me ^ bit ^ diagonal]).astype(jnp.int32)
    gain = norm_gain.reshape(1, -1)

    def plain(offsets, pick=0):
        return [(o, pick) for o in offsets]

    def across(symbols):
        return [(const ^ CORE, (0, 2, 1)[pick]) for const, pick in symbols]

    def after(x, *others):
        return lax.optimization_barrier((x, *others))[0]

    shared = (n // KVH).bit_length() - 1
    raw = act
    kv_send, kv_keep, act, gain = kv_terms(shared, where, act, gain, wk, wv)

    def symbols_of(offsets):
        square = [(0, 0), (0, 1), (0, 2), (diagonal, 0)]
        return [[(const ^ o, pick) for o in offsets] for const, pick in square]

    def other(pieces):
        return [(swap(x, CORE), across(symbols)) for x, symbols in pieces]

    def order(offsets):
        home, one, two, corner = symbols_of(offsets)
        return [corner, two, one, home]

    def columns_of(offsets):
        own = sum(order(offsets), [])
        return own + across(own)

    def halved(kv, arrived=None, offset=0):
        half = kv.shape[0] // 2
        if arrived is None:
            arrived = swap(kv[:half].astype(bf16), offset)
        return kv[half:] + arrived.astype(f32)

    kv = halved(kv_keep + swap(kv_send, CORE), offset=bits[shared])
    row = jnp.stack([act, swap(raw, top)])
    far_columns, far_symbols = fetched(where, wo, width, columns_of(far))
    row, kv, far_columns = lax.optimization_barrier((row, kv, far_columns))
    far_held = (far_columns, far_symbols)
    ride = bits[shared + 1]
    side = turn(row, 0)
    rest = []
    for o in near[1:]:
        if o == ride:
            got = swap(jnp.concatenate([row, kv[: kv.shape[0] // 2].astype(bf16)], axis=2), o)
            kv = halved(kv, got[:, :, width:])
            got = got[:, :, :width]
        else:
            got = swap(row, o)
        rest.append(got)
    groups = []
    for offsets, row, side in (
        ([0, top], row, side),
        ([o ^ t for o in near[1:] for t in (0, top)], jnp.concatenate(rest), None),
    ):
        side = turn(row, 0) if side is None else side
        both = turn(jnp.concatenate([row, side]), 1)
        at = symbols_of(offsets)
        groups.append([(row, at[0]), (side, at[1]), (both, at[2] + at[3])])
    early, last = groups
    for b in bits[shared + 2 :]:
        got = after(swap(kv[: kv.shape[0] // 2].astype(bf16), b), last[1][0])
        kv = halved(kv, got)
    total = kv[0]
    for b in bits[1:shared]:
        total = total + swap(total.astype(bf16), b).astype(f32)
    kv_sums = (total, swap(total, CORE))

    call = functools.partial(query_call, where, gain, weight=wq)
    carry = call(early + other(early))
    carry = call(last[:2] + other(last[:1]), carry=carry)
    both, *carry = lax.optimization_barrier((last[2][0], *carry))
    both = [(both, last[2][1])]
    final = other(both)
    carry = call(other(last[1:2]) + both, carry=carry)
    (attended,) = call(final, carry=carry, extra=(*kv_sums, *rotary_tables(tokens)))

    def round_square(corner, terms, wait=False):
        (two, two_got), (one, one_got), (home, home_got) = terms
        from_corner = turn(corner, 0)
        if wait:
            one = after(one, from_corner)
        got_1 = turn(added_up(one, one_got).astype(bf16), 0)
        two = added_up(two, two_got, from_corner).astype(bf16)
        return [home, home_got, got_1, turn(two, 1)], two

    def added_up(home, *arrived):
        for x in arrived:
            home = home + x.astype(f32)
        return home

    def along_z(blocks):
        return added_up(
            blocks[0], *[swap(blocks[i].astype(bf16), o) for i, o in enumerate(near) if o]
        )

    def theirs(symbols):
        return [(across(s), bf16) for s in symbols]

    def ours(symbols):
        return [(s, f32) for s in symbols]

    project = functools.partial(output_call, held=far_held, width=width)
    sent = project(attended, groups=theirs(order(far)[:1]))
    own = project(after(attended, *sent), groups=ours(order(far)))
    corner = added_up(own[0], swap(sent[0], CORE)).astype(bf16)
    sent = project(after(attended, corner), groups=theirs(order(far)[1:]))
    terms = [(x, swap(y, CORE)) for x, y in zip(own[1:], sent)]
    far_sums, two = round_square(corner, terms)
    near_held = fetched(after(where, sent[-1]), wo, width, columns_of(near))
    sent = output_call(attended, near_held, width, theirs(order(near)))
    own = output_call(after(attended, sent[0]), near_held, width, ours(order(near)))
    terms = [(x, swap(y, CORE)) for x, y in zip(own, sent)]
    corner = added_up(after(own[0], two), terms[0][1]).astype(bf16)
    near_sums, _ = round_square(corner, terms[1:], wait=True)
    got = swap(along_z(added_up(*far_sums)).astype(bf16), top)
    out = added_up(along_z(added_up(*near_sums)), got)
    return out.astype(bf16)


def solution(mesh):
    return jax.shard_map(
        functools.partial(per_device, mesh.shape["wide"]),
        mesh=mesh,
        in_specs=(
            P("groups", "wide"),
            P(),
            P(None, "wide"),
            P("wide", None),
            P("wide", None),
            P("wide", None),
        ),
        out_specs=P("groups", "wide"),
        check_vma=False,
    )
```

```python
import functools

import jax
import jax.numpy as jnp
from jax import lax
from jax.experimental import pallas as pl
from jax.experimental.pallas import tpu as pltpu
from jax.sharding import PartitionSpec as P

HEADS = 128
KVH = 8
HEAD = 128
LANE = 128
EPS = 1e-05
MIB = 1 << 20
CORE = 1
KV_WEIGHT = 16


def combos(bits):
    out = [0]
    for b in bits:
        out = out + [o ^ b for o in out]
    return out


def vmem():
    return pl.BlockSpec(memory_space=pltpu.VMEM)


def smem():
    return pl.BlockSpec(memory_space=pltpu.SMEM)


def hbm():
    return pl.BlockSpec(memory_space=pltpu.HBM)


def in_hbm(x):
    return pltpu.with_memory_space_constraint(x, pltpu.HBM)


def dot(a, b):
    return jnp.dot(a, b, preferred_element_type=jnp.float32)


def fetch_kernel(symbols, width, where, source, target, sems):
    copies = []
    for i, (const, pick) in enumerate(symbols):
        start = pl.multiple_of((where[pick] ^ const) * width, LANE)
        copy = pltpu.make_async_copy(
            source.at[:, pl.ds(start, width)], target.at[i], sems.at[i]
        )
        copy.start()
        copies.append(copy)
    for copy in copies:
        copy.wait()


def fetched(where, weight, width, symbols):
    shape = (len(symbols), weight.shape[0], width)
    blocks = pl.pallas_call(
        functools.partial(fetch_kernel, symbols, width),
        out_shape=jax.ShapeDtypeStruct(shape, weight.dtype),
        in_specs=[smem(), hbm()],
        out_specs=vmem(),
        scratch_shapes=[pltpu.SemaphoreType.DMA((len(symbols),))],
        compiler_params=pltpu.CompilerParams(vmem_limit_bytes=MIB),
        cost_estimate=pl.CostEstimate(
            flops=0, bytes_accessed=4 * shape[0] * shape[1] * shape[2], transcendentals=0
        ),
    )(where, in_hbm(weight))
    return blocks, symbols


def kv_kernel(shared, where, act, gain, wk, wv, send, keep, abuf, gbuf, kbuf, vbuf, sems):
    me = where[0]
    width = act.shape[1]
    own = pl.ds(pl.multiple_of(me * width, LANE), width)
    pairs = [(act, abuf), (gain, gbuf), (wk, kbuf), (wv, vbuf)]
    copies = [pltpu.make_async_copy(x, y, sems.at[i]) for i, (x, y) in enumerate(pairs)]
    for c in copies:
        c.start()
    for c in copies:
        c.wait()
    scaled = (abuf[...].astype(jnp.float32) * gbuf[:, own]).astype(jnp.bfloat16)
    k, v = dot(scaled, kbuf[...]), dot(scaled, vbuf[...])
    core0 = (me & CORE) == 0
    for h in range(KVH):
        off = h ^ (me >> shared)
        spot = 0
        for b in range(KVH.bit_length() - 1):
            spot = spot * 2 + (1 - ((off >> b) & 1))
        kh, vh = k[:, h * HEAD : (h + 1) * HEAD], v[:, h * HEAD : (h + 1) * HEAD]
        keep[spot] = jnp.where(core0, kh, vh)
        send[spot] = jnp.where(core0, vh, kh)


def kv_terms(shared, where, act, gain, wk, wv):
    tokens = act.shape[0]
    return pl.pallas_call(
        functools.partial(kv_kernel, shared),
        out_shape=[jax.ShapeDtypeStruct((KVH, tokens, HEAD), jnp.float32)] * 2
        + [jax.ShapeDtypeStruct(x.shape, x.dtype) for x in (act, gain)],
        in_specs=[smem()] + [hbm()] * 4,
        out_specs=[vmem()] * 4,
        scratch_shapes=[
            pltpu.VMEM(wk.shape, wk.dtype),
            pltpu.VMEM(wv.shape, wv.dtype),
            pltpu.SemaphoreType.DMA((4,)),
        ],
        compiler_params=pltpu.CompilerParams(vmem_limit_bytes=12 * MIB),
        cost_estimate=pl.CostEstimate(
            flops=KV_WEIGHT * 4 * tokens * wk.size,
            bytes_accessed=KV_WEIGHT * 4 * wk.size,
            transcendentals=0,
        ),
    )(where, in_hbm(act), in_hbm(gain), in_hbm(wk), in_hbm(wv))


def attend(queries, k_sum, v_sum, cosine, sine, scale):
    k_rows = (k_sum * scale).astype(jnp.bfloat16).astype(jnp.float32)
    value = (v_sum * scale).astype(jnp.bfloat16)
    tokens, heads = queries.shape[0], queries.shape[1] // HEAD

    def rotate(x, cosine, sine):
        half = HEAD // 2
        turned = jnp.concatenate([x[:, half:], x[:, :half]], axis=1)
        return (x * cosine + turned * sine).astype(jnp.bfloat16)

    def stacked(parts):
        return jnp.concatenate(parts, axis=0)

    key = rotate(k_rows, cosine, sine)
    queries = queries * scale
    rows = stacked([queries[:, h * HEAD : (h + 1) * HEAD] for h in range(heads)])
    query = rotate(rows, stacked([cosine] * heads), stacked([sine] * heads))
    scores = lax.dot_general(
        query, key, (((1,), (1,)), ((), ())), preferred_element_type=jnp.float32
    ) * HEAD ** (-0.5)
    at = lax.broadcasted_iota(jnp.int32, (tokens, tokens), 0)
    seen = at >= lax.broadcasted_iota(jnp.int32, (tokens, tokens), 1)
    bias = jnp.where(seen, 0.0, -jnp.inf)
    scores = scores + stacked([bias] * heads)
    weights = jnp.exp(scores - jnp.max(scores, axis=1, keepdims=True))
    probs = (weights / jnp.sum(weights, axis=1, keepdims=True)).astype(jnp.bfloat16)
    out = dot(probs, value).astype(jnp.bfloat16)
    return jnp.concatenate([out[h * tokens : (h + 1) * tokens] for h in range(heads)], axis=1)


def query_kernel(places, carried, last, *refs):
    refs = list(refs)
    where, gain = refs.pop(0), refs.pop(0)
    pieces = [refs.pop(0) for _ in places]
    weight = refs.pop(0)
    queries = refs.pop(0)[...] if carried else None
    squares = refs.pop(0)[...] if carried else None
    width = pieces[0].shape[2]
    for piece, blocks in zip(pieces, places):
        for block, (const, pick) in enumerate(blocks):
            span = pl.ds(pl.multiple_of((where[pick] ^ const) * width, LANE), width)
            x = piece[block].astype(jnp.float32)
            for c in range(0, width, LANE):
                square = x[:, c : c + LANE] * x[:, c : c + LANE]
                squares = square if squares is None else squares + square
            term = dot((x * gain[:, span]).astype(jnp.bfloat16), weight[span, :])
            queries = term if queries is None else queries + term
    if last:
        mean = jnp.sum(squares, axis=1, keepdims=True) * (1.0 / gain.shape[1])
        mine, other, cosine, sine, out = refs
        core0 = (where[0] & CORE) == 0
        k_sum = jnp.where(core0, mine[...], other[...])
        v_sum = jnp.where(core0, other[...], mine[...])
        out[...] = attend(
            queries, k_sum, v_sum, cosine[...], sine[...], lax.rsqrt(mean + EPS)
        )
    else:
        refs[0][...] = queries
        refs[1][...] = squares


def query_call(where, gain, pieces, weight, carry=(), extra=()):
    arrays, places = [array for array, _ in pieces], [symbols for _, symbols in pieces]
    tokens, width, columns = *arrays[0].shape[1:], weight.shape[1]
    rows = width * sum(len(p) for p in places)
    if extra:
        out_shape = [jax.ShapeDtypeStruct((tokens, columns), jnp.bfloat16)]
    else:
        out_shape = [
            jax.ShapeDtypeStruct((tokens, columns), jnp.float32),
            jax.ShapeDtypeStruct((tokens, LANE), jnp.float32),
        ]
    count = 2 + len(arrays) + len(carry) + len(extra)
    return pl.pallas_call(
        functools.partial(query_kernel, places, bool(carry), bool(extra)),
        out_shape=out_shape,
        in_specs=[smem()] + [vmem()] * count,
        out_specs=[vmem()] * len(out_shape),
        compiler_params=pltpu.CompilerParams(vmem_limit_bytes=4 * MIB),
        cost_estimate=pl.CostEstimate(
            flops=2 * tokens * columns * rows,
            bytes_accessed=2 * columns * rows,
            transcendentals=0,
        ),
    )(where, gain, *arrays, weight, *carry, *extra)


def output_kernel(groups, attended, weight, *outs):
    left = attended[...]
    for spots, out in zip(groups, outs):
        for block, spot in enumerate(spots):
            out[block] = dot(left, weight[spot]).astype(out.dtype)


def output_call(attended, held, width, groups):
    weight, order = held
    tokens, depth = attended.shape
    spots = [[order.index(s) for s in symbols] for symbols, _ in groups]
    columns = width * sum(len(s) for s in spots)
    return pl.pallas_call(
        functools.partial(output_kernel, spots),
        out_shape=[jax.ShapeDtypeStruct((len(s), tokens, width), t) for s, t in groups],
        in_specs=[vmem(), vmem()],
        out_specs=[vmem()] * len(groups),
        compiler_params=pltpu.CompilerParams(vmem_limit_bytes=4 * MIB),
        cost_estimate=pl.CostEstimate(
            flops=2 * tokens * depth * columns,
            bytes_accessed=2 * depth * columns,
            transcendentals=0,
        ),
    )(attended, weight)


def rotary_tables(tokens):
    half = HEAD // 2
    frequency = 500000.0 ** (-(jnp.arange(half, dtype=jnp.float32) * 2.0) / HEAD)
    angles = jnp.arange(tokens, dtype=jnp.float32)[:, None] * frequency[None, :]
    cosine, sine = jnp.cos(angles), jnp.sin(angles)
    return jnp.concatenate([cosine, cosine], axis=1), jnp.concatenate([-sine, sine], axis=1)


def per_device(n, act, norm_gain, wq, wk, wv, wo):
    tokens, width = act.shape
    me = lax.axis_index("wide")
    bits = [1 << i for i in range(n.bit_length() - 1)]
    ways = (bits[1], bits[2])
    diagonal = bits[1] ^ bits[2]
    near, top = combos(bits[3:-1]), bits[-1]
    far = [o ^ top for o in near]
    f32, bf16 = jnp.float32, jnp.bfloat16

    def swap(x, offset):
        return lax.ppermute(x, "wide", [(i, i ^ offset) for i in range(n)])

    def turn(x, step):
        return lax.ppermute(x, "wide", [(i, i ^ ways[(step + (i & CORE)) % 2]) for i in range(n)])

    bit = jnp.where((me & CORE) == 0, ways[0], ways[1])
    where = jnp.stack([me, me ^ bit, me ^ bit ^ diagonal]).astype(jnp.int32)
    gain = norm_gain.reshape(1, -1)

    def plain(offsets, pick=0):
        return [(o, pick) for o in offsets]

    def across(symbols):
        return [(const ^ CORE, (0, 2, 1)[pick]) for const, pick in symbols]

    def after(x, *others):
        return lax.optimization_barrier((x, *others))[0]

    shared = (n // KVH).bit_length() - 1
    raw = act
    kv_send, kv_keep, act, gain = kv_terms(shared, where, act, gain, wk, wv)

    def symbols_of(offsets):
        square = [(0, 0), (0, 1), (0, 2), (diagonal, 0)]
        return [[(const ^ o, pick) for o in offsets] for const, pick in square]

    def other(pieces):
        return [(swap(x, CORE), across(symbols)) for x, symbols in pieces]

    def order(offsets):
        home, one, two, corner = symbols_of(offsets)
        return [corner + one, two, home]

    def columns_of(offsets):
        own = sum(order(offsets), [])
        return own + across(own)

    def halved(kv, arrived=None, offset=0):
        half = kv.shape[0] // 2
        if arrived is None:
            arrived = swap(kv[:half].astype(bf16), offset)
        return kv[half:] + arrived.astype(f32)

    kv = halved(kv_keep + swap(kv_send, CORE), offset=bits[shared])
    row = jnp.stack([act, swap(raw, top)])
    far_blocks, far_symbols = fetched(where, wo, width, columns_of(far))
    row, kv, far_blocks = lax.optimization_barrier((row, kv, far_blocks))
    far_held = (far_blocks, far_symbols)
    ride = bits[shared + 1]
    side = turn(row, 0)
    rest = []
    for o in near[1:]:
        if o == ride:
            got = swap(jnp.concatenate([row, kv[: kv.shape[0] // 2].astype(bf16)], axis=2), o)
            kv = halved(kv, got[:, :, width:])
            got = got[:, :, :width]
        else:
            got = swap(row, o)
        rest.append(got)
    groups = []
    for offsets, row, side in (
        ([0, top], row, side),
        ([o ^ t for o in near[1:] for t in (0, top)], jnp.concatenate(rest), None),
    ):
        if side is None:
            side = turn(row, 0)
            for b in bits[shared + 2 :]:
                kv = halved(kv, offset=b)
            near_blocks, near_symbols = fetched(after(where, row), wo, width, columns_of(near))
            side, kv, near_blocks = lax.optimization_barrier((side, kv, near_blocks))
            near_held = (near_blocks, near_symbols)
        both = turn(jnp.concatenate([row, side]), 1)
        at = symbols_of(offsets)
        groups.append([(row, at[0]), (side, at[1]), (both, at[2] + at[3])])
    early, last = groups
    partners = [swap(kv[0].astype(bf16), o) for o in combos(bits[1:shared])[1:]]

    call = functools.partial(query_call, where, gain, weight=wq)
    carry = call(early + other(early))
    carry = call(last[:2] + other(last[:2]), carry=carry)
    both, *carry = lax.optimization_barrier((last[2][0], *carry))
    both = [(both, last[2][1])]
    total = kv[0]
    for x in partners:
        total = total + after(x, carry[0]).astype(f32)
    final = other(both)
    carry = call(both, carry=carry)
    (attended,) = call(
        final, carry=carry, extra=(total, swap(total, CORE), *rotary_tables(tokens))
    )

    def round_square(first, two, home):
        got = turn(first, 0)
        k = got.shape[0] // 2
        two = added_up(*two, got[:k]).astype(bf16)
        return [*home, got[k:], turn(two, 1)], two

    def added_up(home, *arrived):
        for x in arrived:
            home = home + x.astype(f32)
        return home

    def along_z(blocks):
        return added_up(
            blocks[0], *[swap(blocks[i].astype(bf16), o) for i, o in enumerate(near) if o]
        )

    def theirs(symbols):
        return [(across(s), bf16) for s in symbols]

    def ours(symbols):
        return [(s, f32) for s in symbols]

    def paired(own, sent):
        return [(x, swap(y, CORE)) for x, y in zip(own, sent)]

    project = functools.partial(output_call, held=far_held, width=width)
    sent = project(attended, groups=theirs(order(far)[:1]))
    own = project(after(attended, *sent), groups=ours(order(far)))
    first = added_up(own[0], swap(sent[0], CORE)).astype(bf16)
    sent = project(after(attended, first), groups=theirs(order(far)[1:]))
    far_sums, two = round_square(first, *paired(own[1:], sent))
    project = functools.partial(output_call, held=near_held, width=width)
    sent = project(after(attended, sent[-1]), groups=theirs(order(near)))
    own = project(after(attended, sent[0]), groups=ours(order(near)))
    pairs = paired(own, sent)
    first = added_up(after(pairs[0][0], two), pairs[0][1]).astype(bf16)
    near_sums, _ = round_square(first, *pairs[1:])
    got = swap(along_z(added_up(*far_sums)).astype(bf16), top)
    out = added_up(along_z(added_up(*near_sums)), got)
    return out.astype(bf16)


def solution(mesh):
    return jax.shard_map(
        functools.partial(per_device, mesh.shape["wide"]),
        mesh=mesh,
        in_specs=(
            P("groups", "wide"),
            P(),
            P(None, "wide"),
            P("wide", None),
            P("wide", None),
            P("wide", None),
        ),
        out_specs=P("groups", "wide"),
        check_vma=False,
    )
```

```python
import functools

import jax
import jax.numpy as jnp
from jax import lax
from jax.experimental import pallas as pl
from jax.experimental.pallas import tpu as pltpu
from jax.sharding import PartitionSpec as P

HEADS = 128
KVH = 8
HEAD = 128
LANE = 128
EPS = 1e-05
MIB = 1 << 20
CORE = 1
KV_WEIGHT = 16


def combos(bits):
    out = [0]
    for b in bits:
        out = out + [o ^ b for o in out]
    return out


def vmem():
    return pl.BlockSpec(memory_space=pltpu.VMEM)


def smem():
    return pl.BlockSpec(memory_space=pltpu.SMEM)


def hbm():
    return pl.BlockSpec(memory_space=pltpu.HBM)


def in_hbm(x):
    return pltpu.with_memory_space_constraint(x, pltpu.HBM)


def device(where, symbol):
    const, (i, j) = symbol
    return where[3 * i + j] ^ const


def dot(a, b):
    return jnp.dot(a, b, preferred_element_type=jnp.float32)


def fetch_kernel(symbols, width, where, source, target, sems):
    copies = []
    for i, (const, pick) in enumerate(symbols):
        start = pl.multiple_of((device(where, (const, pick))) * width, LANE)
        copy = pltpu.make_async_copy(
            source.at[:, pl.ds(start, width)], target.at[i], sems.at[i]
        )
        copy.start()
        copies.append(copy)
    for copy in copies:
        copy.wait()


def fetched(where, weight, width, symbols):
    shape = (len(symbols), weight.shape[0], width)
    blocks = pl.pallas_call(
        functools.partial(fetch_kernel, symbols, width),
        out_shape=jax.ShapeDtypeStruct(shape, weight.dtype),
        in_specs=[smem(), hbm()],
        out_specs=vmem(),
        scratch_shapes=[pltpu.SemaphoreType.DMA((len(symbols),))],
        compiler_params=pltpu.CompilerParams(vmem_limit_bytes=MIB),
        cost_estimate=pl.CostEstimate(
            flops=0, bytes_accessed=4 * shape[0] * shape[1] * shape[2], transcendentals=0
        ),
    )(where, in_hbm(weight))
    return blocks, symbols


def kv_kernel(shared, where, act, gain, wk, wv, send, keep, abuf, gbuf, kbuf, vbuf, sems):
    me = where[0]
    width = act.shape[1]
    own = pl.ds(pl.multiple_of(me * width, LANE), width)
    pairs = [(act, abuf), (gain, gbuf), (wk, kbuf), (wv, vbuf)]
    copies = [pltpu.make_async_copy(x, y, sems.at[i]) for i, (x, y) in enumerate(pairs)]
    for c in copies:
        c.start()
    for c in copies:
        c.wait()
    scaled = (abuf[...].astype(jnp.float32) * gbuf[:, own]).astype(jnp.bfloat16)
    k, v = dot(scaled, kbuf[...]), dot(scaled, vbuf[...])
    core0 = (me & CORE) == 0
    for h in range(KVH):
        off = h ^ (me >> shared)
        low, a, b = off & 1, (off >> 1) & 1, (off >> 2) & 1
        spot_0, spot_1 = 7 - (4 * low + 2 * b + a), 7 - (4 * low + 2 * a + b)
        kh, vh = k[:, h * HEAD : (h + 1) * HEAD], v[:, h * HEAD : (h + 1) * HEAD]
        keep[jnp.where(core0, spot_0, spot_1)] = jnp.where(core0, kh, vh)
        send[jnp.where(core0, spot_1, spot_0)] = jnp.where(core0, vh, kh)


def kv_terms(shared, where, act, gain, wk, wv):
    tokens = act.shape[0]
    return pl.pallas_call(
        functools.partial(kv_kernel, shared),
        out_shape=[jax.ShapeDtypeStruct((KVH, tokens, HEAD), jnp.float32)] * 2
        + [jax.ShapeDtypeStruct(x.shape, x.dtype) for x in (act, gain)],
        in_specs=[smem()] + [hbm()] * 4,
        out_specs=[vmem()] * 4,
        scratch_shapes=[
            pltpu.VMEM(wk.shape, wk.dtype),
            pltpu.VMEM(wv.shape, wv.dtype),
            pltpu.SemaphoreType.DMA((4,)),
        ],
        compiler_params=pltpu.CompilerParams(vmem_limit_bytes=12 * MIB),
        cost_estimate=pl.CostEstimate(
            flops=KV_WEIGHT * 4 * tokens * wk.size,
            bytes_accessed=KV_WEIGHT * 4 * wk.size,
            transcendentals=0,
        ),
    )(where, in_hbm(act), in_hbm(gain), in_hbm(wk), in_hbm(wv))


def attend(queries, k_sum, v_sum, cosine, sine, scale):
    k_rows = (k_sum * scale).astype(jnp.bfloat16).astype(jnp.float32)
    value = (v_sum * scale).astype(jnp.bfloat16)
    tokens, heads = queries.shape[0], queries.shape[1] // HEAD

    def rotate(x, cosine, sine):
        half = HEAD // 2
        turned = jnp.concatenate([x[:, half:], x[:, :half]], axis=1)
        return (x * cosine + turned * sine).astype(jnp.bfloat16)

    def stacked(parts):
        return jnp.concatenate(parts, axis=0)

    key = rotate(k_rows, cosine, sine)
    queries = queries * scale
    rows = stacked([queries[:, h * HEAD : (h + 1) * HEAD] for h in range(heads)])
    query = rotate(rows, stacked([cosine] * heads), stacked([sine] * heads))
    scores = lax.dot_general(
        query, key, (((1,), (1,)), ((), ())), preferred_element_type=jnp.float32
    ) * HEAD ** (-0.5)
    at = lax.broadcasted_iota(jnp.int32, (tokens, tokens), 0)
    seen = at >= lax.broadcasted_iota(jnp.int32, (tokens, tokens), 1)
    bias = jnp.where(seen, 0.0, -jnp.inf)
    scores = scores + stacked([bias] * heads)
    weights = jnp.exp(scores - jnp.max(scores, axis=1, keepdims=True))
    probs = (weights / jnp.sum(weights, axis=1, keepdims=True)).astype(jnp.bfloat16)
    out = dot(probs, value).astype(jnp.bfloat16)
    return jnp.concatenate([out[h * tokens : (h + 1) * tokens] for h in range(heads)], axis=1)


def query_kernel(places, carried, last, *refs):
    refs = list(refs)
    where, gain = refs.pop(0), refs.pop(0)
    pieces = [refs.pop(0) for _ in places]
    weight = refs.pop(0)
    queries = refs.pop(0)[...] if carried else None
    squares = refs.pop(0)[...] if carried else None
    width = pieces[0].shape[2]
    for piece, blocks in zip(pieces, places):
        for block, (const, pick) in enumerate(blocks):
            span = pl.ds(pl.multiple_of((device(where, (const, pick))) * width, LANE), width)
            x = piece[block].astype(jnp.float32)
            for c in range(0, width, LANE):
                square = x[:, c : c + LANE] * x[:, c : c + LANE]
                squares = square if squares is None else squares + square
            term = dot((x * gain[:, span]).astype(jnp.bfloat16), weight[span, :])
            queries = term if queries is None else queries + term
    if last:
        mean = jnp.sum(squares, axis=1, keepdims=True) * (1.0 / gain.shape[1])
        mine, other, cosine, sine, out = refs
        core0 = (where[0] & CORE) == 0
        k_sum = jnp.where(core0, mine[...], other[...])
        v_sum = jnp.where(core0, other[...], mine[...])
        out[...] = attend(
            queries, k_sum, v_sum, cosine[...], sine[...], lax.rsqrt(mean + EPS)
        )
    else:
        refs[0][...] = queries
        refs[1][...] = squares


def query_call(where, gain, pieces, weight, carry=(), extra=()):
    arrays, places = [array for array, _ in pieces], [symbols for _, symbols in pieces]
    tokens, width, columns = *arrays[0].shape[1:], weight.shape[1]
    rows = width * sum(len(p) for p in places)
    if extra:
        out_shape = [jax.ShapeDtypeStruct((tokens, columns), jnp.bfloat16)]
    else:
        out_shape = [
            jax.ShapeDtypeStruct((tokens, columns), jnp.float32),
            jax.ShapeDtypeStruct((tokens, LANE), jnp.float32),
        ]
    count = 2 + len(arrays) + len(carry) + len(extra)
    return pl.pallas_call(
        functools.partial(query_kernel, places, bool(carry), bool(extra)),
        out_shape=out_shape,
        in_specs=[smem()] + [vmem()] * count,
        out_specs=[vmem()] * len(out_shape),
        compiler_params=pltpu.CompilerParams(vmem_limit_bytes=4 * MIB),
        cost_estimate=pl.CostEstimate(
            flops=2 * tokens * columns * rows,
            bytes_accessed=2 * columns * rows,
            transcendentals=0,
        ),
    )(where, gain, *arrays, weight, *carry, *extra)


def output_kernel(groups, attended, weight, *outs):
    left = attended[...]
    for spots, out in zip(groups, outs):
        for block, spot in enumerate(spots):
            out[block] = dot(left, weight[spot]).astype(out.dtype)


def output_fetch_kernel(groups, where, attended, weight, *refs):
    outs, buf, sems = refs[: len(groups)], refs[-2], refs[-1]
    copies = []
    for i, (const, pick) in enumerate(sum(groups, [])):
        width = buf.shape[2]
        start = pl.multiple_of((device(where, (const, pick))) * width, LANE)
        copy = pltpu.make_async_copy(weight.at[:, pl.ds(start, width)], buf.at[i], sems.at[i])
        copy.start()
        copies.append(copy)
    left = attended[...]
    i = 0
    for symbols, out in zip(groups, outs):
        for block in range(len(symbols)):
            copies[i].wait()
            out[block] = dot(left, buf[i]).astype(out.dtype)
            i += 1


def output_call(attended, width, groups, held=None, where=None, weight=None):
    tokens, depth = attended.shape
    blocks = sum(len(s) for s, _ in groups)
    if held is not None:
        kernel = functools.partial(
            output_kernel, [[held[1].index(s) for s in symbols] for symbols, _ in groups]
        )
        operands, specs, scratch = (attended, held[0]), [vmem(), vmem()], []
    else:
        kernel = functools.partial(output_fetch_kernel, [symbols for symbols, _ in groups])
        operands, specs = (where, attended, in_hbm(weight)), [smem(), vmem(), hbm()]
        scratch = [
            pltpu.VMEM((blocks, depth, width), weight.dtype),
            pltpu.SemaphoreType.DMA((blocks,)),
        ]
    return pl.pallas_call(
        kernel,
        out_shape=[jax.ShapeDtypeStruct((len(s), tokens, width), t) for s, t in groups],
        in_specs=specs,
        out_specs=[vmem()] * len(groups),
        scratch_shapes=scratch,
        compiler_params=pltpu.CompilerParams(vmem_limit_bytes=10 * MIB),
        cost_estimate=pl.CostEstimate(
            flops=2 * tokens * depth * width * blocks,
            bytes_accessed=2 * depth * width * blocks,
            transcendentals=0,
        ),
    )(*operands)


def rotary_tables(tokens):
    half = HEAD // 2
    frequency = 500000.0 ** (-(jnp.arange(half, dtype=jnp.float32) * 2.0) / HEAD)
    angles = jnp.arange(tokens, dtype=jnp.float32)[:, None] * frequency[None, :]
    cosine, sine = jnp.cos(angles), jnp.sin(angles)
    return jnp.concatenate([cosine, cosine], axis=1), jnp.concatenate([-sine, sine], axis=1)


def per_device(n, act, norm_gain, wq, wk, wv, wo):
    tokens, width = act.shape
    me = lax.axis_index("wide")
    bits = [1 << i for i in range(n.bit_length() - 1)]
    ways = (bits[1], bits[2])
    diagonal = bits[1] ^ bits[2]
    low, z_ways = combos(bits[3:-2]), (bits[-2], bits[-1])
    f32, bf16 = jnp.float32, jnp.bfloat16

    def swap(x, offset):
        return lax.ppermute(x, "wide", [(i, i ^ offset) for i in range(n)])

    def by_core(x, pair, step):
        return lax.ppermute(x, "wide", [(i, i ^ pair[(step + (i & CORE)) % 2]) for i in range(n)])

    def turn(x, step):
        return by_core(x, ways, step)

    def along(x, step):
        return by_core(x, z_ways, step)

    def steps(pair):
        first = jnp.where((me & CORE) == 0, pair[0], pair[1])
        return [jnp.zeros_like(me), first, first ^ pair[0] ^ pair[1]]

    where = jnp.stack([me ^ i ^ j for i in steps(ways) for j in steps(z_ways)]).astype(jnp.int32)
    gain = norm_gain.reshape(1, -1)

    def across(symbols):
        flip = (0, 2, 1)
        return [(const ^ CORE, (flip[i], flip[j])) for const, (i, j) in symbols]

    near = [(o, j) for j in (0, 1) for o in low]
    far = [(o, 2) for o in low] + [(o ^ z_ways[0] ^ z_ways[1], 0) for o in low]

    def after(x, *others):
        return lax.optimization_barrier((x, *others))[0]

    shared = (n // KVH).bit_length() - 1
    raw = act
    kv_send, kv_keep, act, gain = kv_terms(shared, where, act, gain, wk, wv)

    def symbols_of(offsets):
        square = [(0, 0), (0, 1), (0, 2), (diagonal, 0)]
        return [[(const ^ o, (i, j)) for o, j in offsets] for const, i in square]

    def other(pieces):
        return [(swap(x, CORE), across(symbols)) for x, symbols in pieces]

    def order(offsets):
        home, one, two, corner = symbols_of(offsets)
        return [corner + one, two, home]

    def columns_of(offsets):
        own = sum(order(offsets), [])
        return own + across(own)

    def halved(kv, send, way):
        half = kv.shape[0] // 2
        return kv[half:] + send(kv[:half].astype(bf16), way).astype(f32)

    kv = halved(kv_keep + swap(kv_send, CORE), swap, bits[shared])
    far_blocks, far_symbols = fetched(where, wo, width, columns_of(far))
    row = jnp.stack([act] + [swap(raw, o) for o in low[1:]])
    row = jnp.concatenate([row, along(row, 0)])
    row, kv, far_blocks = lax.optimization_barrier((row, kv, far_blocks))
    far_held = (far_blocks, far_symbols)
    groups = []
    for offsets in (near, far):
        if offsets is far:
            half = kv[: kv.shape[0] // 2].astype(bf16)
            k = min(row.shape[0], half.shape[0])
            extra = jnp.zeros((row.shape[0], *half.shape[1:]), bf16).at[:k].set(half[:k])
            got = along(jnp.concatenate([row, extra], axis=2), 1)
            row = got[:, :, :width]
            kv = kv[kv.shape[0] // 2 :] + got[:k, :, width:].astype(f32)
            side = turn(row, 0)
            kv = halved(kv, along, 0)
            side, kv = lax.optimization_barrier((side, kv))
        else:
            side = turn(row, 0)
        both = turn(jnp.concatenate([row, side]), 1)
        at = symbols_of(offsets)
        groups.append([(row, at[0]), (side, at[1]), (both, at[2] + at[3])])
    early, last = groups
    partners = [swap(kv[0].astype(bf16), o) for o in combos(bits[1:shared])[1:]]

    call = functools.partial(query_call, where, gain, weight=wq)
    carry = call(early + other(early))
    carry = call(last[:2] + other(last[:2]), carry=carry)
    both, *carry = lax.optimization_barrier((last[2][0], *carry))
    both = [(both, last[2][1])]
    total = kv[0]
    for x in partners:
        total = total + after(x, carry[0]).astype(f32)
    final = other(both)
    carry = call(both, carry=carry)
    (attended,) = call(
        final, carry=carry, extra=(total, swap(total, CORE), *rotary_tables(tokens))
    )

    def round_square(first, two, home):
        got = turn(first, 0)
        k = got.shape[0] // 2
        two = added_up(*two, got[:k]).astype(bf16)
        return [*home, got[k:]], two

    def added_up(home, *arrived):
        for x in arrived:
            home = home + x.astype(f32)
        return home

    def theirs(symbols):
        return [(across(s), bf16) for s in symbols]

    def ours(symbols):
        return [(s, f32) for s in symbols]

    def paired(own, sent):
        return [(x, swap(y, CORE)) for x, y in zip(own, sent)]

    project = functools.partial(output_call, held=far_held, width=width)
    sent = project(attended, groups=theirs(order(far)[:1]))
    own = project(after(attended, *sent), groups=ours(order(far)))
    first = added_up(own[0], swap(sent[0], CORE)).astype(bf16)
    sent = project(after(attended, first), groups=theirs(order(far)[1:]))
    far_home, far_two = round_square(first, *paired(own[1:], sent))
    far_sum = added_up(*far_home, turn(far_two, 1))
    project = functools.partial(output_call, width=width, where=where, weight=wo)
    sent = project(after(attended, sent[-1]), groups=theirs(order(near)))
    own = project(after(attended, sent[0]), groups=ours(order(near)))
    pairs = paired(own, sent)
    first = added_up(after(pairs[0][0], far_two), pairs[0][1]).astype(bf16)
    near_home, near_two = round_square(first, *pairs[1:])
    k = len(low)
    far_sum = added_up(far_sum[:k], along(far_sum[k:].astype(bf16), 0))
    far_got = along(far_sum.astype(bf16), 1)
    got = [turn(near_two[k:], 1), turn(near_two[:k], 1)]
    near_sum = added_up(*[x[k:] for x in near_home], got[0])
    home_sum = added_up(*[x[:k] for x in near_home], got[1])
    home_sum = added_up(home_sum, along(near_sum.astype(bf16), 0), far_got)
    out = added_up(home_sum[0], *[swap(home_sum[i].astype(bf16), o) for i, o in enumerate(low) if o])
    return out.astype(bf16)


def solution(mesh):
    return jax.shard_map(
        functools.partial(per_device, mesh.shape["wide"]),
        mesh=mesh,
        in_specs=(
            P("groups", "wide"),
            P(),
            P(None, "wide"),
            P("wide", None),
            P("wide", None),
            P("wide", None),
        ),
        out_specs=P("groups", "wide"),
        check_vma=False,
    )
```

```python
import functools

import jax
import jax.numpy as jnp
from jax import lax
from jax.experimental import pallas as pl
from jax.experimental.pallas import tpu as pltpu
from jax.sharding import PartitionSpec as P

HEADS = 128
KVH = 8
HEAD = 128
LANE = 128
EPS = 1e-05
MIB = 1 << 20
CORE = 1
KV_WEIGHT = 16


def combos(bits):
    out = [0]
    for b in bits:
        out = out + [o ^ b for o in out]
    return out


def vmem():
    return pl.BlockSpec(memory_space=pltpu.VMEM)


def smem():
    return pl.BlockSpec(memory_space=pltpu.SMEM)


def hbm():
    return pl.BlockSpec(memory_space=pltpu.HBM)


def in_hbm(x):
    return pltpu.with_memory_space_constraint(x, pltpu.HBM)


def device(where, symbol):
    const, (i, j) = symbol
    return where[3 * i + j] ^ const


def dot(a, b):
    return jnp.dot(a, b, preferred_element_type=jnp.float32)


def fetch_kernel(symbols, width, where, source, target, sems):
    copies = []
    for i, (const, pick) in enumerate(symbols):
        start = pl.multiple_of((device(where, (const, pick))) * width, LANE)
        copy = pltpu.make_async_copy(
            source.at[:, pl.ds(start, width)], target.at[i], sems.at[i]
        )
        copy.start()
        copies.append(copy)
    for copy in copies:
        copy.wait()


def fetched(where, weight, width, symbols):
    shape = (len(symbols), weight.shape[0], width)
    blocks = pl.pallas_call(
        functools.partial(fetch_kernel, symbols, width),
        out_shape=jax.ShapeDtypeStruct(shape, weight.dtype),
        in_specs=[smem(), hbm()],
        out_specs=vmem(),
        scratch_shapes=[pltpu.SemaphoreType.DMA((len(symbols),))],
        compiler_params=pltpu.CompilerParams(vmem_limit_bytes=MIB),
        cost_estimate=pl.CostEstimate(
            flops=0, bytes_accessed=4 * shape[0] * shape[1] * shape[2], transcendentals=0
        ),
    )(where, in_hbm(weight))
    return blocks, symbols


def kv_kernel(shared, where, act, gain, wk, wv, send, keep, abuf, gbuf, kbuf, vbuf, sems):
    me = where[0]
    width = act.shape[1]
    own = pl.ds(pl.multiple_of(me * width, LANE), width)
    pairs = [(act, abuf), (gain, gbuf), (wk, kbuf), (wv, vbuf)]
    copies = [pltpu.make_async_copy(x, y, sems.at[i]) for i, (x, y) in enumerate(pairs)]
    for c in copies:
        c.start()
    for c in copies:
        c.wait()
    scaled = (abuf[...].astype(jnp.float32) * gbuf[:, own]).astype(jnp.bfloat16)
    k, v = dot(scaled, kbuf[...]), dot(scaled, vbuf[...])
    core0 = (me & CORE) == 0
    for h in range(KVH):
        off = h ^ (me >> shared)
        low, a, b = off & 1, (off >> 1) & 1, (off >> 2) & 1
        spot_0, spot_1 = 7 - (4 * low + 2 * b + a), 7 - (4 * low + 2 * a + b)
        kh, vh = k[:, h * HEAD : (h + 1) * HEAD], v[:, h * HEAD : (h + 1) * HEAD]
        keep[jnp.where(core0, spot_0, spot_1)] = jnp.where(core0, kh, vh)
        send[jnp.where(core0, spot_1, spot_0)] = jnp.where(core0, vh, kh)


def kv_terms(shared, where, act, gain, wk, wv):
    tokens = act.shape[0]
    return pl.pallas_call(
        functools.partial(kv_kernel, shared),
        out_shape=[jax.ShapeDtypeStruct((KVH, tokens, HEAD), jnp.float32)] * 2
        + [jax.ShapeDtypeStruct(x.shape, x.dtype) for x in (act, gain)],
        in_specs=[smem()] + [hbm()] * 4,
        out_specs=[vmem()] * 4,
        scratch_shapes=[
            pltpu.VMEM(wk.shape, wk.dtype),
            pltpu.VMEM(wv.shape, wv.dtype),
            pltpu.SemaphoreType.DMA((4,)),
        ],
        compiler_params=pltpu.CompilerParams(vmem_limit_bytes=12 * MIB),
        cost_estimate=pl.CostEstimate(
            flops=KV_WEIGHT * 4 * tokens * wk.size,
            bytes_accessed=KV_WEIGHT * 4 * wk.size,
            transcendentals=0,
        ),
    )(where, in_hbm(act), in_hbm(gain), in_hbm(wk), in_hbm(wv))


def attend(queries, k_sum, v_sum, cosine, sine, scale):
    k_rows = (k_sum * scale).astype(jnp.bfloat16).astype(jnp.float32)
    value = (v_sum * scale).astype(jnp.bfloat16)
    tokens, heads = queries.shape[0], queries.shape[1] // HEAD

    def rotate(x, cosine, sine):
        half = HEAD // 2
        turned = jnp.concatenate([x[:, half:], x[:, :half]], axis=1)
        return (x * cosine + turned * sine).astype(jnp.bfloat16)

    def stacked(parts):
        return jnp.concatenate(parts, axis=0)

    key = rotate(k_rows, cosine, sine)
    queries = queries * scale
    rows = stacked([queries[:, h * HEAD : (h + 1) * HEAD] for h in range(heads)])
    query = rotate(rows, stacked([cosine] * heads), stacked([sine] * heads))
    scores = lax.dot_general(
        query, key, (((1,), (1,)), ((), ())), preferred_element_type=jnp.float32
    ) * HEAD ** (-0.5)
    at = lax.broadcasted_iota(jnp.int32, (tokens, tokens), 0)
    seen = at >= lax.broadcasted_iota(jnp.int32, (tokens, tokens), 1)
    bias = jnp.where(seen, 0.0, -jnp.inf)
    scores = scores + stacked([bias] * heads)
    weights = jnp.exp(scores - jnp.max(scores, axis=1, keepdims=True))
    probs = (weights / jnp.sum(weights, axis=1, keepdims=True)).astype(jnp.bfloat16)
    out = dot(probs, value).astype(jnp.bfloat16)
    return jnp.concatenate([out[h * tokens : (h + 1) * tokens] for h in range(heads)], axis=1)


def query_kernel(places, carried, last, *refs):
    refs = list(refs)
    where, gain = refs.pop(0), refs.pop(0)
    pieces = [refs.pop(0) for _ in places]
    weight = refs.pop(0)
    queries = refs.pop(0)[...] if carried else None
    squares = refs.pop(0)[...] if carried else None
    width = pieces[0].shape[2]
    for piece, blocks in zip(pieces, places):
        for block, (const, pick) in enumerate(blocks):
            span = pl.ds(pl.multiple_of((device(where, (const, pick))) * width, LANE), width)
            x = piece[block].astype(jnp.float32)
            for c in range(0, width, LANE):
                square = x[:, c : c + LANE] * x[:, c : c + LANE]
                squares = square if squares is None else squares + square
            term = dot((x * gain[:, span]).astype(jnp.bfloat16), weight[span, :])
            queries = term if queries is None else queries + term
    if last:
        mean = jnp.sum(squares, axis=1, keepdims=True) * (1.0 / gain.shape[1])
        mine, other, cosine, sine, out = refs
        core0 = (where[0] & CORE) == 0
        k_sum = jnp.where(core0, mine[...], other[...])
        v_sum = jnp.where(core0, other[...], mine[...])
        out[...] = attend(
            queries, k_sum, v_sum, cosine[...], sine[...], lax.rsqrt(mean + EPS)
        )
    else:
        refs[0][...] = queries
        refs[1][...] = squares


def query_call(where, gain, pieces, weight, carry=(), extra=()):
    arrays, places = [array for array, _ in pieces], [symbols for _, symbols in pieces]
    tokens, width, columns = *arrays[0].shape[1:], weight.shape[1]
    rows = width * sum(len(p) for p in places)
    if extra:
        out_shape = [jax.ShapeDtypeStruct((tokens, columns), jnp.bfloat16)]
    else:
        out_shape = [
            jax.ShapeDtypeStruct((tokens, columns), jnp.float32),
            jax.ShapeDtypeStruct((tokens, LANE), jnp.float32),
        ]
    count = 2 + len(arrays) + len(carry) + len(extra)
    return pl.pallas_call(
        functools.partial(query_kernel, places, bool(carry), bool(extra)),
        out_shape=out_shape,
        in_specs=[smem()] + [vmem()] * count,
        out_specs=[vmem()] * len(out_shape),
        compiler_params=pltpu.CompilerParams(vmem_limit_bytes=4 * MIB),
        cost_estimate=pl.CostEstimate(
            flops=2 * tokens * columns * rows,
            bytes_accessed=2 * columns * rows,
            transcendentals=0,
        ),
    )(where, gain, *arrays, weight, *carry, *extra)


def output_kernel(groups, attended, weight, *outs):
    left = attended[...]
    for spots, out in zip(groups, outs):
        for block, spot in enumerate(spots):
            out[block] = dot(left, weight[spot]).astype(out.dtype)


def output_fetch_kernel(groups, where, attended, weight, *refs):
    outs, buf, sems = refs[: len(groups)], refs[-2], refs[-1]
    copies = []
    for i, (const, pick) in enumerate(sum(groups, [])):
        width = buf.shape[2]
        start = pl.multiple_of((device(where, (const, pick))) * width, LANE)
        copy = pltpu.make_async_copy(weight.at[:, pl.ds(start, width)], buf.at[i], sems.at[i])
        copy.start()
        copies.append(copy)
    left = attended[...]
    i = 0
    for symbols, out in zip(groups, outs):
        for block in range(len(symbols)):
            copies[i].wait()
            out[block] = dot(left, buf[i]).astype(out.dtype)
            i += 1


def output_call(attended, width, groups, held=None, where=None, weight=None):
    tokens, depth = attended.shape
    blocks = sum(len(s) for s, _ in groups)
    if held is not None:
        kernel = functools.partial(
            output_kernel, [[held[1].index(s) for s in symbols] for symbols, _ in groups]
        )
        operands, specs, scratch = (attended, held[0]), [vmem(), vmem()], []
    else:
        kernel = functools.partial(output_fetch_kernel, [symbols for symbols, _ in groups])
        operands, specs = (where, attended, in_hbm(weight)), [smem(), vmem(), hbm()]
        scratch = [
            pltpu.VMEM((blocks, depth, width), weight.dtype),
            pltpu.SemaphoreType.DMA((blocks,)),
        ]
    return pl.pallas_call(
        kernel,
        out_shape=[jax.ShapeDtypeStruct((len(s), tokens, width), t) for s, t in groups],
        in_specs=specs,
        out_specs=[vmem()] * len(groups),
        scratch_shapes=scratch,
        compiler_params=pltpu.CompilerParams(vmem_limit_bytes=10 * MIB),
        cost_estimate=pl.CostEstimate(
            flops=2 * tokens * depth * width * blocks,
            bytes_accessed=2 * depth * width * blocks,
            transcendentals=0,
        ),
    )(*operands)


def rotary_tables(tokens):
    half = HEAD // 2
    frequency = 500000.0 ** (-(jnp.arange(half, dtype=jnp.float32) * 2.0) / HEAD)
    angles = jnp.arange(tokens, dtype=jnp.float32)[:, None] * frequency[None, :]
    cosine, sine = jnp.cos(angles), jnp.sin(angles)
    return jnp.concatenate([cosine, cosine], axis=1), jnp.concatenate([-sine, sine], axis=1)


def per_device(n, act, norm_gain, wq, wk, wv, wo):
    tokens, width = act.shape
    me = lax.axis_index("wide")
    bits = [1 << i for i in range(n.bit_length() - 1)]
    ways = (bits[1], bits[2])
    diagonal = bits[1] ^ bits[2]
    low, z_ways = combos(bits[3:-2]), (bits[-2], bits[-1])
    f32, bf16 = jnp.float32, jnp.bfloat16

    def swap(x, offset):
        return lax.ppermute(x, "wide", [(i, i ^ offset) for i in range(n)])

    def by_core(x, pair, step):
        return lax.ppermute(x, "wide", [(i, i ^ pair[(step + (i & CORE)) % 2]) for i in range(n)])

    def turn(x, step):
        return by_core(x, ways, step)

    def along(x, step):
        return by_core(x, z_ways, step)

    def steps(pair):
        first = jnp.where((me & CORE) == 0, pair[0], pair[1])
        return [jnp.zeros_like(me), first, first ^ pair[0] ^ pair[1]]

    where = jnp.stack([me ^ i ^ j for i in steps(ways) for j in steps(z_ways)]).astype(jnp.int32)
    gain = norm_gain.reshape(1, -1)

    def across(symbols):
        flip = (0, 2, 1)
        return [(const ^ CORE, (flip[i], flip[j])) for const, (i, j) in symbols]

    near = [(o, j) for j in (0, 1) for o in low]
    far = [(o, 2) for o in low] + [(o ^ z_ways[0] ^ z_ways[1], 0) for o in low]

    def after(x, *others):
        return lax.optimization_barrier((x, *others))[0]

    shared = (n // KVH).bit_length() - 1
    raw = act
    kv_send, kv_keep, act, gain = kv_terms(shared, where, act, gain, wk, wv)

    def symbols_of(offsets):
        square = [(0, 0), (0, 1), (0, 2), (diagonal, 0)]
        return [[(const ^ o, (i, j)) for o, j in offsets] for const, i in square]

    def other(pieces):
        return [(swap(x, CORE), across(symbols)) for x, symbols in pieces]

    def order(offsets):
        home, one, two, corner = symbols_of(offsets)
        return [corner + one, two, home]

    def columns_of(offsets):
        own = sum(order(offsets), [])
        return own + across(own)

    def halved(kv, send, way):
        half = kv.shape[0] // 2
        return kv[half:] + send(kv[:half].astype(bf16), way).astype(f32)

    kv = halved(kv_keep + swap(kv_send, CORE), swap, bits[shared])
    home, mid = near[: len(low)], near[len(low) :]
    row = jnp.stack([act] + [swap(raw, o) for o in low[1:]])
    groups, kept = [], None
    for offsets in (home, mid, far):
        if offsets is mid:
            kept, row, kv = lax.optimization_barrier((row, along(row, 0), kv))
            row, kv = lax.optimization_barrier((row, kv, groups[0][1][0]))[:2]
        elif offsets is far:
            half = kv[: kv.shape[0] // 2].astype(bf16)
            row = jnp.concatenate([kept, row])
            k = min(row.shape[0], half.shape[0])
            extra = jnp.zeros((row.shape[0], *half.shape[1:]), bf16).at[:k].set(half[:k])
            got = along(jnp.concatenate([row, extra], axis=2), 1)
            got = after(got, groups[1][2][0])
            row = got[:, :, :width]
            kv = kv[kv.shape[0] // 2 :] + got[:k, :, width:].astype(f32)
        side = turn(row, 0)
        if offsets is far:
            kv = halved(kv, along, 0)
            blocks, far_symbols = fetched(after(where, row), wo, width, columns_of(far))
            side, kv, blocks = lax.optimization_barrier((side, kv, blocks))
            far_held = (blocks, far_symbols)
        elif offsets is mid:
            side = after(side, groups[0][2][0])
        both = turn(jnp.concatenate([row, side]), 1)
        at = symbols_of(offsets)
        groups.append([(row, at[0]), (side, at[1]), (both, at[2] + at[3])])
    early, last = groups[0] + groups[1], groups[2]
    partners = [swap(kv[0].astype(bf16), o) for o in combos(bits[1:shared])[1:]]

    call = functools.partial(query_call, where, gain, weight=wq)
    carry = call(early + other(early))
    carry = call(last[:2] + other(last[:2]), carry=carry)
    both, *carry = lax.optimization_barrier((last[2][0], *carry))
    both = [(both, last[2][1])]
    total = kv[0]
    for x in partners:
        total = total + after(x, carry[0]).astype(f32)
    final = other(both)
    carry = call(both, carry=carry)
    (attended,) = call(
        final, carry=carry, extra=(total, swap(total, CORE), *rotary_tables(tokens))
    )

    def round_square(first, two, home):
        got = turn(first, 0)
        k = got.shape[0] // 2
        two = added_up(*two, got[:k]).astype(bf16)
        return [*home, got[k:]], two

    def added_up(home, *arrived):
        for x in arrived:
            home = home + x.astype(f32)
        return home

    def theirs(symbols):
        return [(across(s), bf16) for s in symbols]

    def ours(symbols):
        return [(s, f32) for s in symbols]

    def paired(own, sent):
        return [(x, swap(y, CORE)) for x, y in zip(own, sent)]

    project = functools.partial(output_call, held=far_held, width=width)
    sent = project(attended, groups=theirs(order(far)[:1]))
    own = project(after(attended, *sent), groups=ours(order(far)))
    first = added_up(own[0], swap(sent[0], CORE)).astype(bf16)
    sent = project(after(attended, first), groups=theirs(order(far)[1:]))
    far_home, far_two = round_square(first, *paired(own[1:], sent))
    far_sum = added_up(*far_home, turn(far_two, 1))
    project = functools.partial(output_call, width=width, where=where, weight=wo)
    sent = project(after(attended, sent[-1]), groups=theirs(order(near)))
    own = project(after(attended, sent[0]), groups=ours(order(near)))
    pairs = paired(own, sent)
    first = added_up(after(pairs[0][0], far_two), pairs[0][1]).astype(bf16)
    near_home, near_two = round_square(first, *pairs[1:])
    far_got = along(far_sum.astype(bf16), 1)
    k = len(low)
    got = [turn(near_two[k:], 1), turn(near_two[:k], 1)]
    near_sum = added_up(*[x[k:] for x in near_home], got[0], far_got[k:])
    home_sum = added_up(*[x[:k] for x in near_home], got[1], far_got[:k])
    home_sum = added_up(home_sum, along(near_sum.astype(bf16), 0))
    out = added_up(home_sum[0], *[swap(home_sum[i].astype(bf16), o) for i, o in enumerate(low) if o])
    return out.astype(bf16)


def solution(mesh):
    return jax.shard_map(
        functools.partial(per_device, mesh.shape["wide"]),
        mesh=mesh,
        in_specs=(
            P("groups", "wide"),
            P(),
            P(None, "wide"),
            P("wide", None),
            P("wide", None),
            P("wide", None),
        ),
        out_specs=P("groups", "wide"),
        check_vma=False,
    )
```

```python
import functools

import jax
import jax.numpy as jnp
from jax import lax
from jax.experimental import pallas as pl
from jax.experimental.pallas import tpu as pltpu
from jax.sharding import PartitionSpec as P

HEADS = 128
KVH = 8
HEAD = 128
LANE = 128
EPS = 1e-05
MIB = 1 << 20
CORE = 1
KV_WEIGHT = 16


def combos(bits):
    out = [0]
    for b in bits:
        out = out + [o ^ b for o in out]
    return out


def vmem():
    return pl.BlockSpec(memory_space=pltpu.VMEM)


def smem():
    return pl.BlockSpec(memory_space=pltpu.SMEM)


def hbm():
    return pl.BlockSpec(memory_space=pltpu.HBM)


def in_hbm(x):
    return pltpu.with_memory_space_constraint(x, pltpu.HBM)


def device(where, symbol):
    const, (i, j) = symbol
    return where[3 * i + j] ^ const


def dot(a, b):
    return jnp.dot(a, b, preferred_element_type=jnp.float32)


def fetch_kernel(symbols, width, where, source, target, sems):
    copies = []
    for i, (const, pick) in enumerate(symbols):
        start = pl.multiple_of((device(where, (const, pick))) * width, LANE)
        copy = pltpu.make_async_copy(
            source.at[:, pl.ds(start, width)], target.at[i], sems.at[i]
        )
        copy.start()
        copies.append(copy)
    for copy in copies:
        copy.wait()


def fetched(where, weight, width, symbols):
    shape = (len(symbols), weight.shape[0], width)
    blocks = pl.pallas_call(
        functools.partial(fetch_kernel, symbols, width),
        out_shape=jax.ShapeDtypeStruct(shape, weight.dtype),
        in_specs=[smem(), hbm()],
        out_specs=vmem(),
        scratch_shapes=[pltpu.SemaphoreType.DMA((len(symbols),))],
        compiler_params=pltpu.CompilerParams(vmem_limit_bytes=MIB),
        cost_estimate=pl.CostEstimate(
            flops=0, bytes_accessed=4 * shape[0] * shape[1] * shape[2], transcendentals=0
        ),
    )(where, in_hbm(weight))
    return blocks, symbols


def kv_kernel(shared, where, act, gain, wk, wv, send, keep, abuf, gbuf, kbuf, vbuf, sems):
    me = where[0]
    width = act.shape[1]
    own = pl.ds(pl.multiple_of(me * width, LANE), width)
    pairs = [(act, abuf), (gain, gbuf), (wk, kbuf), (wv, vbuf)]
    copies = [pltpu.make_async_copy(x, y, sems.at[i]) for i, (x, y) in enumerate(pairs)]
    for c in copies:
        c.start()
    for c in copies:
        c.wait()
    scaled = (abuf[...].astype(jnp.float32) * gbuf[:, own]).astype(jnp.bfloat16)
    k, v = dot(scaled, kbuf[...]), dot(scaled, vbuf[...])
    core0 = (me & CORE) == 0
    for h in range(KVH):
        off = h ^ (me >> shared)
        low, a, b = off & 1, (off >> 1) & 1, (off >> 2) & 1
        spot_0, spot_1 = 7 - (4 * low + 2 * b + a), 7 - (4 * low + 2 * a + b)
        kh, vh = k[:, h * HEAD : (h + 1) * HEAD], v[:, h * HEAD : (h + 1) * HEAD]
        keep[jnp.where(core0, spot_0, spot_1)] = jnp.where(core0, kh, vh)
        send[jnp.where(core0, spot_1, spot_0)] = jnp.where(core0, vh, kh)


def kv_terms(shared, where, act, gain, wk, wv):
    tokens = act.shape[0]
    return pl.pallas_call(
        functools.partial(kv_kernel, shared),
        out_shape=[jax.ShapeDtypeStruct((KVH, tokens, HEAD), jnp.float32)] * 2
        + [jax.ShapeDtypeStruct(x.shape, x.dtype) for x in (act, gain)],
        in_specs=[smem()] + [hbm()] * 4,
        out_specs=[vmem()] * 4,
        scratch_shapes=[
            pltpu.VMEM(wk.shape, wk.dtype),
            pltpu.VMEM(wv.shape, wv.dtype),
            pltpu.SemaphoreType.DMA((4,)),
        ],
        compiler_params=pltpu.CompilerParams(vmem_limit_bytes=12 * MIB),
        cost_estimate=pl.CostEstimate(
            flops=KV_WEIGHT * 4 * tokens * wk.size,
            bytes_accessed=KV_WEIGHT * 4 * wk.size,
            transcendentals=0,
        ),
    )(where, in_hbm(act), in_hbm(gain), in_hbm(wk), in_hbm(wv))


def attend(queries, k_sum, v_sum, cosine, sine, scale):
    k_rows = (k_sum * scale).astype(jnp.bfloat16).astype(jnp.float32)
    value = (v_sum * scale).astype(jnp.bfloat16)
    tokens, heads = queries.shape[0], queries.shape[1] // HEAD

    def rotate(x, cosine, sine):
        half = HEAD // 2
        turned = jnp.concatenate([x[:, half:], x[:, :half]], axis=1)
        return (x * cosine + turned * sine).astype(jnp.bfloat16)

    def stacked(parts):
        return jnp.concatenate(parts, axis=0)

    key = rotate(k_rows, cosine, sine)
    queries = queries * scale
    rows = stacked([queries[:, h * HEAD : (h + 1) * HEAD] for h in range(heads)])
    query = rotate(rows, stacked([cosine] * heads), stacked([sine] * heads))
    scores = lax.dot_general(
        query, key, (((1,), (1,)), ((), ())), preferred_element_type=jnp.float32
    ) * HEAD ** (-0.5)
    at = lax.broadcasted_iota(jnp.int32, (tokens, tokens), 0)
    seen = at >= lax.broadcasted_iota(jnp.int32, (tokens, tokens), 1)
    bias = jnp.where(seen, 0.0, -jnp.inf)
    scores = scores + stacked([bias] * heads)
    weights = jnp.exp(scores - jnp.max(scores, axis=1, keepdims=True))
    probs = (weights / jnp.sum(weights, axis=1, keepdims=True)).astype(jnp.bfloat16)
    out = dot(probs, value).astype(jnp.bfloat16)
    return jnp.concatenate([out[h * tokens : (h + 1) * tokens] for h in range(heads)], axis=1)


def query_kernel(places, carried, last, *refs):
    refs = list(refs)
    where, gain = refs.pop(0), refs.pop(0)
    pieces = [refs.pop(0) for _ in places]
    weight = refs.pop(0)
    queries = refs.pop(0)[...] if carried else None
    squares = refs.pop(0)[...] if carried else None
    width = pieces[0].shape[2]
    for piece, blocks in zip(pieces, places):
        for block, (const, pick) in enumerate(blocks):
            span = pl.ds(pl.multiple_of((device(where, (const, pick))) * width, LANE), width)
            x = piece[block].astype(jnp.float32)
            for c in range(0, width, LANE):
                square = x[:, c : c + LANE] * x[:, c : c + LANE]
                squares = square if squares is None else squares + square
            term = dot((x * gain[:, span]).astype(jnp.bfloat16), weight[span, :])
            queries = term if queries is None else queries + term
    if last:
        mean = jnp.sum(squares, axis=1, keepdims=True) * (1.0 / gain.shape[1])
        mine, other, cosine, sine, out = refs
        core0 = (where[0] & CORE) == 0
        k_sum = jnp.where(core0, mine[...], other[...])
        v_sum = jnp.where(core0, other[...], mine[...])
        out[...] = attend(
            queries, k_sum, v_sum, cosine[...], sine[...], lax.rsqrt(mean + EPS)
        )
    else:
        refs[0][...] = queries
        refs[1][...] = squares


def query_call(where, gain, pieces, weight, carry=(), extra=()):
    arrays, places = [array for array, _ in pieces], [symbols for _, symbols in pieces]
    tokens, width, columns = *arrays[0].shape[1:], weight.shape[1]
    rows = width * sum(len(p) for p in places)
    if extra:
        out_shape = [jax.ShapeDtypeStruct((tokens, columns), jnp.bfloat16)]
    else:
        out_shape = [
            jax.ShapeDtypeStruct((tokens, columns), jnp.float32),
            jax.ShapeDtypeStruct((tokens, LANE), jnp.float32),
        ]
    count = 2 + len(arrays) + len(carry) + len(extra)
    return pl.pallas_call(
        functools.partial(query_kernel, places, bool(carry), bool(extra)),
        out_shape=out_shape,
        in_specs=[smem()] + [vmem()] * count,
        out_specs=[vmem()] * len(out_shape),
        compiler_params=pltpu.CompilerParams(vmem_limit_bytes=4 * MIB),
        cost_estimate=pl.CostEstimate(
            flops=2 * tokens * columns * rows,
            bytes_accessed=2 * columns * rows,
            transcendentals=0,
        ),
    )(where, gain, *arrays, weight, *carry, *extra)


def output_kernel(groups, attended, weight, *outs):
    left = attended[...]
    for spots, out in zip(groups, outs):
        for block, spot in enumerate(spots):
            out[block] = dot(left, weight[spot]).astype(out.dtype)


def output_fetch_kernel(groups, where, attended, weight, *refs):
    outs, buf, sems = refs[: len(groups)], refs[-2], refs[-1]
    copies = []
    for i, (const, pick) in enumerate(sum(groups, [])):
        width = buf.shape[2]
        start = pl.multiple_of((device(where, (const, pick))) * width, LANE)
        copy = pltpu.make_async_copy(weight.at[:, pl.ds(start, width)], buf.at[i], sems.at[i])
        copy.start()
        copies.append(copy)
    left = attended[...]
    i = 0
    for symbols, out in zip(groups, outs):
        for block in range(len(symbols)):
            copies[i].wait()
            out[block] = dot(left, buf[i]).astype(out.dtype)
            i += 1


def output_call(attended, width, groups, held=None, where=None, weight=None):
    tokens, depth = attended.shape
    blocks = sum(len(s) for s, _ in groups)
    if held is not None:
        kernel = functools.partial(
            output_kernel, [[held[1].index(s) for s in symbols] for symbols, _ in groups]
        )
        operands, specs, scratch = (attended, held[0]), [vmem(), vmem()], []
    else:
        kernel = functools.partial(output_fetch_kernel, [symbols for symbols, _ in groups])
        operands, specs = (where, attended, in_hbm(weight)), [smem(), vmem(), hbm()]
        scratch = [
            pltpu.VMEM((blocks, depth, width), weight.dtype),
            pltpu.SemaphoreType.DMA((blocks,)),
        ]
    return pl.pallas_call(
        kernel,
        out_shape=[jax.ShapeDtypeStruct((len(s), tokens, width), t) for s, t in groups],
        in_specs=specs,
        out_specs=[vmem()] * len(groups),
        scratch_shapes=scratch,
        compiler_params=pltpu.CompilerParams(vmem_limit_bytes=10 * MIB),
        cost_estimate=pl.CostEstimate(
            flops=2 * tokens * depth * width * blocks,
            bytes_accessed=2 * depth * width * blocks,
            transcendentals=0,
        ),
    )(*operands)


def rotary_tables(tokens):
    half = HEAD // 2
    frequency = 500000.0 ** (-(jnp.arange(half, dtype=jnp.float32) * 2.0) / HEAD)
    angles = jnp.arange(tokens, dtype=jnp.float32)[:, None] * frequency[None, :]
    cosine, sine = jnp.cos(angles), jnp.sin(angles)
    return jnp.concatenate([cosine, cosine], axis=1), jnp.concatenate([-sine, sine], axis=1)


def per_device(n, act, norm_gain, wq, wk, wv, wo):
    tokens, width = act.shape
    me = lax.axis_index("wide")
    bits = [1 << i for i in range(n.bit_length() - 1)]
    ways = (bits[1], bits[2])
    diagonal = bits[1] ^ bits[2]
    low, z_ways = combos(bits[3:-2]), (bits[-2], bits[-1])
    f32, bf16 = jnp.float32, jnp.bfloat16

    def swap(x, offset):
        return lax.ppermute(x, "wide", [(i, i ^ offset) for i in range(n)])

    def by_core(x, pair, step):
        return lax.ppermute(x, "wide", [(i, i ^ pair[(step + (i & CORE)) % 2]) for i in range(n)])

    def turn(x, step):
        return by_core(x, ways, step)

    def along(x, step):
        return by_core(x, z_ways, step)

    def steps(pair):
        first = jnp.where((me & CORE) == 0, pair[0], pair[1])
        return [jnp.zeros_like(me), first, first ^ pair[0] ^ pair[1]]

    where = jnp.stack([me ^ i ^ j for i in steps(ways) for j in steps(z_ways)]).astype(jnp.int32)
    gain = norm_gain.reshape(1, -1)

    def across(symbols):
        flip = (0, 2, 1)
        return [(const ^ CORE, (flip[i], flip[j])) for const, (i, j) in symbols]

    near = [(o, j) for j in (0, 1) for o in low]
    far = [(o, 2) for o in low] + [(o ^ z_ways[0] ^ z_ways[1], 0) for o in low]

    def after(x, *others):
        return lax.optimization_barrier((x, *others))[0]

    shared = (n // KVH).bit_length() - 1
    raw = act
    kv_send, kv_keep, act, gain = kv_terms(shared, where, act, gain, wk, wv)

    def symbols_of(offsets):
        square = [(0, 0), (0, 1), (0, 2), (diagonal, 0)]
        return [[(const ^ o, (i, j)) for o, j in offsets] for const, i in square]

    def other(pieces):
        return [(swap(x, CORE), across(symbols)) for x, symbols in pieces]

    def order(offsets):
        home, one, two, corner = symbols_of(offsets)
        return [corner + one, two, home]

    def columns_of(offsets):
        own = sum(order(offsets), [])
        return own + across(own)

    home, mid = near[: len(low)], near[len(low) :]
    own = jnp.stack([act] + [swap(raw, o) for o in low[1:]])
    side = turn(own, 0)
    both = turn(jnp.concatenate([own, side]), 1)
    middle = after(along(own, 0), side)
    last_row = along(jnp.concatenate([own, middle]), 1)
    middle_side = after(turn(middle, 0), both)
    joined = jnp.concatenate([middle, middle_side])
    middle_both = turn(joined, 1)
    last_row = after(last_row, middle_both)
    last_side = turn(last_row, 0)
    blocks, far_symbols = fetched(after(where, last_row), wo, width, columns_of(far))
    last_side, blocks = lax.optimization_barrier((last_side, blocks))
    far_held = (blocks, far_symbols)
    last_both = turn(jnp.concatenate([last_row, last_side]), 1)

    kv = kv_keep + swap(kv_send, CORE)
    for send, way, then in (
        (swap, bits[shared], middle),
        (along, 1, middle_side),
        (along, 0, last_side),
    ):
        half = kv.shape[0] // 2
        got = after(send(kv[:half].astype(bf16), way), then)
        kv = kv[half:] + got.astype(f32)

    def pieces_of(row, side, both, offsets):
        at = symbols_of(offsets)
        return [(row, at[0]), (side, at[1]), (both, at[2] + at[3])]

    early = pieces_of(own, side, both, home) + pieces_of(middle, middle_side, middle_both, mid)
    last = pieces_of(last_row, last_side, last_both, far)
    partners = [swap(kv[0].astype(bf16), o) for o in combos(bits[1:shared])[1:]]

    call = functools.partial(query_call, where, gain, weight=wq)
    carry = call(early + other(early))
    carry = call(last[:2] + other(last[:2]), carry=carry)
    both, *carry = lax.optimization_barrier((last[2][0], *carry))
    both = [(both, last[2][1])]
    total = kv[0]
    for x in partners:
        total = total + after(x, carry[0]).astype(f32)
    final = other(both)
    carry = call(both, carry=carry)
    (attended,) = call(
        final, carry=carry, extra=(total, swap(total, CORE), *rotary_tables(tokens))
    )

    def round_square(first, two, home):
        got = turn(first, 0)
        k = got.shape[0] // 2
        two = added_up(*two, got[:k]).astype(bf16)
        return [*home, got[k:]], two

    def added_up(home, *arrived):
        for x in arrived:
            home = home + x.astype(f32)
        return home

    def theirs(symbols):
        return [(across(s), bf16) for s in symbols]

    def ours(symbols):
        return [(s, f32) for s in symbols]

    def paired(own, sent):
        return [(x, swap(y, CORE)) for x, y in zip(own, sent)]

    project = functools.partial(output_call, held=far_held, width=width)
    sent = project(attended, groups=theirs(order(far)[:1]))
    own = project(after(attended, *sent), groups=ours(order(far)))
    first = added_up(own[0], swap(sent[0], CORE)).astype(bf16)
    sent = project(after(attended, first), groups=theirs(order(far)[1:]))
    far_home, far_two = round_square(first, *paired(own[1:], sent))
    far_sum = added_up(*far_home, turn(far_two, 1))
    project = functools.partial(output_call, width=width, where=where, weight=wo)
    sent = project(after(attended, sent[-1]), groups=theirs(order(near)))
    own = project(after(attended, sent[0]), groups=ours(order(near)))
    pairs = paired(own, sent)
    first = added_up(after(pairs[0][0], far_two), pairs[0][1]).astype(bf16)
    near_home, near_two = round_square(first, *pairs[1:])
    far_got = along(far_sum.astype(bf16), 1)
    k = len(low)
    near_sum = added_up(*near_home, turn(near_two, 1), far_got)
    home_sum = added_up(near_sum[:k], along(near_sum[k:].astype(bf16), 0))
    out = added_up(home_sum[0], *[swap(home_sum[i].astype(bf16), o) for i, o in enumerate(low) if o])
    return out.astype(bf16)


def solution(mesh):
    return jax.shard_map(
        functools.partial(per_device, mesh.shape["wide"]),
        mesh=mesh,
        in_specs=(
            P("groups", "wide"),
            P(),
            P(None, "wide"),
            P("wide", None),
            P("wide", None),
            P("wide", None),
        ),
        out_specs=P("groups", "wide"),
        check_vma=False,
    )
```

```python
import functools

import jax
import jax.numpy as jnp
from jax import lax
from jax.experimental import pallas as pl
from jax.experimental.pallas import tpu as pltpu
from jax.sharding import PartitionSpec as P

HEADS = 128
KVH = 8
HEAD = 128
LANE = 128
EPS = 1e-05
MIB = 1 << 20
CORE = 1
KV_WEIGHT = 16


def combos(bits):
    out = [0]
    for b in bits:
        out = out + [o ^ b for o in out]
    return out


def vmem():
    return pl.BlockSpec(memory_space=pltpu.VMEM)


def smem():
    return pl.BlockSpec(memory_space=pltpu.SMEM)


def hbm():
    return pl.BlockSpec(memory_space=pltpu.HBM)


def in_hbm(x):
    return pltpu.with_memory_space_constraint(x, pltpu.HBM)


def device(where, symbol):
    const, (i, j) = symbol
    return where[3 * i + j] ^ const


def dot(a, b):
    return jnp.dot(a, b, preferred_element_type=jnp.float32)


def fetch_kernel(symbols, width, where, source, target, sems):
    copies = []
    for i, (const, pick) in enumerate(symbols):
        start = pl.multiple_of((device(where, (const, pick))) * width, LANE)
        copy = pltpu.make_async_copy(
            source.at[:, pl.ds(start, width)], target.at[i], sems.at[i]
        )
        copy.start()
        copies.append(copy)
    for copy in copies:
        copy.wait()


def fetched(where, weight, width, symbols):
    shape = (len(symbols), weight.shape[0], width)
    blocks = pl.pallas_call(
        functools.partial(fetch_kernel, symbols, width),
        out_shape=jax.ShapeDtypeStruct(shape, weight.dtype),
        in_specs=[smem(), hbm()],
        out_specs=vmem(),
        scratch_shapes=[pltpu.SemaphoreType.DMA((len(symbols),))],
        compiler_params=pltpu.CompilerParams(vmem_limit_bytes=MIB),
        cost_estimate=pl.CostEstimate(
            flops=0, bytes_accessed=4 * shape[0] * shape[1] * shape[2], transcendentals=0
        ),
    )(where, in_hbm(weight))
    return blocks, symbols


def kv_kernel(shared, where, act, gain, wk, wv, send, keep, abuf, gbuf, kbuf, vbuf, sems):
    me = where[0]
    width = act.shape[1]
    own = pl.ds(pl.multiple_of(me * width, LANE), width)
    pairs = [(act, abuf), (gain, gbuf), (wk, kbuf), (wv, vbuf)]
    copies = [pltpu.make_async_copy(x, y, sems.at[i]) for i, (x, y) in enumerate(pairs)]
    for c in copies:
        c.start()
    for c in copies:
        c.wait()
    scaled = (abuf[...].astype(jnp.float32) * gbuf[:, own]).astype(jnp.bfloat16)
    k, v = dot(scaled, kbuf[...]), dot(scaled, vbuf[...])
    core0 = (me & CORE) == 0
    for h in range(KVH):
        off = h ^ (me >> shared)
        low, a, b = off & 1, (off >> 1) & 1, (off >> 2) & 1
        spot_0, spot_1 = 7 - (4 * low + 2 * b + a), 7 - (4 * low + 2 * a + b)
        kh, vh = k[:, h * HEAD : (h + 1) * HEAD], v[:, h * HEAD : (h + 1) * HEAD]
        keep[jnp.where(core0, spot_0, spot_1)] = jnp.where(core0, kh, vh)
        send[jnp.where(core0, spot_1, spot_0)] = jnp.where(core0, vh, kh)


def kv_terms(shared, where, act, gain, wk, wv):
    tokens = act.shape[0]
    return pl.pallas_call(
        functools.partial(kv_kernel, shared),
        out_shape=[jax.ShapeDtypeStruct((KVH, tokens, HEAD), jnp.float32)] * 2
        + [jax.ShapeDtypeStruct(x.shape, x.dtype) for x in (act, gain)],
        in_specs=[smem()] + [hbm()] * 4,
        out_specs=[vmem()] * 4,
        scratch_shapes=[
            pltpu.VMEM(wk.shape, wk.dtype),
            pltpu.VMEM(wv.shape, wv.dtype),
            pltpu.SemaphoreType.DMA((4,)),
        ],
        compiler_params=pltpu.CompilerParams(vmem_limit_bytes=12 * MIB),
        cost_estimate=pl.CostEstimate(
            flops=KV_WEIGHT * 4 * tokens * wk.size,
            bytes_accessed=KV_WEIGHT * 4 * wk.size,
            transcendentals=0,
        ),
    )(where, in_hbm(act), in_hbm(gain), in_hbm(wk), in_hbm(wv))


def attend(queries, k_sum, v_sum, cosine, sine, scale):
    k_rows = (k_sum * scale).astype(jnp.bfloat16).astype(jnp.float32)
    value = (v_sum * scale).astype(jnp.bfloat16)
    tokens, heads = queries.shape[0], queries.shape[1] // HEAD

    def rotate(x, cosine, sine):
        half = HEAD // 2
        turned = jnp.concatenate([x[:, half:], x[:, :half]], axis=1)
        return (x * cosine + turned * sine).astype(jnp.bfloat16)

    def stacked(parts):
        return jnp.concatenate(parts, axis=0)

    key = rotate(k_rows, cosine, sine)
    queries = queries * scale
    rows = stacked([queries[:, h * HEAD : (h + 1) * HEAD] for h in range(heads)])
    query = rotate(rows, stacked([cosine] * heads), stacked([sine] * heads))
    scores = lax.dot_general(
        query, key, (((1,), (1,)), ((), ())), preferred_element_type=jnp.float32
    ) * HEAD ** (-0.5)
    at = lax.broadcasted_iota(jnp.int32, (tokens, tokens), 0)
    seen = at >= lax.broadcasted_iota(jnp.int32, (tokens, tokens), 1)
    bias = jnp.where(seen, 0.0, -jnp.inf)
    scores = scores + stacked([bias] * heads)
    weights = jnp.exp(scores - jnp.max(scores, axis=1, keepdims=True))
    probs = (weights / jnp.sum(weights, axis=1, keepdims=True)).astype(jnp.bfloat16)
    out = dot(probs, value).astype(jnp.bfloat16)
    return jnp.concatenate([out[h * tokens : (h + 1) * tokens] for h in range(heads)], axis=1)


def query_kernel(places, carried, last, *refs):
    refs = list(refs)
    where, gain = refs.pop(0), refs.pop(0)
    pieces = [refs.pop(0) for _ in places]
    weight = refs.pop(0)
    queries = refs.pop(0)[...] if carried else None
    squares = refs.pop(0)[...] if carried else None
    width = pieces[0].shape[2]
    for piece, blocks in zip(pieces, places):
        for block, (const, pick) in enumerate(blocks):
            span = pl.ds(pl.multiple_of((device(where, (const, pick))) * width, LANE), width)
            x = piece[block].astype(jnp.float32)
            for c in range(0, width, LANE):
                square = x[:, c : c + LANE] * x[:, c : c + LANE]
                squares = square if squares is None else squares + square
            term = dot((x * gain[:, span]).astype(jnp.bfloat16), weight[span, :])
            queries = term if queries is None else queries + term
    if last:
        mean = jnp.sum(squares, axis=1, keepdims=True) * (1.0 / gain.shape[1])
        mine, other, cosine, sine, out = refs
        core0 = (where[0] & CORE) == 0
        k_sum = jnp.where(core0, mine[...], other[...])
        v_sum = jnp.where(core0, other[...], mine[...])
        out[...] = attend(
            queries, k_sum, v_sum, cosine[...], sine[...], lax.rsqrt(mean + EPS)
        )
    else:
        refs[0][...] = queries
        refs[1][...] = squares


def query_call(where, gain, pieces, weight, carry=(), extra=()):
    arrays, places = [array for array, _ in pieces], [symbols for _, symbols in pieces]
    tokens, width, columns = *arrays[0].shape[1:], weight.shape[1]
    rows = width * sum(len(p) for p in places)
    if extra:
        out_shape = [jax.ShapeDtypeStruct((tokens, columns), jnp.bfloat16)]
    else:
        out_shape = [
            jax.ShapeDtypeStruct((tokens, columns), jnp.float32),
            jax.ShapeDtypeStruct((tokens, LANE), jnp.float32),
        ]
    count = 2 + len(arrays) + len(carry) + len(extra)
    return pl.pallas_call(
        functools.partial(query_kernel, places, bool(carry), bool(extra)),
        out_shape=out_shape,
        in_specs=[smem()] + [vmem()] * count,
        out_specs=[vmem()] * len(out_shape),
        compiler_params=pltpu.CompilerParams(vmem_limit_bytes=4 * MIB),
        cost_estimate=pl.CostEstimate(
            flops=2 * tokens * columns * rows,
            bytes_accessed=2 * columns * rows,
            transcendentals=0,
        ),
    )(where, gain, *arrays, weight, *carry, *extra)


def output_kernel(groups, attended, weight, *outs):
    left = attended[...]
    for spots, out in zip(groups, outs):
        for block, spot in enumerate(spots):
            out[block] = dot(left, weight[spot]).astype(out.dtype)


def output_fetch_kernel(groups, where, attended, weight, *refs):
    outs, buf, sems = refs[: len(groups)], refs[-2], refs[-1]
    copies = []
    for i, (const, pick) in enumerate(sum(groups, [])):
        width = buf.shape[2]
        start = pl.multiple_of((device(where, (const, pick))) * width, LANE)
        copy = pltpu.make_async_copy(weight.at[:, pl.ds(start, width)], buf.at[i], sems.at[i])
        copy.start()
        copies.append(copy)
    left = attended[...]
    i = 0
    for symbols, out in zip(groups, outs):
        for block in range(len(symbols)):
            copies[i].wait()
            out[block] = dot(left, buf[i]).astype(out.dtype)
            i += 1


def output_call(attended, width, groups, held=None, where=None, weight=None):
    tokens, depth = attended.shape
    blocks = sum(len(s) for s, _ in groups)
    if held is not None:
        kernel = functools.partial(
            output_kernel, [[held[1].index(s) for s in symbols] for symbols, _ in groups]
        )
        operands, specs, scratch = (attended, held[0]), [vmem(), vmem()], []
    else:
        kernel = functools.partial(output_fetch_kernel, [symbols for symbols, _ in groups])
        operands, specs = (where, attended, in_hbm(weight)), [smem(), vmem(), hbm()]
        scratch = [
            pltpu.VMEM((blocks, depth, width), weight.dtype),
            pltpu.SemaphoreType.DMA((blocks,)),
        ]
    return pl.pallas_call(
        kernel,
        out_shape=[jax.ShapeDtypeStruct((len(s), tokens, width), t) for s, t in groups],
        in_specs=specs,
        out_specs=[vmem()] * len(groups),
        scratch_shapes=scratch,
        compiler_params=pltpu.CompilerParams(vmem_limit_bytes=10 * MIB),
        cost_estimate=pl.CostEstimate(
            flops=2 * tokens * depth * width * blocks,
            bytes_accessed=2 * depth * width * blocks,
            transcendentals=0,
        ),
    )(*operands)


def rotary_tables(tokens):
    half = HEAD // 2
    frequency = 500000.0 ** (-(jnp.arange(half, dtype=jnp.float32) * 2.0) / HEAD)
    angles = jnp.arange(tokens, dtype=jnp.float32)[:, None] * frequency[None, :]
    cosine, sine = jnp.cos(angles), jnp.sin(angles)
    return jnp.concatenate([cosine, cosine], axis=1), jnp.concatenate([-sine, sine], axis=1)


def per_device(n, act, norm_gain, wq, wk, wv, wo):
    tokens, width = act.shape
    me = lax.axis_index("wide")
    bits = [1 << i for i in range(n.bit_length() - 1)]
    ways = (bits[1], bits[2])
    diagonal = bits[1] ^ bits[2]
    low, z_ways = combos(bits[3:-2]), (bits[-2], bits[-1])
    f32, bf16 = jnp.float32, jnp.bfloat16

    def swap(x, offset):
        return lax.ppermute(x, "wide", [(i, i ^ offset) for i in range(n)])

    def by_core(x, pair, step):
        return lax.ppermute(x, "wide", [(i, i ^ pair[(step + (i & CORE)) % 2]) for i in range(n)])

    def turn(x, step):
        return by_core(x, ways, step)

    def along(x, step):
        return by_core(x, z_ways, step)

    def steps(pair):
        first = jnp.where((me & CORE) == 0, pair[0], pair[1])
        return [jnp.zeros_like(me), first, first ^ pair[0] ^ pair[1]]

    where = jnp.stack([me ^ i ^ j for i in steps(ways) for j in steps(z_ways)]).astype(jnp.int32)
    gain = norm_gain.reshape(1, -1)

    def across(symbols):
        flip = (0, 2, 1)
        return [(const ^ CORE, (flip[i], flip[j])) for const, (i, j) in symbols]

    near = [(o, j) for j in (0, 1) for o in low]
    far = [(o, 2) for o in low] + [(o ^ z_ways[0] ^ z_ways[1], 0) for o in low]

    def after(x, *others):
        return lax.optimization_barrier((x, *others))[0]

    shared = (n // KVH).bit_length() - 1
    raw = act
    kv_send, kv_keep, act, gain = kv_terms(shared, where, act, gain, wk, wv)

    def symbols_of(offsets):
        square = [(0, 0), (0, 1), (0, 2), (diagonal, 0)]
        return [[(const ^ o, (i, j)) for o, j in offsets] for const, i in square]

    def other(pieces):
        return [(swap(x, CORE), across(symbols)) for x, symbols in pieces]

    def order(offsets):
        home, one, two, corner = symbols_of(offsets)
        return [corner + one, two, home]

    def columns_of(offsets):
        own = sum(order(offsets), [])
        return own + across(own)

    def halved(kv, send, way):
        half = kv.shape[0] // 2
        return kv[half:] + send(kv[:half].astype(bf16), way).astype(f32)

    kv = halved(kv_keep + swap(kv_send, CORE), swap, bits[shared])
    row = jnp.stack([act] + [swap(raw, o) for o in low[1:]])
    row = jnp.concatenate([row, along(row, 0)])
    groups = []
    for offsets in (near, far):
        if offsets is far:
            half = kv[: kv.shape[0] // 2].astype(bf16)
            k = min(row.shape[0], half.shape[0])
            extra = jnp.zeros((row.shape[0], *half.shape[1:]), bf16).at[:k].set(half[:k])
            got = along(jnp.concatenate([row, extra], axis=2), 1)
            row = got[:, :, :width]
            kv = kv[kv.shape[0] // 2 :] + got[:k, :, width:].astype(f32)
            side = turn(row, 0)
            kv = halved(kv, along, 0)
            blocks, far_symbols = fetched(after(where, row), wo, width, columns_of(far))
            side, kv, blocks = lax.optimization_barrier((side, kv, blocks))
            far_held = (blocks, far_symbols)
        else:
            side = turn(row, 0)
        both = turn(jnp.concatenate([row, side]), 1)
        at = symbols_of(offsets)
        groups.append([(row, at[0]), (side, at[1]), (both, at[2] + at[3])])
    early, last = groups
    early[2] = (after(early[2][0], blocks), early[2][1])
    partners = [swap(kv[0].astype(bf16), o) for o in combos(bits[1:shared])[1:]]

    call = functools.partial(query_call, where, gain, weight=wq)
    carry = call(early + other(early))
    carry = call(last[:2] + other(last[:2]), carry=carry)
    both, *carry = lax.optimization_barrier((last[2][0], *carry))
    both = [(both, last[2][1])]
    total = kv[0]
    for x in partners:
        total = total + after(x, carry[0]).astype(f32)
    final = other(both)
    carry = call(both, carry=carry)
    (attended,) = call(
        final, carry=carry, extra=(total, swap(total, CORE), *rotary_tables(tokens))
    )

    def round_square(first, two, home):
        got = turn(first, 0)
        k = got.shape[0] // 2
        two = added_up(*two, got[:k]).astype(bf16)
        return [*home, got[k:]], two

    def added_up(home, *arrived):
        for x in arrived:
            home = home + x.astype(f32)
        return home

    def theirs(symbols):
        return [(across(s), bf16) for s in symbols]

    def ours(symbols):
        return [(s, f32) for s in symbols]

    def paired(own, sent):
        return [(x, swap(y, CORE)) for x, y in zip(own, sent)]

    project = functools.partial(output_call, held=far_held, width=width)
    sent = project(attended, groups=theirs(order(far)[:1]))
    own = project(after(attended, *sent), groups=ours(order(far)))
    first = added_up(own[0], swap(sent[0], CORE)).astype(bf16)
    sent = project(after(attended, first), groups=theirs(order(far)[1:]))
    far_home, far_two = round_square(first, *paired(own[1:], sent))
    far_sum = added_up(*far_home, turn(far_two, 1))
    project = functools.partial(output_call, width=width, where=where, weight=wo)
    sent = project(after(attended, sent[-1]), groups=theirs(order(near)))
    own = project(after(attended, sent[0]), groups=ours(order(near)))
    pairs = paired(own, sent)
    first = added_up(after(pairs[0][0], far_two), pairs[0][1]).astype(bf16)
    near_home, near_two = round_square(first, *pairs[1:])
    k = len(low)
    far_sum = added_up(far_sum[:k], along(far_sum[k:].astype(bf16), 0))
    far_got = along(far_sum.astype(bf16), 1)
    near_sum = added_up(*near_home, turn(near_two, 1))
    home_sum = added_up(near_sum[:k], along(near_sum[k:].astype(bf16), 0), far_got)
    out = added_up(home_sum[0], *[swap(home_sum[i].astype(bf16), o) for i, o in enumerate(low) if o])
    return out.astype(bf16)


def solution(mesh):
    return jax.shard_map(
        functools.partial(per_device, mesh.shape["wide"]),
        mesh=mesh,
        in_specs=(
            P("groups", "wide"),
            P(),
            P(None, "wide"),
            P("wide", None),
            P("wide", None),
            P("wide", None),
        ),
        out_specs=P("groups", "wide"),
        check_vma=False,
    )
```

```python
import functools

import jax
import jax.numpy as jnp
from jax import lax
from jax.experimental import pallas as pl
from jax.experimental.pallas import tpu as pltpu
from jax.sharding import PartitionSpec as P

HEADS = 128
KVH = 8
HEAD = 128
LANE = 128
EPS = 1e-05
MIB = 1 << 20
CORE = 1
KV_WEIGHT = 16


def combos(bits):
    out = [0]
    for b in bits:
        out = out + [o ^ b for o in out]
    return out


def vmem():
    return pl.BlockSpec(memory_space=pltpu.VMEM)


def smem():
    return pl.BlockSpec(memory_space=pltpu.SMEM)


def hbm():
    return pl.BlockSpec(memory_space=pltpu.HBM)


def in_hbm(x):
    return pltpu.with_memory_space_constraint(x, pltpu.HBM)


def device(where, symbol):
    const, (i, j) = symbol
    return where[3 * i + j] ^ const


def dot(a, b):
    return jnp.dot(a, b, preferred_element_type=jnp.float32)


def fetch_kernel(symbols, width, where, source, target, sems):
    copies = []
    for i, (const, pick) in enumerate(symbols):
        start = pl.multiple_of((device(where, (const, pick))) * width, LANE)
        copy = pltpu.make_async_copy(
            source.at[:, pl.ds(start, width)], target.at[i], sems.at[i]
        )
        copy.start()
        copies.append(copy)
    for copy in copies:
        copy.wait()


def fetched(where, weight, width, symbols):
    shape = (len(symbols), weight.shape[0], width)
    blocks = pl.pallas_call(
        functools.partial(fetch_kernel, symbols, width),
        out_shape=jax.ShapeDtypeStruct(shape, weight.dtype),
        in_specs=[smem(), hbm()],
        out_specs=vmem(),
        scratch_shapes=[pltpu.SemaphoreType.DMA((len(symbols),))],
        compiler_params=pltpu.CompilerParams(vmem_limit_bytes=MIB),
        cost_estimate=pl.CostEstimate(
            flops=0, bytes_accessed=4 * shape[0] * shape[1] * shape[2], transcendentals=0
        ),
    )(where, in_hbm(weight))
    return blocks, symbols


def kv_kernel(shared, where, act, gain, wk, wv, send, keep, abuf, gbuf, kbuf, vbuf, sems):
    me = where[0]
    width = act.shape[1]
    own = pl.ds(pl.multiple_of(me * width, LANE), width)
    pairs = [(act, abuf), (gain, gbuf), (wk, kbuf), (wv, vbuf)]
    copies = [pltpu.make_async_copy(x, y, sems.at[i]) for i, (x, y) in enumerate(pairs)]
    for c in copies:
        c.start()
    copies[0].wait()
    copies[1].wait()
    scaled = (abuf[...].astype(jnp.float32) * gbuf[:, own]).astype(jnp.bfloat16)
    copies[2].wait()
    k = dot(scaled, kbuf[...])
    copies[3].wait()
    v = dot(scaled, vbuf[...])
    core0 = (me & CORE) == 0
    for h in range(KVH):
        off = h ^ (me >> shared)
        low, a, b = off & 1, (off >> 1) & 1, (off >> 2) & 1
        spot_0, spot_1 = 7 - (4 * low + 2 * b + a), 7 - (4 * low + 2 * a + b)
        kh, vh = k[:, h * HEAD : (h + 1) * HEAD], v[:, h * HEAD : (h + 1) * HEAD]
        keep[jnp.where(core0, spot_0, spot_1)] = jnp.where(core0, kh, vh)
        send[jnp.where(core0, spot_1, spot_0)] = jnp.where(core0, vh, kh)


def kv_terms(shared, where, act, gain, wk, wv):
    tokens = act.shape[0]
    return pl.pallas_call(
        functools.partial(kv_kernel, shared),
        out_shape=[jax.ShapeDtypeStruct((KVH, tokens, HEAD), jnp.float32)] * 2
        + [jax.ShapeDtypeStruct(x.shape, x.dtype) for x in (act, gain)],
        in_specs=[smem()] + [hbm()] * 4,
        out_specs=[vmem()] * 4,
        scratch_shapes=[
            pltpu.VMEM(wk.shape, wk.dtype),
            pltpu.VMEM(wv.shape, wv.dtype),
            pltpu.SemaphoreType.DMA((4,)),
        ],
        compiler_params=pltpu.CompilerParams(vmem_limit_bytes=12 * MIB),
        cost_estimate=pl.CostEstimate(
            flops=KV_WEIGHT * 4 * tokens * wk.size,
            bytes_accessed=KV_WEIGHT * 4 * wk.size,
            transcendentals=0,
        ),
    )(where, in_hbm(act), in_hbm(gain), in_hbm(wk), in_hbm(wv))


def attend(queries, k_sum, v_sum, cosine, sine, scale):
    k_rows = (k_sum * scale).astype(jnp.bfloat16).astype(jnp.float32)
    value = (v_sum * scale).astype(jnp.bfloat16)
    tokens, heads = queries.shape[0], queries.shape[1] // HEAD

    def rotate(x, cosine, sine):
        half = HEAD // 2
        turned = jnp.concatenate([x[:, half:], x[:, :half]], axis=1)
        return (x * cosine + turned * sine).astype(jnp.bfloat16)

    def stacked(parts):
        return jnp.concatenate(parts, axis=0)

    key = rotate(k_rows, cosine, sine)
    queries = queries * scale
    rows = stacked([queries[:, h * HEAD : (h + 1) * HEAD] for h in range(heads)])
    query = rotate(rows, stacked([cosine] * heads), stacked([sine] * heads))
    scores = lax.dot_general(
        query, key, (((1,), (1,)), ((), ())), preferred_element_type=jnp.float32
    ) * HEAD ** (-0.5)
    at = lax.broadcasted_iota(jnp.int32, (tokens, tokens), 0)
    seen = at >= lax.broadcasted_iota(jnp.int32, (tokens, tokens), 1)
    bias = jnp.where(seen, 0.0, -jnp.inf)
    scores = scores + stacked([bias] * heads)
    weights = jnp.exp(scores - jnp.max(scores, axis=1, keepdims=True))
    probs = (weights / jnp.sum(weights, axis=1, keepdims=True)).astype(jnp.bfloat16)
    out = dot(probs, value).astype(jnp.bfloat16)
    return jnp.concatenate([out[h * tokens : (h + 1) * tokens] for h in range(heads)], axis=1)


def query_kernel(places, carried, last, *refs):
    refs = list(refs)
    where, gain = refs.pop(0), refs.pop(0)
    pieces = [refs.pop(0) for _ in places]
    weight = refs.pop(0)
    queries = refs.pop(0)[...] if carried else None
    squares = refs.pop(0)[...] if carried else None
    width = pieces[0].shape[2]
    for piece, blocks in zip(pieces, places):
        for block, (const, pick) in enumerate(blocks):
            span = pl.ds(pl.multiple_of((device(where, (const, pick))) * width, LANE), width)
            x = piece[block].astype(jnp.float32)
            for c in range(0, width, LANE):
                square = x[:, c : c + LANE] * x[:, c : c + LANE]
                squares = square if squares is None else squares + square
            term = dot((x * gain[:, span]).astype(jnp.bfloat16), weight[span, :])
            queries = term if queries is None else queries + term
    if last:
        mean = jnp.sum(squares, axis=1, keepdims=True) * (1.0 / gain.shape[1])
        mine, other, cosine, sine, out = refs
        core0 = (where[0] & CORE) == 0
        k_sum = jnp.where(core0, mine[...], other[...])
        v_sum = jnp.where(core0, other[...], mine[...])
        out[...] = attend(
            queries, k_sum, v_sum, cosine[...], sine[...], lax.rsqrt(mean + EPS)
        )
    else:
        refs[0][...] = queries
        refs[1][...] = squares


def query_call(where, gain, pieces, weight, carry=(), extra=()):
    arrays, places = [array for array, _ in pieces], [symbols for _, symbols in pieces]
    tokens, width, columns = *arrays[0].shape[1:], weight.shape[1]
    rows = width * sum(len(p) for p in places)
    if extra:
        out_shape = [jax.ShapeDtypeStruct((tokens, columns), jnp.bfloat16)]
    else:
        out_shape = [
            jax.ShapeDtypeStruct((tokens, columns), jnp.float32),
            jax.ShapeDtypeStruct((tokens, LANE), jnp.float32),
        ]
    count = 2 + len(arrays) + len(carry) + len(extra)
    return pl.pallas_call(
        functools.partial(query_kernel, places, bool(carry), bool(extra)),
        out_shape=out_shape,
        in_specs=[smem()] + [vmem()] * count,
        out_specs=[vmem()] * len(out_shape),
        compiler_params=pltpu.CompilerParams(vmem_limit_bytes=4 * MIB),
        cost_estimate=pl.CostEstimate(
            flops=2 * tokens * columns * rows,
            bytes_accessed=2 * columns * rows,
            transcendentals=0,
        ),
    )(where, gain, *arrays, weight, *carry, *extra)


def output_kernel(groups, attended, weight, *outs):
    left = attended[...]
    for spots, out in zip(groups, outs):
        for block, spot in enumerate(spots):
            out[block] = dot(left, weight[spot]).astype(out.dtype)


def output_call(attended, width, groups, held):
    weight, order = held
    tokens, depth = attended.shape
    spots = [[order.index(s) for s in symbols] for symbols, _ in groups]
    columns = width * sum(len(s) for s in spots)
    return pl.pallas_call(
        functools.partial(output_kernel, spots),
        out_shape=[jax.ShapeDtypeStruct((len(s), tokens, width), t) for s, t in groups],
        in_specs=[vmem(), vmem()],
        out_specs=[vmem()] * len(groups),
        compiler_params=pltpu.CompilerParams(vmem_limit_bytes=4 * MIB),
        cost_estimate=pl.CostEstimate(
            flops=2 * tokens * depth * columns,
            bytes_accessed=2 * depth * columns,
            transcendentals=0,
        ),
    )(attended, weight)


def rotary_tables(tokens):
    half = HEAD // 2
    frequency = 500000.0 ** (-(jnp.arange(half, dtype=jnp.float32) * 2.0) / HEAD)
    angles = jnp.arange(tokens, dtype=jnp.float32)[:, None] * frequency[None, :]
    cosine, sine = jnp.cos(angles), jnp.sin(angles)
    return jnp.concatenate([cosine, cosine], axis=1), jnp.concatenate([-sine, sine], axis=1)


def per_device(n, act, norm_gain, wq, wk, wv, wo):
    tokens, width = act.shape
    me = lax.axis_index("wide")
    bits = [1 << i for i in range(n.bit_length() - 1)]
    ways = (bits[1], bits[2])
    diagonal = bits[1] ^ bits[2]
    low, z_ways = combos(bits[3:-2]), (bits[-2], bits[-1])
    f32, bf16 = jnp.float32, jnp.bfloat16

    def swap(x, offset):
        return lax.ppermute(x, "wide", [(i, i ^ offset) for i in range(n)])

    def by_core(x, pair, step):
        return lax.ppermute(x, "wide", [(i, i ^ pair[(step + (i & CORE)) % 2]) for i in range(n)])

    def turn(x, step):
        return by_core(x, ways, step)

    def along(x, step):
        return by_core(x, z_ways, step)

    def steps(pair):
        first = jnp.where((me & CORE) == 0, pair[0], pair[1])
        return [jnp.zeros_like(me), first, first ^ pair[0] ^ pair[1]]

    where = jnp.stack([me ^ i ^ j for i in steps(ways) for j in steps(z_ways)]).astype(jnp.int32)
    gain = norm_gain.reshape(1, -1)

    def across(symbols):
        flip = (0, 2, 1)
        return [(const ^ CORE, (flip[i], flip[j])) for const, (i, j) in symbols]

    near = [(o, j) for j in (0, 1) for o in low]
    far = [(o, 2) for o in low] + [(o ^ z_ways[0] ^ z_ways[1], 0) for o in low]

    def after(x, *others):
        return lax.optimization_barrier((x, *others))[0]

    shared = (n // KVH).bit_length() - 1
    raw = act
    kv_send, kv_keep, act, gain = kv_terms(shared, where, act, gain, wk, wv)

    def symbols_of(offsets):
        square = [(0, 0), (0, 1), (0, 2), (diagonal, 0)]
        return [[(const ^ o, (i, j)) for o, j in offsets] for const, i in square]

    def other(pieces):
        return [(swap(x, CORE), across(symbols)) for x, symbols in pieces]

    def order(offsets):
        home, one, two, corner = symbols_of(offsets)
        return [corner + one, two, home]

    def columns_of(offsets):
        own = sum(order(offsets), [])
        return own + across(own)

    def halved(kv, send, way):
        half = kv.shape[0] // 2
        return kv[half:] + send(kv[:half].astype(bf16), way).astype(f32)

    kv = halved(kv_keep + swap(kv_send, CORE), swap, bits[shared])
    row = jnp.stack([act] + [swap(raw, o) for o in low[1:]])
    row = jnp.concatenate([row, along(row, 0)])
    groups = []
    for offsets in (near, far):
        if offsets is far:
            half = kv[: kv.shape[0] // 2].astype(bf16)
            k = min(row.shape[0], half.shape[0])
            extra = jnp.zeros((row.shape[0], *half.shape[1:]), bf16).at[:k].set(half[:k])
            got = along(jnp.concatenate([row, extra], axis=2), 1)
            near_blocks, near_symbols = fetched(after(where, joined), wo, width, columns_of(near))
            got, near_blocks = lax.optimization_barrier((got, near_blocks))
            near_held = (near_blocks, near_symbols)
            row = got[:, :, :width]
            kv = kv[kv.shape[0] // 2 :] + got[:k, :, width:].astype(f32)
            side = turn(row, 0)
            kv = halved(kv, along, 0)
            blocks, far_symbols = fetched(after(where, row), wo, width, columns_of(far))
            side, kv, blocks = lax.optimization_barrier((side, kv, blocks))
            far_held = (blocks, far_symbols)
        else:
            side = turn(row, 0)
        joined = jnp.concatenate([row, side])
        both = turn(joined, 1)
        at = symbols_of(offsets)
        groups.append([(row, at[0]), (side, at[1]), (both, at[2] + at[3])])
    early, last = groups
    early[2] = (after(early[2][0], blocks), early[2][1])
    partners = [swap(kv[0].astype(bf16), o) for o in combos(bits[1:shared])[1:]]

    call = functools.partial(query_call, where, gain, weight=wq)
    carry = call(early + other(early))
    carry = call(last[:2] + other(last[:2]), carry=carry)
    both, *carry = lax.optimization_barrier((last[2][0], *carry))
    both = [(both, last[2][1])]
    total = kv[0]
    for x in partners:
        total = total + after(x, carry[0]).astype(f32)
    final = other(both)
    carry = call(both, carry=carry)
    (attended,) = call(
        final, carry=carry, extra=(total, swap(total, CORE), *rotary_tables(tokens))
    )

    def round_square(first, two, home):
        got = turn(first, 0)
        k = got.shape[0] // 2
        two = added_up(*two, got[:k]).astype(bf16)
        return [*home, got[k:]], two

    def added_up(home, *arrived):
        for x in arrived:
            home = home + x.astype(f32)
        return home

    def theirs(symbols):
        return [(across(s), bf16) for s in symbols]

    def ours(symbols):
        return [(s, f32) for s in symbols]

    def paired(own, sent):
        return [(x, swap(y, CORE)) for x, y in zip(own, sent)]

    project = functools.partial(output_call, held=far_held, width=width)
    home, one, two, corner = symbols_of(far)
    sent = project(attended, groups=theirs([corner]))
    own = project(after(attended, *sent), groups=ours([corner, one, two, home]))
    first = added_up(own[0], swap(sent[0], CORE)).astype(bf16)
    from_corner = turn(first, 0)
    sent = project(after(attended, first), groups=theirs([one, two, home]))
    one, two, home = paired(own[1:], sent)
    got_one = turn(added_up(*one).astype(bf16), 0)
    far_two = added_up(*two, from_corner).astype(bf16)
    far_sum = added_up(*home, got_one, turn(far_two, 1))
    project = functools.partial(output_call, held=near_held, width=width)
    sent = project(after(attended, sent[-1]), groups=theirs(order(near)))
    own = project(after(attended, sent[0], got_one), groups=ours(order(near)))
    pairs = paired(own, sent)
    first = added_up(after(pairs[0][0], far_two), pairs[0][1]).astype(bf16)
    near_home, near_two = round_square(first, *pairs[1:])
    k = len(low)
    far_sum = added_up(far_sum[:k], along(far_sum[k:].astype(bf16), 0))
    far_got = along(far_sum.astype(bf16), 1)
    near_sum = added_up(*near_home, turn(near_two, 1))
    home_sum = added_up(near_sum[:k], along(near_sum[k:].astype(bf16), 0), far_got)
    out = added_up(home_sum[0], *[swap(home_sum[i].astype(bf16), o) for i, o in enumerate(low) if o])
    return out.astype(bf16)


def solution(mesh):
    return jax.shard_map(
        functools.partial(per_device, mesh.shape["wide"]),
        mesh=mesh,
        in_specs=(
            P("groups", "wide"),
            P(),
            P(None, "wide"),
            P("wide", None),
            P("wide", None),
            P("wide", None),
        ),
        out_specs=P("groups", "wide"),
        check_vma=False,
    )
```

```python
import functools

import jax
import jax.numpy as jnp
from jax import lax
from jax.experimental import pallas as pl
from jax.experimental.pallas import tpu as pltpu
from jax.sharding import PartitionSpec as P

HEADS = 128
KVH = 8
HEAD = 128
LANE = 128
EPS = 1e-05
MIB = 1 << 20
CORE = 1
KV_WEIGHT = 16


def combos(bits):
    out = [0]
    for b in bits:
        out = out + [o ^ b for o in out]
    return out


def vmem():
    return pl.BlockSpec(memory_space=pltpu.VMEM)


def smem():
    return pl.BlockSpec(memory_space=pltpu.SMEM)


def hbm():
    return pl.BlockSpec(memory_space=pltpu.HBM)


def in_hbm(x):
    return pltpu.with_memory_space_constraint(x, pltpu.HBM)


def device(where, symbol):
    const, (i, j) = symbol
    return where[3 * i + j] ^ const


def dot(a, b):
    return jnp.dot(a, b, preferred_element_type=jnp.float32)


def fetch_kernel(symbols, width, where, source, target, sems):
    copies = []
    for i, (const, pick) in enumerate(symbols):
        start = pl.multiple_of((device(where, (const, pick))) * width, LANE)
        copy = pltpu.make_async_copy(
            source.at[:, pl.ds(start, width)], target.at[i], sems.at[i]
        )
        copy.start()
        copies.append(copy)
    for copy in copies:
        copy.wait()


def fetched(where, weight, width, symbols):
    shape = (len(symbols), weight.shape[0], width)
    blocks = pl.pallas_call(
        functools.partial(fetch_kernel, symbols, width),
        out_shape=jax.ShapeDtypeStruct(shape, weight.dtype),
        in_specs=[smem(), hbm()],
        out_specs=vmem(),
        scratch_shapes=[pltpu.SemaphoreType.DMA((len(symbols),))],
        compiler_params=pltpu.CompilerParams(vmem_limit_bytes=MIB),
        cost_estimate=pl.CostEstimate(
            flops=0, bytes_accessed=4 * shape[0] * shape[1] * shape[2], transcendentals=0
        ),
    )(where, in_hbm(weight))
    return blocks, symbols


def kv_kernel(shared, where, act, gain, wk, wv, send, keep, abuf, gbuf, kbuf, vbuf, sems):
    me = where[0]
    width = act.shape[1]
    own = pl.ds(pl.multiple_of(me * width, LANE), width)
    pairs = [(act, abuf), (gain, gbuf), (wk, kbuf), (wv, vbuf)]
    copies = [pltpu.make_async_copy(x, y, sems.at[i]) for i, (x, y) in enumerate(pairs)]
    for c in copies:
        c.start()
    copies[0].wait()
    copies[1].wait()
    scaled = (abuf[...].astype(jnp.float32) * gbuf[:, own]).astype(jnp.bfloat16)
    copies[2].wait()
    k = dot(scaled, kbuf[...])
    copies[3].wait()
    v = dot(scaled, vbuf[...])
    core0 = (me & CORE) == 0
    for h in range(KVH):
        off = h ^ (me >> shared)
        low, a, b = off & 1, (off >> 1) & 1, (off >> 2) & 1
        spot_0, spot_1 = 7 - (4 * low + 2 * b + a), 7 - (4 * low + 2 * a + b)
        kh, vh = k[:, h * HEAD : (h + 1) * HEAD], v[:, h * HEAD : (h + 1) * HEAD]
        keep[jnp.where(core0, spot_0, spot_1)] = jnp.where(core0, kh, vh)
        send[jnp.where(core0, spot_1, spot_0)] = jnp.where(core0, vh, kh)


def kv_terms(shared, where, act, gain, wk, wv):
    tokens = act.shape[0]
    return pl.pallas_call(
        functools.partial(kv_kernel, shared),
        out_shape=[jax.ShapeDtypeStruct((KVH, tokens, HEAD), jnp.float32)] * 2
        + [jax.ShapeDtypeStruct(x.shape, x.dtype) for x in (act, gain)],
        in_specs=[smem()] + [hbm()] * 4,
        out_specs=[vmem()] * 4,
        scratch_shapes=[
            pltpu.VMEM(wk.shape, wk.dtype),
            pltpu.VMEM(wv.shape, wv.dtype),
            pltpu.SemaphoreType.DMA((4,)),
        ],
        compiler_params=pltpu.CompilerParams(vmem_limit_bytes=12 * MIB),
        cost_estimate=pl.CostEstimate(
            flops=KV_WEIGHT * 4 * tokens * wk.size,
            bytes_accessed=KV_WEIGHT * 4 * wk.size,
            transcendentals=0,
        ),
    )(where, in_hbm(act), in_hbm(gain), in_hbm(wk), in_hbm(wv))


def attend(queries, k_sum, v_sum, cosine, sine, scale):
    k_rows = (k_sum * scale).astype(jnp.bfloat16).astype(jnp.float32)
    value = (v_sum * scale).astype(jnp.bfloat16)
    tokens, heads = queries.shape[0], queries.shape[1] // HEAD

    def rotate(x, cosine, sine):
        half = HEAD // 2
        turned = jnp.concatenate([x[:, half:], x[:, :half]], axis=1)
        return (x * cosine + turned * sine).astype(jnp.bfloat16)

    def stacked(parts):
        return jnp.concatenate(parts, axis=0)

    key = rotate(k_rows, cosine, sine)
    queries = queries * scale
    rows = stacked([queries[:, h * HEAD : (h + 1) * HEAD] for h in range(heads)])
    query = rotate(rows, stacked([cosine] * heads), stacked([sine] * heads))
    scores = lax.dot_general(
        query, key, (((1,), (1,)), ((), ())), preferred_element_type=jnp.float32
    ) * HEAD ** (-0.5)
    at = lax.broadcasted_iota(jnp.int32, (tokens, tokens), 0)
    seen = at >= lax.broadcasted_iota(jnp.int32, (tokens, tokens), 1)
    bias = jnp.where(seen, 0.0, -jnp.inf)
    scores = scores + stacked([bias] * heads)
    weights = jnp.exp(scores - jnp.max(scores, axis=1, keepdims=True))
    probs = (weights / jnp.sum(weights, axis=1, keepdims=True)).astype(jnp.bfloat16)
    out = dot(probs, value).astype(jnp.bfloat16)
    return jnp.concatenate([out[h * tokens : (h + 1) * tokens] for h in range(heads)], axis=1)


def query_kernel(places, carried, last, *refs):
    refs = list(refs)
    where, gain = refs.pop(0), refs.pop(0)
    pieces = [refs.pop(0) for _ in places]
    weight = refs.pop(0)
    queries = refs.pop(0)[...] if carried else None
    squares = refs.pop(0)[...] if carried else None
    width = pieces[0].shape[2]
    for piece, blocks in zip(pieces, places):
        for block, (const, pick) in enumerate(blocks):
            span = pl.ds(pl.multiple_of((device(where, (const, pick))) * width, LANE), width)
            x = piece[block].astype(jnp.float32)
            for c in range(0, width, LANE):
                square = x[:, c : c + LANE] * x[:, c : c + LANE]
                squares = square if squares is None else squares + square
            term = dot((x * gain[:, span]).astype(jnp.bfloat16), weight[span, :])
            queries = term if queries is None else queries + term
    if last:
        mean = jnp.sum(squares, axis=1, keepdims=True) * (1.0 / gain.shape[1])
        mine, other, cosine, sine, out = refs
        core0 = (where[0] & CORE) == 0
        k_sum = jnp.where(core0, mine[...], other[...])
        v_sum = jnp.where(core0, other[...], mine[...])
        out[...] = attend(
            queries, k_sum, v_sum, cosine[...], sine[...], lax.rsqrt(mean + EPS)
        )
    else:
        refs[0][...] = queries
        refs[1][...] = squares


def query_call(where, gain, pieces, weight, carry=(), extra=()):
    arrays, places = [array for array, _ in pieces], [symbols for _, symbols in pieces]
    tokens, width, columns = *arrays[0].shape[1:], weight.shape[1]
    rows = width * sum(len(p) for p in places)
    if extra:
        out_shape = [jax.ShapeDtypeStruct((tokens, columns), jnp.bfloat16)]
    else:
        out_shape = [
            jax.ShapeDtypeStruct((tokens, columns), jnp.float32),
            jax.ShapeDtypeStruct((tokens, LANE), jnp.float32),
        ]
    count = 2 + len(arrays) + len(carry) + len(extra)
    return pl.pallas_call(
        functools.partial(query_kernel, places, bool(carry), bool(extra)),
        out_shape=out_shape,
        in_specs=[smem()] + [vmem()] * count,
        out_specs=[vmem()] * len(out_shape),
        compiler_params=pltpu.CompilerParams(vmem_limit_bytes=4 * MIB),
        cost_estimate=pl.CostEstimate(
            flops=2 * tokens * columns * rows,
            bytes_accessed=2 * columns * rows,
            transcendentals=0,
        ),
    )(where, gain, *arrays, weight, *carry, *extra)


def output_kernel(groups, attended, weight, *outs):
    left = attended[...]
    for spots, out in zip(groups, outs):
        for block, spot in enumerate(spots):
            out[block] = dot(left, weight[spot]).astype(out.dtype)


def output_call(attended, width, groups, held):
    weight, order = held
    tokens, depth = attended.shape
    spots = [[order.index(s) for s in symbols] for symbols, _ in groups]
    columns = width * sum(len(s) for s in spots)
    return pl.pallas_call(
        functools.partial(output_kernel, spots),
        out_shape=[jax.ShapeDtypeStruct((len(s), tokens, width), t) for s, t in groups],
        in_specs=[vmem(), vmem()],
        out_specs=[vmem()] * len(groups),
        compiler_params=pltpu.CompilerParams(vmem_limit_bytes=4 * MIB),
        cost_estimate=pl.CostEstimate(
            flops=2 * tokens * depth * columns,
            bytes_accessed=2 * depth * columns,
            transcendentals=0,
        ),
    )(attended, weight)


def rotary_tables(tokens):
    half = HEAD // 2
    frequency = 500000.0 ** (-(jnp.arange(half, dtype=jnp.float32) * 2.0) / HEAD)
    angles = jnp.arange(tokens, dtype=jnp.float32)[:, None] * frequency[None, :]
    cosine, sine = jnp.cos(angles), jnp.sin(angles)
    return jnp.concatenate([cosine, cosine], axis=1), jnp.concatenate([-sine, sine], axis=1)


def per_device(n, act, norm_gain, wq, wk, wv, wo):
    tokens, width = act.shape
    me = lax.axis_index("wide")
    bits = [1 << i for i in range(n.bit_length() - 1)]
    ways = (bits[1], bits[2])
    diagonal = bits[1] ^ bits[2]
    low, z_ways = combos(bits[3:-2]), (bits[-2], bits[-1])
    f32, bf16 = jnp.float32, jnp.bfloat16

    def swap(x, offset):
        return lax.ppermute(x, "wide", [(i, i ^ offset) for i in range(n)])

    def by_core(x, pair, step):
        return lax.ppermute(x, "wide", [(i, i ^ pair[(step + (i & CORE)) % 2]) for i in range(n)])

    def turn(x, step):
        return by_core(x, ways, step)

    def along(x, step):
        return by_core(x, z_ways, step)

    def steps(pair):
        first = jnp.where((me & CORE) == 0, pair[0], pair[1])
        return [jnp.zeros_like(me), first, first ^ pair[0] ^ pair[1]]

    where = jnp.stack([me ^ i ^ j for i in steps(ways) for j in steps(z_ways)]).astype(jnp.int32)
    gain = norm_gain.reshape(1, -1)

    def across(symbols):
        flip = (0, 2, 1)
        return [(const ^ CORE, (flip[i], flip[j])) for const, (i, j) in symbols]

    near = [(o, j) for j in (0, 1) for o in low]
    far = [(o, 2) for o in low] + [(o ^ z_ways[0] ^ z_ways[1], 0) for o in low]

    def after(x, *others):
        return lax.optimization_barrier((x, *others))[0]

    shared = (n // KVH).bit_length() - 1
    raw = act
    kv_send, kv_keep, act, gain = kv_terms(shared, where, act, gain, wk, wv)

    def symbols_of(offsets):
        square = [(0, 0), (0, 1), (0, 2), (diagonal, 0)]
        return [[(const ^ o, (i, j)) for o, j in offsets] for const, i in square]

    def other(pieces):
        return [(swap(x, CORE), across(symbols)) for x, symbols in pieces]

    def order(offsets):
        home, one, two, corner = symbols_of(offsets)
        return [corner + one, two, home]

    def columns_of(offsets):
        own = sum(order(offsets), [])
        return own + across(own)

    def halved(kv, send, way):
        half = kv.shape[0] // 2
        return kv[half:] + send(kv[:half].astype(bf16), way).astype(f32)

    kv = halved(kv_keep + swap(kv_send, CORE), swap, bits[shared])
    row = jnp.stack([act] + [swap(raw, o) for o in low[1:]])
    row = jnp.concatenate([row, along(row, 0)])
    groups = []
    for offsets in (near, far):
        if offsets is far:
            half = kv[: kv.shape[0] // 2].astype(bf16)
            k = min(row.shape[0], half.shape[0])
            extra = jnp.zeros((row.shape[0], *half.shape[1:]), bf16).at[:k].set(half[:k])
            got = along(jnp.concatenate([row, extra], axis=2), 1)
            near_blocks, near_symbols = fetched(after(where, joined), wo, width, columns_of(near))
            got, near_blocks = lax.optimization_barrier((got, near_blocks))
            near_held = (near_blocks, near_symbols)
            row = got[:, :, :width]
            kv = kv[kv.shape[0] // 2 :] + got[:k, :, width:].astype(f32)
            side = turn(row, 0)
            kv = halved(kv, along, 0)
            blocks, far_symbols = fetched(after(where, row), wo, width, columns_of(far))
            side, kv, blocks = lax.optimization_barrier((side, kv, blocks))
            far_held = (blocks, far_symbols)
        else:
            side = turn(row, 0)
        joined = jnp.concatenate([row, side])
        both = turn(joined, 1)
        at = symbols_of(offsets)
        groups.append([(row, at[0]), (side, at[1]), (both, at[2] + at[3])])
    early, last = groups
    early[2] = (after(early[2][0], blocks), early[2][1])
    partners = [swap(kv[0].astype(bf16), o) for o in combos(bits[1:shared])[1:]]

    call = functools.partial(query_call, where, gain, weight=wq)
    carry = call(early + other(early))
    carry = call(last[:2] + other(last[:2]), carry=carry)
    both, *carry = lax.optimization_barrier((last[2][0], *carry))
    both = [(both, last[2][1])]
    total = kv[0]
    for x in partners:
        total = total + after(x, carry[0]).astype(f32)
    final = other(both)
    carry = call(both, carry=carry)
    (attended,) = call(
        final, carry=carry, extra=(total, swap(total, CORE), *rotary_tables(tokens))
    )

    def round_square(first, two, home):
        got = turn(first, 0)
        k = got.shape[0] // 2
        two = added_up(*two, got[:k]).astype(bf16)
        return [*home, got[k:]], two

    def added_up(home, *arrived):
        for x in arrived:
            home = home + x.astype(f32)
        return home

    def theirs(symbols):
        return [(across(s), bf16) for s in symbols]

    def ours(symbols):
        return [(s, f32) for s in symbols]

    def paired(own, sent):
        return [(x, swap(y, CORE)) for x, y in zip(own, sent)]

    project = functools.partial(output_call, held=far_held, width=width)
    home, one, two, corner = symbols_of(far)
    sent = project(attended, groups=theirs([corner]))
    sent += project(after(attended, *sent), groups=theirs([one, two, home]))
    own = project(after(attended, sent[-1]), groups=ours([corner, one, two, home]))
    corner, one, two, home = paired(own, sent)
    from_corner = turn(added_up(*corner).astype(bf16), 0)
    got_one = turn(added_up(*one).astype(bf16), 0)
    far_two = added_up(*two, from_corner).astype(bf16)
    far_sum = added_up(*home, got_one, turn(far_two, 1))
    project = functools.partial(output_call, held=near_held, width=width)
    sent = project(after(attended, sent[-1]), groups=theirs(order(near)))
    own = project(after(attended, sent[0], got_one), groups=ours(order(near)))
    pairs = paired(own, sent)
    first = added_up(after(pairs[0][0], far_two), pairs[0][1]).astype(bf16)
    near_home, near_two = round_square(first, *pairs[1:])
    far_got = along(far_sum.astype(bf16), 1)
    near_sum = added_up(*near_home, turn(near_two, 1), far_got)
    k = len(low)
    home_sum = added_up(near_sum[:k], along(near_sum[k:].astype(bf16), 0))
    out = added_up(home_sum[0], *[swap(home_sum[i].astype(bf16), o) for i, o in enumerate(low) if o])
    return out.astype(bf16)


def solution(mesh):
    return jax.shard_map(
        functools.partial(per_device, mesh.shape["wide"]),
        mesh=mesh,
        in_specs=(
            P("groups", "wide"),
            P(),
            P(None, "wide"),
            P("wide", None),
            P("wide", None),
            P("wide", None),
        ),
        out_specs=P("groups", "wide"),
        check_vma=False,
    )
```

```python
import functools

import jax
import jax.numpy as jnp
from jax import lax
from jax.experimental import pallas as pl
from jax.experimental.pallas import tpu as pltpu
from jax.sharding import PartitionSpec as P

HEADS = 128
KVH = 8
HEAD = 128
LANE = 128
EPS = 1e-05
MIB = 1 << 20
CORE = 1
KV_WEIGHT = 16


def combos(bits):
    out = [0]
    for b in bits:
        out = out + [o ^ b for o in out]
    return out


def vmem():
    return pl.BlockSpec(memory_space=pltpu.VMEM)


def smem():
    return pl.BlockSpec(memory_space=pltpu.SMEM)


def hbm():
    return pl.BlockSpec(memory_space=pltpu.HBM)


def in_hbm(x):
    return pltpu.with_memory_space_constraint(x, pltpu.HBM)


def device(where, symbol):
    const, (i, j) = symbol
    return where[3 * i + j] ^ const


def dot(a, b):
    return jnp.dot(a, b, preferred_element_type=jnp.float32)


def fetch_kernel(symbols, width, where, source, target, sems):
    copies = []
    for i, (const, pick) in enumerate(symbols):
        start = pl.multiple_of((device(where, (const, pick))) * width, LANE)
        copy = pltpu.make_async_copy(
            source.at[:, pl.ds(start, width)], target.at[i], sems.at[i]
        )
        copy.start()
        copies.append(copy)
    for copy in copies:
        copy.wait()


def fetched(where, weight, width, symbols):
    shape = (len(symbols), weight.shape[0], width)
    blocks = pl.pallas_call(
        functools.partial(fetch_kernel, symbols, width),
        out_shape=jax.ShapeDtypeStruct(shape, weight.dtype),
        in_specs=[smem(), hbm()],
        out_specs=vmem(),
        scratch_shapes=[pltpu.SemaphoreType.DMA((len(symbols),))],
        compiler_params=pltpu.CompilerParams(vmem_limit_bytes=MIB),
        cost_estimate=pl.CostEstimate(
            flops=0, bytes_accessed=4 * shape[0] * shape[1] * shape[2], transcendentals=0
        ),
    )(where, in_hbm(weight))
    return blocks, symbols


def kv_kernel(shared, where, act, gain, wk, wv, send, keep, abuf, gbuf, kbuf, vbuf, sems):
    me = where[0]
    width = act.shape[1]
    own = pl.ds(pl.multiple_of(me * width, LANE), width)
    pairs = [(act, abuf), (gain, gbuf), (wk, kbuf), (wv, vbuf)]
    copies = [pltpu.make_async_copy(x, y, sems.at[i]) for i, (x, y) in enumerate(pairs)]
    for c in copies:
        c.start()
    copies[0].wait()
    copies[1].wait()
    scaled = (abuf[...].astype(jnp.float32) * gbuf[:, own]).astype(jnp.bfloat16)
    copies[2].wait()
    k = dot(scaled, kbuf[...])
    copies[3].wait()
    v = dot(scaled, vbuf[...])
    core0 = (me & CORE) == 0
    for h in range(KVH):
        off = h ^ (me >> shared)
        low, a, b = off & 1, (off >> 1) & 1, (off >> 2) & 1
        spot_0, spot_1 = 7 - (4 * low + 2 * b + a), 7 - (4 * low + 2 * a + b)
        kh, vh = k[:, h * HEAD : (h + 1) * HEAD], v[:, h * HEAD : (h + 1) * HEAD]
        keep[jnp.where(core0, spot_0, spot_1)] = jnp.where(core0, kh, vh)
        send[jnp.where(core0, spot_1, spot_0)] = jnp.where(core0, vh, kh)


def kv_terms(shared, where, act, gain, wk, wv):
    tokens = act.shape[0]
    return pl.pallas_call(
        functools.partial(kv_kernel, shared),
        out_shape=[jax.ShapeDtypeStruct((KVH, tokens, HEAD), jnp.float32)] * 2
        + [jax.ShapeDtypeStruct(x.shape, x.dtype) for x in (act, gain)],
        in_specs=[smem()] + [hbm()] * 4,
        out_specs=[vmem()] * 4,
        scratch_shapes=[
            pltpu.VMEM(wk.shape, wk.dtype),
            pltpu.VMEM(wv.shape, wv.dtype),
            pltpu.SemaphoreType.DMA((4,)),
        ],
        compiler_params=pltpu.CompilerParams(vmem_limit_bytes=12 * MIB),
        cost_estimate=pl.CostEstimate(
            flops=KV_WEIGHT * 4 * tokens * wk.size,
            bytes_accessed=KV_WEIGHT * 4 * wk.size,
            transcendentals=0,
        ),
    )(where, in_hbm(act), in_hbm(gain), in_hbm(wk), in_hbm(wv))


def attend(queries, k_sum, v_sum, cosine, sine, scale):
    k_rows = (k_sum * scale).astype(jnp.bfloat16).astype(jnp.float32)
    value = (v_sum * scale).astype(jnp.bfloat16)
    tokens, heads = queries.shape[0], queries.shape[1] // HEAD

    def rotate(x, cosine, sine):
        half = HEAD // 2
        turned = jnp.concatenate([x[:, half:], x[:, :half]], axis=1)
        return (x * cosine + turned * sine).astype(jnp.bfloat16)

    def stacked(parts):
        return jnp.concatenate(parts, axis=0)

    key = rotate(k_rows, cosine, sine)
    queries = queries * scale
    rows = stacked([queries[:, h * HEAD : (h + 1) * HEAD] for h in range(heads)])
    query = rotate(rows, stacked([cosine] * heads), stacked([sine] * heads))
    scores = lax.dot_general(
        query, key, (((1,), (1,)), ((), ())), preferred_element_type=jnp.float32
    ) * HEAD ** (-0.5)
    at = lax.broadcasted_iota(jnp.int32, (tokens, tokens), 0)
    seen = at >= lax.broadcasted_iota(jnp.int32, (tokens, tokens), 1)
    bias = jnp.where(seen, 0.0, -jnp.inf)
    scores = scores + stacked([bias] * heads)
    weights = jnp.exp(scores - jnp.max(scores, axis=1, keepdims=True))
    probs = (weights / jnp.sum(weights, axis=1, keepdims=True)).astype(jnp.bfloat16)
    out = dot(probs, value).astype(jnp.bfloat16)
    return jnp.concatenate([out[h * tokens : (h + 1) * tokens] for h in range(heads)], axis=1)


def query_kernel(places, carried, last, *refs):
    refs = list(refs)
    where, gain = refs.pop(0), refs.pop(0)
    pieces = [refs.pop(0) for _ in places]
    weight = refs.pop(0)
    queries = refs.pop(0)[...] if carried else None
    squares = refs.pop(0)[...] if carried else None
    width = pieces[0].shape[2]
    for piece, blocks in zip(pieces, places):
        for block, (const, pick) in enumerate(blocks):
            span = pl.ds(pl.multiple_of((device(where, (const, pick))) * width, LANE), width)
            x = piece[block].astype(jnp.float32)
            for c in range(0, width, LANE):
                square = x[:, c : c + LANE] * x[:, c : c + LANE]
                squares = square if squares is None else squares + square
            term = dot((x * gain[:, span]).astype(jnp.bfloat16), weight[span, :])
            queries = term if queries is None else queries + term
    if last:
        mean = jnp.sum(squares, axis=1, keepdims=True) * (1.0 / gain.shape[1])
        mine, other, cosine, sine, out = refs
        core0 = (where[0] & CORE) == 0
        k_sum = jnp.where(core0, mine[...], other[...])
        v_sum = jnp.where(core0, other[...], mine[...])
        out[...] = attend(
            queries, k_sum, v_sum, cosine[...], sine[...], lax.rsqrt(mean + EPS)
        )
    else:
        refs[0][...] = queries
        refs[1][...] = squares


def query_call(where, gain, pieces, weight, carry=(), extra=()):
    arrays, places = [array for array, _ in pieces], [symbols for _, symbols in pieces]
    tokens, width, columns = *arrays[0].shape[1:], weight.shape[1]
    rows = width * sum(len(p) for p in places)
    if extra:
        out_shape = [jax.ShapeDtypeStruct((tokens, columns), jnp.bfloat16)]
    else:
        out_shape = [
            jax.ShapeDtypeStruct((tokens, columns), jnp.float32),
            jax.ShapeDtypeStruct((tokens, LANE), jnp.float32),
        ]
    count = 2 + len(arrays) + len(carry) + len(extra)
    return pl.pallas_call(
        functools.partial(query_kernel, places, bool(carry), bool(extra)),
        out_shape=out_shape,
        in_specs=[smem()] + [vmem()] * count,
        out_specs=[vmem()] * len(out_shape),
        compiler_params=pltpu.CompilerParams(vmem_limit_bytes=4 * MIB),
        cost_estimate=pl.CostEstimate(
            flops=2 * tokens * columns * rows,
            bytes_accessed=2 * columns * rows,
            transcendentals=0,
        ),
    )(where, gain, *arrays, weight, *carry, *extra)


def output_kernel(groups, attended, weight, *outs):
    left = attended[...]
    for spots, out in zip(groups, outs):
        for block, spot in enumerate(spots):
            out[block] = dot(left, weight[spot]).astype(out.dtype)


def output_call(attended, width, groups, held):
    weight, order = held
    tokens, depth = attended.shape
    spots = [[order.index(s) for s in symbols] for symbols, _ in groups]
    columns = width * sum(len(s) for s in spots)
    return pl.pallas_call(
        functools.partial(output_kernel, spots),
        out_shape=[jax.ShapeDtypeStruct((len(s), tokens, width), t) for s, t in groups],
        in_specs=[vmem(), vmem()],
        out_specs=[vmem()] * len(groups),
        compiler_params=pltpu.CompilerParams(vmem_limit_bytes=4 * MIB),
        cost_estimate=pl.CostEstimate(
            flops=2 * tokens * depth * columns,
            bytes_accessed=2 * depth * columns,
            transcendentals=0,
        ),
    )(attended, weight)


def rotary_tables(tokens):
    half = HEAD // 2
    frequency = 500000.0 ** (-(jnp.arange(half, dtype=jnp.float32) * 2.0) / HEAD)
    angles = jnp.arange(tokens, dtype=jnp.float32)[:, None] * frequency[None, :]
    cosine, sine = jnp.cos(angles), jnp.sin(angles)
    return jnp.concatenate([cosine, cosine], axis=1), jnp.concatenate([-sine, sine], axis=1)


def per_device(n, act, norm_gain, wq, wk, wv, wo):
    tokens, width = act.shape
    me = lax.axis_index("wide")
    bits = [1 << i for i in range(n.bit_length() - 1)]
    ways = (bits[1], bits[2])
    diagonal = bits[1] ^ bits[2]
    low, z_ways = combos(bits[3:-2]), (bits[-2], bits[-1])
    f32, bf16 = jnp.float32, jnp.bfloat16

    def swap(x, offset):
        return lax.ppermute(x, "wide", [(i, i ^ offset) for i in range(n)])

    def by_core(x, pair, step):
        return lax.ppermute(x, "wide", [(i, i ^ pair[(step + (i & CORE)) % 2]) for i in range(n)])

    def turn(x, step):
        return by_core(x, ways, step)

    def along(x, step):
        return by_core(x, z_ways, step)

    def steps(pair):
        first = jnp.where((me & CORE) == 0, pair[0], pair[1])
        return [jnp.zeros_like(me), first, first ^ pair[0] ^ pair[1]]

    where = jnp.stack([me ^ i ^ j for i in steps(ways) for j in steps(z_ways)]).astype(jnp.int32)
    gain = norm_gain.reshape(1, -1)

    def across(symbols):
        flip = (0, 2, 1)
        return [(const ^ CORE, (flip[i], flip[j])) for const, (i, j) in symbols]

    near = [(o, j) for j in (0, 1) for o in low]
    far = [(o, 2) for o in low] + [(o ^ z_ways[0] ^ z_ways[1], 0) for o in low]

    def after(x, *others):
        return lax.optimization_barrier((x, *others))[0]

    shared = (n // KVH).bit_length() - 1
    raw = act
    kv_send, kv_keep, act, gain = kv_terms(shared, where, act, gain, wk, wv)

    def symbols_of(offsets):
        square = [(0, 0), (0, 1), (0, 2), (diagonal, 0)]
        return [[(const ^ o, (i, j)) for o, j in offsets] for const, i in square]

    def other(pieces):
        return [(swap(x, CORE), across(symbols)) for x, symbols in pieces]

    def order(offsets):
        home, one, two, corner = symbols_of(offsets)
        return [corner + one, two, home]

    def columns_of(offsets):
        own = sum(order(offsets), [])
        return own + across(own)

    def halved(kv, send, way):
        half = kv.shape[0] // 2
        return kv[half:] + send(kv[:half].astype(bf16), way).astype(f32)

    kv = halved(kv_keep + swap(kv_send, CORE), swap, bits[shared])
    row = jnp.stack([act] + [swap(raw, o) for o in low[1:]])
    row = jnp.concatenate([row, along(row, 0)])
    groups = []
    for offsets in (near, far):
        if offsets is far:
            half = kv[: kv.shape[0] // 2].astype(bf16)
            k = min(row.shape[0], half.shape[0])
            extra = jnp.zeros((row.shape[0], *half.shape[1:]), bf16).at[:k].set(half[:k])
            got = along(jnp.concatenate([row, extra], axis=2), 1)
            near_blocks, near_symbols = fetched(after(where, joined), wo, width, columns_of(near))
            got, near_blocks = lax.optimization_barrier((got, near_blocks))
            near_held = (near_blocks, near_symbols)
            row = got[:, :, :width]
            kv = kv[kv.shape[0] // 2 :] + got[:k, :, width:].astype(f32)
            side = turn(row, 0)
            kv = halved(kv, along, 0)
            blocks, far_symbols = fetched(after(where, row), wo, width, columns_of(far))
            side, kv, blocks = lax.optimization_barrier((side, kv, blocks))
            far_held = (blocks, far_symbols)
        else:
            side = turn(row, 0)
        joined = jnp.concatenate([row, side])
        both = turn(joined, 1)
        at = symbols_of(offsets)
        groups.append([(row, at[0]), (side, at[1]), (both, at[2] + at[3])])
    early, last = groups
    early[2] = (after(early[2][0], blocks), early[2][1])
    partners = [swap(kv[0].astype(bf16), o) for o in combos(bits[1:shared])[1:]]

    call = functools.partial(query_call, where, gain, weight=wq)
    carry = call(early + other(early))
    carry = call(last[:2] + other(last[:2]), carry=carry)
    tables = rotary_tables(tokens)
    both, tables, partners, *carry = lax.optimization_barrier(
        (last[2][0], tables, partners, *carry)
    )
    both = [(both, last[2][1])]
    total = kv[0]
    for x in partners:
        total = total + x.astype(f32)
    final = other(both)
    carry = call(both, carry=carry)
    (attended,) = call(
        final, carry=carry, extra=(total, swap(total, CORE), *tables)
    )

    def round_square(first, two, home):
        got = turn(first, 0)
        k = got.shape[0] // 2
        two = added_up(*two, got[:k]).astype(bf16)
        return [*home, got[k:]], two

    def added_up(home, *arrived):
        for x in arrived:
            home = home + x.astype(f32)
        return home

    def theirs(symbols):
        return [(across(s), bf16) for s in symbols]

    def ours(symbols):
        return [(s, f32) for s in symbols]

    def paired(own, sent):
        return [(x, swap(y, CORE)) for x, y in zip(own, sent)]

    project = functools.partial(output_call, held=far_held, width=width)
    home, one, two, corner = symbols_of(far)
    sent = project(attended, groups=theirs([corner]))
    sent += project(after(attended, *sent), groups=theirs([one, two, home]))
    own = project(after(attended, sent[-1]), groups=ours([corner, one, two, home]))
    corner, one, two, home = paired(own, sent)
    from_corner = turn(added_up(*corner).astype(bf16), 0)
    got_one = turn(added_up(*one).astype(bf16), 0)
    far_two = added_up(*two, from_corner).astype(bf16)
    far_sum = added_up(*home, got_one, turn(far_two, 1))
    project = functools.partial(output_call, held=near_held, width=width)
    sent = project(after(attended, sent[-1]), groups=theirs(order(near)))
    own = project(after(attended, sent[0], got_one), groups=ours(order(near)))
    pairs = paired(own, sent)
    first = added_up(after(pairs[0][0], far_two), pairs[0][1]).astype(bf16)
    near_home, near_two = round_square(first, *pairs[1:])
    far_got = along(far_sum.astype(bf16), 1)
    k = len(low)
    got = [turn(near_two[k:], 1), turn(near_two[:k], 1)]
    near_sum = added_up(*[x[k:] for x in near_home], got[0], far_got[k:])
    home_sum = added_up(*[x[:k] for x in near_home], got[1], far_got[:k])
    home_sum = added_up(home_sum, along(near_sum.astype(bf16), 0))
    out = added_up(home_sum[0], *[swap(home_sum[i].astype(bf16), o) for i, o in enumerate(low) if o])
    return out.astype(bf16)


def solution(mesh):
    return jax.shard_map(
        functools.partial(per_device, mesh.shape["wide"]),
        mesh=mesh,
        in_specs=(
            P("groups", "wide"),
            P(),
            P(None, "wide"),
            P("wide", None),
            P("wide", None),
            P("wide", None),
        ),
        out_specs=P("groups", "wide"),
        check_vma=False,
    )
```

```python
import functools

import jax
import jax.numpy as jnp
from jax import lax
from jax.experimental import pallas as pl
from jax.experimental.pallas import tpu as pltpu
from jax.sharding import PartitionSpec as P

HEADS = 128
KVH = 8
HEAD = 128
LANE = 128
EPS = 1e-05
MIB = 1 << 20
CORE = 1
KV_WEIGHT = 16


def combos(bits):
    out = [0]
    for b in bits:
        out = out + [o ^ b for o in out]
    return out


def vmem():
    return pl.BlockSpec(memory_space=pltpu.VMEM)


def smem():
    return pl.BlockSpec(memory_space=pltpu.SMEM)


def hbm():
    return pl.BlockSpec(memory_space=pltpu.HBM)


def in_hbm(x):
    return pltpu.with_memory_space_constraint(x, pltpu.HBM)


def device(where, symbol):
    const, (i, j) = symbol
    return where[3 * i + j] ^ const


def dot(a, b):
    return jnp.dot(a, b, preferred_element_type=jnp.float32)


def fetch_kernel(symbols, width, where, source, target, sems):
    copies = []
    for i, (const, pick) in enumerate(symbols):
        start = pl.multiple_of((device(where, (const, pick))) * width, LANE)
        copy = pltpu.make_async_copy(
            source.at[:, pl.ds(start, width)], target.at[i], sems.at[i]
        )
        copy.start()
        copies.append(copy)
    for copy in copies:
        copy.wait()


def fetched(where, weight, width, symbols):
    shape = (len(symbols), weight.shape[0], width)
    blocks = pl.pallas_call(
        functools.partial(fetch_kernel, symbols, width),
        out_shape=jax.ShapeDtypeStruct(shape, weight.dtype),
        in_specs=[smem(), hbm()],
        out_specs=vmem(),
        scratch_shapes=[pltpu.SemaphoreType.DMA((len(symbols),))],
        compiler_params=pltpu.CompilerParams(vmem_limit_bytes=MIB),
        cost_estimate=pl.CostEstimate(
            flops=0, bytes_accessed=4 * shape[0] * shape[1] * shape[2], transcendentals=0
        ),
    )(where, in_hbm(weight))
    return blocks, symbols


def kv_kernel(shared, where, act, gain, wk, wv, send, keep, abuf, gbuf, kbuf, vbuf, sems):
    me = where[0]
    width = act.shape[1]
    own = pl.ds(pl.multiple_of(me * width, LANE), width)
    pairs = [(act, abuf), (gain, gbuf), (wk, kbuf), (wv, vbuf)]
    copies = [pltpu.make_async_copy(x, y, sems.at[i]) for i, (x, y) in enumerate(pairs)]
    for c in copies:
        c.start()
    copies[0].wait()
    copies[1].wait()
    scaled = (abuf[...].astype(jnp.float32) * gbuf[:, own]).astype(jnp.bfloat16)
    copies[2].wait()
    k = dot(scaled, kbuf[...])
    copies[3].wait()
    v = dot(scaled, vbuf[...])
    core0 = (me & CORE) == 0
    for h in range(KVH):
        off = h ^ (me >> shared)
        low, a, b = off & 1, (off >> 1) & 1, (off >> 2) & 1
        spot_0, spot_1 = 7 - (4 * low + 2 * b + a), 7 - (4 * low + 2 * a + b)
        kh, vh = k[:, h * HEAD : (h + 1) * HEAD], v[:, h * HEAD : (h + 1) * HEAD]
        keep[jnp.where(core0, spot_0, spot_1)] = jnp.where(core0, kh, vh)
        send[jnp.where(core0, spot_1, spot_0)] = jnp.where(core0, vh, kh)


def kv_terms(shared, where, act, gain, wk, wv):
    tokens = act.shape[0]
    return pl.pallas_call(
        functools.partial(kv_kernel, shared),
        out_shape=[jax.ShapeDtypeStruct((KVH, tokens, HEAD), jnp.float32)] * 2
        + [jax.ShapeDtypeStruct(x.shape, x.dtype) for x in (act, gain)],
        in_specs=[smem()] + [hbm()] * 4,
        out_specs=[vmem()] * 4,
        scratch_shapes=[
            pltpu.VMEM(wk.shape, wk.dtype),
            pltpu.VMEM(wv.shape, wv.dtype),
            pltpu.SemaphoreType.DMA((4,)),
        ],
        compiler_params=pltpu.CompilerParams(vmem_limit_bytes=12 * MIB),
        cost_estimate=pl.CostEstimate(
            flops=KV_WEIGHT * 4 * tokens * wk.size,
            bytes_accessed=KV_WEIGHT * 4 * wk.size,
            transcendentals=0,
        ),
    )(where, in_hbm(act), in_hbm(gain), in_hbm(wk), in_hbm(wv))


def attend(queries, k_sum, v_sum, cosine, sine, scale):
    k_rows = (k_sum * scale).astype(jnp.bfloat16).astype(jnp.float32)
    value = (v_sum * scale).astype(jnp.bfloat16)
    tokens, heads = queries.shape[0], queries.shape[1] // HEAD

    def rotate(x, cosine, sine):
        half = HEAD // 2
        turned = jnp.concatenate([x[:, half:], x[:, :half]], axis=1)
        return (x * cosine + turned * sine).astype(jnp.bfloat16)

    def stacked(parts):
        return jnp.concatenate(parts, axis=0)

    key = rotate(k_rows, cosine, sine)
    queries = queries * scale
    rows = stacked([queries[:, h * HEAD : (h + 1) * HEAD] for h in range(heads)])
    query = rotate(rows, stacked([cosine] * heads), stacked([sine] * heads))
    scores = lax.dot_general(
        query, key, (((1,), (1,)), ((), ())), preferred_element_type=jnp.float32
    ) * HEAD ** (-0.5)
    at = lax.broadcasted_iota(jnp.int32, (tokens, tokens), 0)
    seen = at >= lax.broadcasted_iota(jnp.int32, (tokens, tokens), 1)
    bias = jnp.where(seen, 0.0, -jnp.inf)
    scores = scores + stacked([bias] * heads)
    weights = jnp.exp(scores - jnp.max(scores, axis=1, keepdims=True))
    probs = (weights / jnp.sum(weights, axis=1, keepdims=True)).astype(jnp.bfloat16)
    out = dot(probs, value).astype(jnp.bfloat16)
    return jnp.concatenate([out[h * tokens : (h + 1) * tokens] for h in range(heads)], axis=1)


def query_kernel(places, carried, last, *refs):
    refs = list(refs)
    where, gain = refs.pop(0), refs.pop(0)
    pieces = [refs.pop(0) for _ in places]
    weight = refs.pop(0)
    queries = refs.pop(0)[...] if carried else None
    squares = refs.pop(0)[...] if carried else None
    width = pieces[0].shape[2]
    for piece, blocks in zip(pieces, places):
        for block, (const, pick) in enumerate(blocks):
            span = pl.ds(pl.multiple_of((device(where, (const, pick))) * width, LANE), width)
            x = piece[block].astype(jnp.float32)
            for c in range(0, width, LANE):
                square = x[:, c : c + LANE] * x[:, c : c + LANE]
                squares = square if squares is None else squares + square
            term = dot((x * gain[:, span]).astype(jnp.bfloat16), weight[span, :])
            queries = term if queries is None else queries + term
    if last:
        mean = jnp.sum(squares, axis=1, keepdims=True) * (1.0 / gain.shape[1])
        mine, other, cosine, sine, out = refs
        core0 = (where[0] & CORE) == 0
        k_sum = jnp.where(core0, mine[...], other[...])
        v_sum = jnp.where(core0, other[...], mine[...])
        out[...] = attend(
            queries, k_sum, v_sum, cosine[...], sine[...], lax.rsqrt(mean + EPS)
        )
    else:
        refs[0][...] = queries
        refs[1][...] = squares


def query_call(where, gain, pieces, weight, carry=(), extra=()):
    arrays, places = [array for array, _ in pieces], [symbols for _, symbols in pieces]
    tokens, width, columns = *arrays[0].shape[1:], weight.shape[1]
    rows = width * sum(len(p) for p in places)
    if extra:
        out_shape = [jax.ShapeDtypeStruct((tokens, columns), jnp.bfloat16)]
    else:
        out_shape = [
            jax.ShapeDtypeStruct((tokens, columns), jnp.float32),
            jax.ShapeDtypeStruct((tokens, LANE), jnp.float32),
        ]
    count = 2 + len(arrays) + len(carry) + len(extra)
    return pl.pallas_call(
        functools.partial(query_kernel, places, bool(carry), bool(extra)),
        out_shape=out_shape,
        in_specs=[smem()] + [vmem()] * count,
        out_specs=[vmem()] * len(out_shape),
        compiler_params=pltpu.CompilerParams(vmem_limit_bytes=4 * MIB),
        cost_estimate=pl.CostEstimate(
            flops=2 * tokens * columns * rows,
            bytes_accessed=2 * columns * rows,
            transcendentals=0,
        ),
    )(where, gain, *arrays, weight, *carry, *extra)


def output_kernel(groups, attended, weight, *outs):
    left = attended[...]
    for spots, out in zip(groups, outs):
        for block, spot in enumerate(spots):
            out[block] = dot(left, weight[spot]).astype(out.dtype)


def output_call(attended, width, groups, held):
    weight, order = held
    tokens, depth = attended.shape
    spots = [[order.index(s) for s in symbols] for symbols, _ in groups]
    columns = width * sum(len(s) for s in spots)
    return pl.pallas_call(
        functools.partial(output_kernel, spots),
        out_shape=[jax.ShapeDtypeStruct((len(s), tokens, width), t) for s, t in groups],
        in_specs=[vmem(), vmem()],
        out_specs=[vmem()] * len(groups),
        compiler_params=pltpu.CompilerParams(vmem_limit_bytes=4 * MIB),
        cost_estimate=pl.CostEstimate(
            flops=2 * tokens * depth * columns,
            bytes_accessed=2 * depth * columns,
            transcendentals=0,
        ),
    )(attended, weight)


def rotary_tables(tokens):
    half = HEAD // 2
    frequency = 500000.0 ** (-(jnp.arange(half, dtype=jnp.float32) * 2.0) / HEAD)
    angles = jnp.arange(tokens, dtype=jnp.float32)[:, None] * frequency[None, :]
    cosine, sine = jnp.cos(angles), jnp.sin(angles)
    return jnp.concatenate([cosine, cosine], axis=1), jnp.concatenate([-sine, sine], axis=1)


def per_device(n, act, norm_gain, wq, wk, wv, wo):
    tokens, width = act.shape
    me = lax.axis_index("wide")
    bits = [1 << i for i in range(n.bit_length() - 1)]
    ways = (bits[1], bits[2])
    diagonal = bits[1] ^ bits[2]
    low, z_ways = combos(bits[3:-2]), (bits[-2], bits[-1])
    f32, bf16 = jnp.float32, jnp.bfloat16

    def swap(x, offset):
        return lax.ppermute(x, "wide", [(i, i ^ offset) for i in range(n)])

    def by_core(x, pair, step):
        return lax.ppermute(x, "wide", [(i, i ^ pair[(step + (i & CORE)) % 2]) for i in range(n)])

    def turn(x, step):
        return by_core(x, ways, step)

    def along(x, step):
        return by_core(x, z_ways, step)

    def steps(pair):
        first = jnp.where((me & CORE) == 0, pair[0], pair[1])
        return [jnp.zeros_like(me), first, first ^ pair[0] ^ pair[1]]

    where = jnp.stack([me ^ i ^ j for i in steps(ways) for j in steps(z_ways)]).astype(jnp.int32)
    gain = norm_gain.reshape(1, -1)

    def across(symbols):
        flip = (0, 2, 1)
        return [(const ^ CORE, (flip[i], flip[j])) for const, (i, j) in symbols]

    near = [(o, j) for j in (0, 1) for o in low]
    far = [(o, 2) for o in low] + [(o ^ z_ways[0] ^ z_ways[1], 0) for o in low]

    def after(x, *others):
        return lax.optimization_barrier((x, *others))[0]

    shared = (n // KVH).bit_length() - 1
    raw = act
    kv_send, kv_keep, act, gain = kv_terms(shared, where, act, gain, wk, wv)

    def symbols_of(offsets):
        square = [(0, 0), (0, 1), (0, 2), (diagonal, 0)]
        return [[(const ^ o, (i, j)) for o, j in offsets] for const, i in square]

    def other(pieces):
        return [(swap(x, CORE), across(symbols)) for x, symbols in pieces]

    def order(offsets):
        home, one, two, corner = symbols_of(offsets)
        return [corner + one, two, home]

    def columns_of(offsets):
        own = sum(order(offsets), [])
        return own + across(own)

    def halved(kv, send, way):
        half = kv.shape[0] // 2
        return kv[half:] + send(kv[:half].astype(bf16), way).astype(f32)

    kv = halved(kv_keep + swap(kv_send, CORE), swap, bits[shared])
    row = jnp.stack([act] + [swap(raw, o) for o in low[1:]])
    row = jnp.concatenate([row, along(row, 0)])
    groups = []
    for offsets in (near, far):
        if offsets is far:
            half = kv[: kv.shape[0] // 2].astype(bf16)
            k = min(row.shape[0], half.shape[0])
            extra = jnp.zeros((row.shape[0], *half.shape[1:]), bf16).at[:k].set(half[:k])
            got = along(jnp.concatenate([row, extra], axis=2), 1)
            near_blocks, near_symbols = fetched(after(where, joined), wo, width, columns_of(near))
            got, near_blocks = lax.optimization_barrier((got, near_blocks))
            near_held = (near_blocks, near_symbols)
            row = got[:, :, :width]
            kv = kv[kv.shape[0] // 2 :] + got[:k, :, width:].astype(f32)
            side = turn(row, 0)
            kv = halved(kv, along, 0)
            blocks, far_symbols = fetched(after(where, row), wo, width, columns_of(far))
            side, kv, blocks = lax.optimization_barrier((side, kv, blocks))
            far_held = (blocks, far_symbols)
        else:
            side = turn(row, 0)
        joined = jnp.concatenate([row, side])
        both = turn(joined, 1)
        at = symbols_of(offsets)
        groups.append([(row, at[0]), (side, at[1]), (both, at[2] + at[3])])
    early, last = groups
    early[2] = (after(early[2][0], blocks, joined), early[2][1])
    total = kv[0]
    for b in bits[1:shared]:
        total = total + swap(total.astype(bf16), b).astype(f32)
    sums = (total, swap(total, CORE))

    call = functools.partial(query_call, where, gain, weight=wq)
    carry = call(early + other(early))
    carry = call(last[:2] + other(last[:2]), carry=carry)
    tables = rotary_tables(tokens)
    both, tables, sums, *carry = lax.optimization_barrier((last[2][0], tables, sums, *carry))
    both = [(both, last[2][1])]
    final = other(both)
    carry = call(both, carry=carry)
    (attended,) = call(final, carry=carry, extra=(*sums, *tables))

    def round_square(first, two, home):
        got = turn(first, 0)
        k = got.shape[0] // 2
        two = added_up(*two, got[:k]).astype(bf16)
        return [*home, got[k:]], two

    def added_up(home, *arrived):
        for x in arrived:
            home = home + x.astype(f32)
        return home

    def theirs(symbols):
        return [(across(s), bf16) for s in symbols]

    def ours(symbols):
        return [(s, f32) for s in symbols]

    def paired(own, sent):
        return [(x, swap(y, CORE)) for x, y in zip(own, sent)]

    project = functools.partial(output_call, held=far_held, width=width)
    home, one, two, corner = symbols_of(far)
    sent = project(attended, groups=theirs([corner]))
    sent += project(after(attended, *sent), groups=theirs([one, two, home]))
    own = project(after(attended, sent[-1]), groups=ours([corner, one, two, home]))
    corner, one, two, home = paired(own, sent)
    from_corner = turn(added_up(*corner).astype(bf16), 0)
    got_one = turn(added_up(*one).astype(bf16), 0)
    far_two = added_up(*two, from_corner).astype(bf16)
    far_sum = added_up(*home, got_one, turn(far_two, 1))
    project = functools.partial(output_call, held=near_held, width=width)
    sent = project(after(attended, sent[-1]), groups=theirs(order(near)))
    own = project(after(attended, sent[0], got_one), groups=ours(order(near)))
    pairs = paired(own, sent)
    first = added_up(after(pairs[0][0], far_two), pairs[0][1]).astype(bf16)
    near_home, near_two = round_square(first, *pairs[1:])
    far_got = along(far_sum.astype(bf16), 1)
    k = len(low)
    got = [turn(near_two[k:], 1), turn(near_two[:k], 1)]
    near_sum = added_up(*[x[k:] for x in near_home], got[0], far_got[k:])
    home_sum = added_up(*[x[:k] for x in near_home], got[1], far_got[:k])
    home_sum = added_up(home_sum, along(near_sum.astype(bf16), 0))
    out = added_up(home_sum[0], *[swap(home_sum[i].astype(bf16), o) for i, o in enumerate(low) if o])
    return out.astype(bf16)


def solution(mesh):
    return jax.shard_map(
        functools.partial(per_device, mesh.shape["wide"]),
        mesh=mesh,
        in_specs=(
            P("groups", "wide"),
            P(),
            P(None, "wide"),
            P("wide", None),
            P("wide", None),
            P("wide", None),
        ),
        out_specs=P("groups", "wide"),
        check_vma=False,
    )
```

```python
import functools

import jax
import jax.numpy as jnp
from jax import lax
from jax.experimental import pallas as pl
from jax.experimental.pallas import tpu as pltpu
from jax.sharding import PartitionSpec as P

HEADS = 128
KVH = 8
HEAD = 128
LANE = 128
EPS = 1e-05
MIB = 1 << 20
CORE = 1
KV_WEIGHT = 16


def combos(bits):
    out = [0]
    for b in bits:
        out = out + [o ^ b for o in out]
    return out


def vmem():
    return pl.BlockSpec(memory_space=pltpu.VMEM)


def smem():
    return pl.BlockSpec(memory_space=pltpu.SMEM)


def hbm():
    return pl.BlockSpec(memory_space=pltpu.HBM)


def in_hbm(x):
    return pltpu.with_memory_space_constraint(x, pltpu.HBM)


def device(where, symbol):
    const, (i, j) = symbol
    return where[3 * i + j] ^ const


def dot(a, b):
    return jnp.dot(a, b, preferred_element_type=jnp.float32)


def fetch_kernel(symbols, width, where, source, target, sems):
    copies = []
    for i, (const, pick) in enumerate(symbols):
        start = pl.multiple_of((device(where, (const, pick))) * width, LANE)
        copy = pltpu.make_async_copy(
            source.at[:, pl.ds(start, width)], target.at[i], sems.at[i]
        )
        copy.start()
        copies.append(copy)
    for copy in copies:
        copy.wait()


def fetched(where, weight, width, symbols):
    shape = (len(symbols), weight.shape[0], width)
    blocks = pl.pallas_call(
        functools.partial(fetch_kernel, symbols, width),
        out_shape=jax.ShapeDtypeStruct(shape, weight.dtype),
        in_specs=[smem(), hbm()],
        out_specs=vmem(),
        scratch_shapes=[pltpu.SemaphoreType.DMA((len(symbols),))],
        compiler_params=pltpu.CompilerParams(vmem_limit_bytes=MIB),
        cost_estimate=pl.CostEstimate(
            flops=0, bytes_accessed=4 * shape[0] * shape[1] * shape[2], transcendentals=0
        ),
    )(where, in_hbm(weight))
    return blocks, symbols


def kv_kernel(shared, where, act, gain, wk, wv, send, keep, abuf, gbuf, kbuf, vbuf, sems):
    me = where[0]
    width = act.shape[1]
    own = pl.ds(pl.multiple_of(me * width, LANE), width)
    pairs = [(act, abuf), (gain, gbuf), (wk, kbuf), (wv, vbuf)]
    copies = [pltpu.make_async_copy(x, y, sems.at[i]) for i, (x, y) in enumerate(pairs)]
    for c in copies:
        c.start()
    copies[0].wait()
    copies[1].wait()
    scaled = (abuf[...].astype(jnp.float32) * gbuf[:, own]).astype(jnp.bfloat16)
    copies[2].wait()
    k = dot(scaled, kbuf[...])
    copies[3].wait()
    v = dot(scaled, vbuf[...])
    core0 = (me & CORE) == 0
    for h in range(KVH):
        off = h ^ (me >> shared)
        low, a, b = off & 1, (off >> 1) & 1, (off >> 2) & 1
        spot_0, spot_1 = 7 - (4 * low + 2 * b + a), 7 - (4 * low + 2 * a + b)
        kh, vh = k[:, h * HEAD : (h + 1) * HEAD], v[:, h * HEAD : (h + 1) * HEAD]
        keep[jnp.where(core0, spot_0, spot_1)] = jnp.where(core0, kh, vh)
        send[jnp.where(core0, spot_1, spot_0)] = jnp.where(core0, vh, kh)


def kv_terms(shared, where, act, gain, wk, wv):
    tokens = act.shape[0]
    return pl.pallas_call(
        functools.partial(kv_kernel, shared),
        out_shape=[jax.ShapeDtypeStruct((KVH, tokens, HEAD), jnp.float32)] * 2
        + [jax.ShapeDtypeStruct(x.shape, x.dtype) for x in (act, gain)],
        in_specs=[smem()] + [hbm()] * 4,
        out_specs=[vmem()] * 4,
        scratch_shapes=[
            pltpu.VMEM(wk.shape, wk.dtype),
            pltpu.VMEM(wv.shape, wv.dtype),
            pltpu.SemaphoreType.DMA((4,)),
        ],
        compiler_params=pltpu.CompilerParams(vmem_limit_bytes=12 * MIB),
        cost_estimate=pl.CostEstimate(
            flops=KV_WEIGHT * 4 * tokens * wk.size,
            bytes_accessed=KV_WEIGHT * 4 * wk.size,
            transcendentals=0,
        ),
    )(where, in_hbm(act), in_hbm(gain), in_hbm(wk), in_hbm(wv))


def attend(queries, k_sum, v_sum, cosine, sine, scale):
    k_rows = (k_sum * scale).astype(jnp.bfloat16).astype(jnp.float32)
    value = (v_sum * scale).astype(jnp.bfloat16)
    tokens, heads = queries.shape[0], queries.shape[1] // HEAD

    def rotate(x, cosine, sine):
        half = HEAD // 2
        turned = jnp.concatenate([x[:, half:], x[:, :half]], axis=1)
        return (x * cosine + turned * sine).astype(jnp.bfloat16)

    def stacked(parts):
        return jnp.concatenate(parts, axis=0)

    key = rotate(k_rows, cosine, sine)
    queries = queries * scale
    rows = stacked([queries[:, h * HEAD : (h + 1) * HEAD] for h in range(heads)])
    query = rotate(rows, stacked([cosine] * heads), stacked([sine] * heads))
    scores = lax.dot_general(
        query, key, (((1,), (1,)), ((), ())), preferred_element_type=jnp.float32
    ) * HEAD ** (-0.5)
    at = lax.broadcasted_iota(jnp.int32, (tokens, tokens), 0)
    seen = at >= lax.broadcasted_iota(jnp.int32, (tokens, tokens), 1)
    bias = jnp.where(seen, 0.0, -jnp.inf)
    scores = scores + stacked([bias] * heads)
    weights = jnp.exp(scores - jnp.max(scores, axis=1, keepdims=True))
    probs = (weights / jnp.sum(weights, axis=1, keepdims=True)).astype(jnp.bfloat16)
    out = dot(probs, value).astype(jnp.bfloat16)
    return jnp.concatenate([out[h * tokens : (h + 1) * tokens] for h in range(heads)], axis=1)


def query_kernel(places, carried, last, *refs):
    refs = list(refs)
    where, gain = refs.pop(0), refs.pop(0)
    pieces = [refs.pop(0) for _ in places]
    weight = refs.pop(0)
    queries = refs.pop(0)[...] if carried else None
    squares = refs.pop(0)[...] if carried else None
    width = pieces[0].shape[2]
    for piece, blocks in zip(pieces, places):
        for block, (const, pick) in enumerate(blocks):
            span = pl.ds(pl.multiple_of((device(where, (const, pick))) * width, LANE), width)
            x = piece[block].astype(jnp.float32)
            for c in range(0, width, LANE):
                square = x[:, c : c + LANE] * x[:, c : c + LANE]
                squares = square if squares is None else squares + square
            term = dot((x * gain[:, span]).astype(jnp.bfloat16), weight[span, :])
            queries = term if queries is None else queries + term
    if last:
        mean = jnp.sum(squares, axis=1, keepdims=True) * (1.0 / gain.shape[1])
        mine, other, cosine, sine, out = refs
        core0 = (where[0] & CORE) == 0
        k_sum = jnp.where(core0, mine[...], other[...])
        v_sum = jnp.where(core0, other[...], mine[...])
        out[...] = attend(
            queries, k_sum, v_sum, cosine[...], sine[...], lax.rsqrt(mean + EPS)
        )
    else:
        refs[0][...] = queries
        refs[1][...] = squares


def query_call(where, gain, pieces, weight, carry=(), extra=()):
    arrays, places = [array for array, _ in pieces], [symbols for _, symbols in pieces]
    tokens, width, columns = *arrays[0].shape[1:], weight.shape[1]
    rows = width * sum(len(p) for p in places)
    if extra:
        out_shape = [jax.ShapeDtypeStruct((tokens, columns), jnp.bfloat16)]
    else:
        out_shape = [
            jax.ShapeDtypeStruct((tokens, columns), jnp.float32),
            jax.ShapeDtypeStruct((tokens, LANE), jnp.float32),
        ]
    count = 2 + len(arrays) + len(carry) + len(extra)
    return pl.pallas_call(
        functools.partial(query_kernel, places, bool(carry), bool(extra)),
        out_shape=out_shape,
        in_specs=[smem()] + [vmem()] * count,
        out_specs=[vmem()] * len(out_shape),
        compiler_params=pltpu.CompilerParams(vmem_limit_bytes=4 * MIB),
        cost_estimate=pl.CostEstimate(
            flops=2 * tokens * columns * rows,
            bytes_accessed=2 * columns * rows,
            transcendentals=0,
        ),
    )(where, gain, *arrays, weight, *carry, *extra)


def output_kernel(groups, attended, weight, *outs):
    left = attended[...]
    for spots, out in zip(groups, outs):
        for block, spot in enumerate(spots):
            out[block] = dot(left, weight[spot]).astype(out.dtype)


def output_call(attended, width, groups, held):
    weight, order = held
    tokens, depth = attended.shape
    spots = [[order.index(s) for s in symbols] for symbols, _ in groups]
    columns = width * sum(len(s) for s in spots)
    return pl.pallas_call(
        functools.partial(output_kernel, spots),
        out_shape=[jax.ShapeDtypeStruct((len(s), tokens, width), t) for s, t in groups],
        in_specs=[vmem(), vmem()],
        out_specs=[vmem()] * len(groups),
        compiler_params=pltpu.CompilerParams(vmem_limit_bytes=4 * MIB),
        cost_estimate=pl.CostEstimate(
            flops=2 * tokens * depth * columns,
            bytes_accessed=2 * depth * columns,
            transcendentals=0,
        ),
    )(attended, weight)


def rotary_tables(tokens):
    half = HEAD // 2
    frequency = 500000.0 ** (-(jnp.arange(half, dtype=jnp.float32) * 2.0) / HEAD)
    angles = jnp.arange(tokens, dtype=jnp.float32)[:, None] * frequency[None, :]
    cosine, sine = jnp.cos(angles), jnp.sin(angles)
    return jnp.concatenate([cosine, cosine], axis=1), jnp.concatenate([-sine, sine], axis=1)


def per_device(n, act, norm_gain, wq, wk, wv, wo):
    tokens, width = act.shape
    me = lax.axis_index("wide")
    bits = [1 << i for i in range(n.bit_length() - 1)]
    ways = (bits[1], bits[2])
    diagonal = bits[1] ^ bits[2]
    low, z_ways = combos(bits[3:-2]), (bits[-2], bits[-1])
    f32, bf16 = jnp.float32, jnp.bfloat16

    def swap(x, offset):
        return lax.ppermute(x, "wide", [(i, i ^ offset) for i in range(n)])

    def by_core(x, pair, step):
        return lax.ppermute(x, "wide", [(i, i ^ pair[(step + (i & CORE)) % 2]) for i in range(n)])

    def turn(x, step):
        return by_core(x, ways, step)

    def along(x, step):
        return by_core(x, z_ways, step)

    def steps(pair):
        first = jnp.where((me & CORE) == 0, pair[0], pair[1])
        return [jnp.zeros_like(me), first, first ^ pair[0] ^ pair[1]]

    where = jnp.stack([me ^ i ^ j for i in steps(ways) for j in steps(z_ways)]).astype(jnp.int32)
    gain = norm_gain.reshape(1, -1)

    def across(symbols):
        flip = (0, 2, 1)
        return [(const ^ CORE, (flip[i], flip[j])) for const, (i, j) in symbols]

    near = [(o, j) for j in (0, 1) for o in low]
    far = [(o, 2) for o in low] + [(o ^ z_ways[0] ^ z_ways[1], 0) for o in low]

    def after(x, *others):
        return lax.optimization_barrier((x, *others))[0]

    shared = (n // KVH).bit_length() - 1
    raw = act
    kv_send, kv_keep, act, gain = kv_terms(shared, where, act, gain, wk, wv)

    def symbols_of(offsets):
        square = [(0, 0), (0, 1), (0, 2), (diagonal, 0)]
        return [[(const ^ o, (i, j)) for o, j in offsets] for const, i in square]

    def other(pieces):
        return [(swap(x, CORE), across(symbols)) for x, symbols in pieces]

    def order(offsets):
        home, one, two, corner = symbols_of(offsets)
        return [corner + one, two, home]

    def columns_of(offsets):
        own = sum(order(offsets), [])
        return own + across(own)

    def halved(kv, send, way):
        half = kv.shape[0] // 2
        return kv[half:] + send(kv[:half].astype(bf16), way).astype(f32)

    kv = halved(kv_keep + swap(kv_send, CORE), swap, bits[shared])
    row = jnp.stack([act] + [swap(raw, o) for o in low[1:]])
    row = jnp.concatenate([row, along(row, 0)])
    groups = []
    for offsets in (near, far):
        if offsets is far:
            half = kv[: kv.shape[0] // 2].astype(bf16)
            k = min(row.shape[0], half.shape[0])
            extra = jnp.zeros((row.shape[0], *half.shape[1:]), bf16).at[:k].set(half[:k])
            got = along(jnp.concatenate([row, extra], axis=2), 1)
            near_blocks, near_symbols = fetched(after(where, joined), wo, width, columns_of(near))
            got, near_blocks = lax.optimization_barrier((got, near_blocks))
            near_held = (near_blocks, near_symbols)
            row = got[:, :, :width]
            kv = kv[kv.shape[0] // 2 :] + got[:k, :, width:].astype(f32)
            side = turn(row, 0)
            kv = halved(kv, along, 0)
            blocks, far_symbols = fetched(after(where, row), wo, width, columns_of(far))
            side, kv, blocks = lax.optimization_barrier((side, kv, blocks))
            far_held = (blocks, far_symbols)
        else:
            side = turn(row, 0)
        joined = jnp.concatenate([row, side])
        both = turn(joined, 1)
        at = symbols_of(offsets)
        groups.append([(row, at[0]), (side, at[1]), (both, at[2] + at[3])])
    early, last = groups
    early[2] = (after(early[2][0], blocks, joined), early[2][1])
    partners = [swap(kv[0].astype(bf16), o) for o in combos(bits[1:shared])[1:]]

    call = functools.partial(query_call, where, gain, weight=wq)
    carry = call(early + other(early))
    carry = call(last[:2] + other(last[:2]), carry=carry)
    tables = rotary_tables(tokens)
    both, tables, partners, *carry = lax.optimization_barrier(
        (last[2][0], tables, partners, *carry)
    )
    both = [(both, last[2][1])]
    total = kv[0]
    for x in partners:
        total = total + x.astype(f32)
    final = other(both)
    carry = call(both, carry=carry)
    (attended,) = call(
        final, carry=carry, extra=(total, swap(total, CORE), *tables)
    )

    def round_square(first, two, home):
        got = turn(first, 0)
        k = got.shape[0] // 2
        two = added_up(*two, got[:k]).astype(bf16)
        return [*home, got[k:]], two

    def added_up(home, *arrived):
        for x in arrived:
            home = home + x.astype(f32)
        return home

    def theirs(symbols):
        return [(across(s), bf16) for s in symbols]

    def ours(symbols):
        return [(s, f32) for s in symbols]

    def paired(own, sent):
        return [(x, swap(y, CORE)) for x, y in zip(own, sent)]

    project = functools.partial(output_call, held=far_held, width=width)
    home, one, two, corner = symbols_of(far)
    sent = project(attended, groups=theirs([corner]))
    sent += project(after(attended, *sent), groups=theirs([one, two, home]))
    own = project(after(attended, sent[-1]), groups=ours([corner, one, two, home]))
    corner, one, two, home = paired(own, sent)
    from_corner = turn(added_up(*corner).astype(bf16), 0)
    got_one = turn(added_up(*one).astype(bf16), 0)
    far_two = added_up(*two, from_corner).astype(bf16)
    far_sum = added_up(*home, got_one, turn(far_two, 1))
    project = functools.partial(output_call, held=near_held, width=width)
    sent = project(after(attended, sent[-1]), groups=theirs(order(near)))
    own = project(after(attended, sent[0], got_one), groups=ours(order(near)))
    pairs = paired(own, sent)
    first = added_up(after(pairs[0][0], far_two), pairs[0][1]).astype(bf16)
    near_home, near_two = round_square(first, *pairs[1:])
    far_got = along(far_sum.astype(bf16), 1)
    k = len(low)
    got = [turn(near_two[k:], 1), turn(near_two[:k], 1)]
    near_sum = added_up(*[x[k:] for x in near_home], got[0], far_got[k:])
    home_sum = added_up(*[x[:k] for x in near_home], got[1], far_got[:k])
    home_sum = added_up(home_sum, along(near_sum.astype(bf16), 0))
    out = added_up(home_sum[0], *[swap(home_sum[i].astype(bf16), o) for i, o in enumerate(low) if o])
    return out.astype(bf16)


def solution(mesh):
    return jax.shard_map(
        functools.partial(per_device, mesh.shape["wide"]),
        mesh=mesh,
        in_specs=(
            P("groups", "wide"),
            P(),
            P(None, "wide"),
            P("wide", None),
            P("wide", None),
            P("wide", None),
        ),
        out_specs=P("groups", "wide"),
        check_vma=False,
    )
```
